512 devices in a mesh: row: 32 (over y, x), col: 16 (over z, core).
Axes of the slice: x: 4, y: 8, z: 8, core: 2. Of those that a mesh axis runs over, the one named last changes fastest.
Arguments:
- trailing_grad: float32 [16384, 16384], P('row', 'col'), as said below
- factor_rows: float32 [16384, 1024], P(('row', 'col')), may hold values from -0.046875 to 0.046875
- factor_grad: float32 [16384, 1024], P(('row', 'col')), may hold values from -6 to 6
- diag_factor: float32 [2, 512, 512], P(None, 'row'), as said below
- cross_factor: float32 [512, 512], P('row'), may hold values from -0.25 to 0.25
- cross_grad: float32 [512, 1024], P('row', 'col'), may hold values from -6 to 6
- corner_grad: float32 [512, 512], P('row', 'col'), may hold values from -6 to 6
Outputs:
- rows_grad: float32 [16384, 1024], P(('row', 'col'))
- blocks_grad: float32 [2, 512, 512], P(None, 'row', 'col')
- coupling_grad: float32 [512, 512], P('row', 'col')
The draws below stay inside these ranges and needn't reach their ends.
Inputs may be any that keep to these rules, and one draw needn't show every extreme that they name: `trailing_grad`: symmetric. `diag_factor`: each of the two 512 x 512 blocks is lower triangular with its diagonal between 1 and 2.
All inputs are finite; a program needn't handle non-finite values.
Results may differ from the reference program's by a relative error of at most 0.00018.
Values sent between devices are 32-bit elements; how exact they have to be, the bound alone decides.
A program may use at most 64 MiB of HBM per device.

```python
import jax
import jax.numpy as jnp
from jax import lax

B = 512
K = 1024
M = 16384


def draw_trailing_grad(key, part):
    key = jax.random.fold_in(key, 1)
    base = jax.random.normal(key, (M, M), jnp.float32)
    return (base + base.T) * 0.70710678


def draw_diag_factor(key, part):
    key = jax.random.fold_in(key, 2)
    first, second = jax.random.split(key)
    diagonal = jax.random.uniform(first, (2, B), jnp.float32, 1.0, 2.0)
    spread = jax.random.normal(second, (2, B, B), jnp.float32)
    lower = jnp.tril(spread, -1) * (0.4 * B ** (-0.5))
    return lower + diagonal[:, :, None] * jnp.eye(B, dtype=jnp.float32)[None, :, :]


def shard_levels(rng, dims, cuts, low, top_value):
    factor_of = 1.0
    for dim, blocks in cuts:
        steps = jax.random.uniform(jax.random.fold_in(jax.random.fold_in(rng, 6), dim), (blocks,), jnp.float32, low / len(cuts), top_value / len(cuts))
        factor_of = factor_of * jnp.repeat(jnp.exp(steps), dims[dim] // blocks).reshape((-1,) + (1,) * (len(dims) - 1 - dim))
    return factor_of


def bell_draw(own_key, extent, scale, limit, shards=(), kind=jnp.bfloat16):
    gain = shard_levels(own_key, extent, shards, -0.22, 0.18) if shards else 1.0
    values = jax.random.normal(own_key, extent, jnp.float32) * scale * gain
    return jnp.minimum(jnp.maximum(values, -limit), limit).astype(kind)


def setup_inputs(seed: int = 0) -> dict:
    streams_of = jax.random.split(jax.random.key(seed), 8)
    trailing_grad = draw_trailing_grad(jax.random.fold_in(streams_of[7], 71), 0)
    factor_rows = bell_draw(streams_of[1], (M, K), M ** -0.5, 0.046875, ((0, 512),), jnp.float32)
    factor_grad = bell_draw(streams_of[2], (M, K), 1.0, 6.0, ((0, 512),), jnp.float32)
    diag_factor = draw_diag_factor(jax.random.fold_in(streams_of[7], 71), 0)
    cross_factor = bell_draw(streams_of[4], (B, B), B ** -0.5, 0.25, ((0, 32),), jnp.float32)
    cross_grad = bell_draw(streams_of[5], (B, K), 1.0, 6.0, ((0, 32), (1, 16)), jnp.float32)
    corner_grad = bell_draw(streams_of[6], (B, B), 1.0, 6.0, ((0, 32), (1, 16)), jnp.float32)
    return dict(trailing_grad=trailing_grad, factor_rows=factor_rows, factor_grad=factor_grad, diag_factor=diag_factor, cross_factor=cross_factor, cross_grad=cross_grad, corner_grad=corner_grad)


highest = lax.Precision.HIGHEST

def matmul(left, right):
    return jnp.dot(left.astype(jnp.float32), right.astype(jnp.float32), precision=highest, preferred_element_type=jnp.float32)

def inner_t(left, right):
    return lax.dot_general(left.astype(jnp.float32), right.astype(jnp.float32), (((0,), (0,)), ((), ())), precision=highest, preferred_element_type=jnp.float32)

def lower_inverse(factor):
    identity = jnp.eye(factor.shape[0], dtype=jnp.float32)
    return lax.linalg.triangular_solve(factor, identity, left_side=True, lower=True)

def block_adjoint(factor, inverse, lowered_grad):
    identity = jnp.eye(factor.shape[0], dtype=jnp.float32)
    product = inner_t(factor, lowered_grad)
    lowered = jnp.tril(product) - 0.5 * product * identity
    return 0.5 * inner_t(inverse, matmul(lowered + lowered.T, inverse))

def reference(trailing_grad, factor_rows, factor_grad, diag_factor, cross_factor, cross_grad, corner_grad):
    first_inverse = lower_inverse(diag_factor[0])
    second_inverse = lower_inverse(diag_factor[1])
    product = matmul(trailing_grad, factor_rows)
    second_adjoint = matmul(factor_grad[:, B:] - 2.0 * product[:, B:], second_inverse)
    panel_total = cross_grad - inner_t(second_adjoint, factor_rows)
    second_block = block_adjoint(diag_factor[1], second_inverse, jnp.tril(panel_total[:, B:]))
    coupling = matmul(panel_total[:, :B] - 2.0 * matmul(second_block, cross_factor), first_inverse)
    first_adjoint = matmul(factor_grad[:, :B] - 2.0 * product[:, :B] - matmul(second_adjoint, cross_factor), first_inverse)
    first_grad = jnp.tril(corner_grad - inner_t(first_adjoint, factor_rows[:, :B]) - inner_t(coupling, cross_factor))
    first_block = block_adjoint(diag_factor[0], first_inverse, first_grad)
    return (jnp.concatenate([first_adjoint, second_adjoint], 1), jnp.stack([first_block, second_block]), coupling)
```

```python
import functools

import jax
import jax.numpy as jnp
from jax import lax
from jax.experimental import pallas as pl
from jax.experimental.pallas import tpu as pltpu
from jax.sharding import PartitionSpec as P

MESH = pl.DeviceIdType.MESH
F32 = jnp.float32
BF16 = jnp.bfloat16
NX, NY, NZ = 4, 8, 8
CHIPS_RING = NZ
NG = 2
B = 512
W = B // NG
ROWS = 32
ORDER = (0, -1, 1, -2, 2, -3, 3, -4)


def split(a):
    hi = a.astype(BF16)
    return hi, (a - hi.astype(F32)).astype(BF16)


def dot(a, b):
    return jnp.dot(a, b, preferred_element_type=F32)


def mm_split(a, b):
    return dot(a[0], b[0]) + (dot(a[0], b[1]) + dot(a[1], b[0]))


def mm(a, b):
    return mm_split(split(a), split(b))


def gather_kernel(
    t_ref, r_ref, f_ref, g_ref, x_ref,
    tbuf, thi, tlo, band, rbuf, psum, sbuf, fbuf, xr, xo, xst, xs, xs2, gm, gy, sg, gx, gz, gsib,
    sib_s, sib_r, loc, zs, zr, ys, xsm, rr, ss, sr, as_, ar, gys, gyr, gxs, gxr, gas, gar, gzs, gzr,
):
    row = lax.axis_index("row")
    col = lax.axis_index("col")
    y, x = row // NX, lax.rem(row, NX)
    z, k = col // 2, lax.rem(col, 2)

    def dev(px, py, pz, pk):
        return {"row": py * NX + px, "col": pz * 2 + pk}

    def up(v, s, n):
        return lax.rem(v + (s + n), n)

    sib = dev(x, y, z, 1 - k)
    zpeer = [dev(x, y, up(z, s, NZ), k) for s in range(1, NZ)]
    ypeer = [dev(x, up(y, s, NY), z, k) for s in range(1, NY)]
    xpeer = [dev(up(x, s, NX), y, z, k) for s in range(1, NX)]
    zup, zdn = zpeer[0], zpeer[-1]
    yup, ydn = ypeer[0], ypeer[-1]
    xup, xdn = xpeer[0], xpeer[-1]
    d = up(y - z, NY, NY)

    barrier = pltpu.get_barrier_semaphore()
    partners = [sib] + zpeer + ypeer + xpeer
    for p in partners:
        pl.semaphore_signal(barrier, inc=1, device_id=p, device_id_type=MESH)
    pl.semaphore_wait(barrier, len(partners))

    sends = []

    def put(src, dst, ssem, rsem, target, cond=None):
        c = pltpu.make_async_remote_copy(
            src_ref=src, dst_ref=dst, send_sem=ssem, recv_sem=rsem, device_id=target, device_id_type=MESH
        )
        if cond is None:
            c.start()
        else:
            pl.when(cond)(c.start)
        sends.append((c, cond))

    def got(ref, sem):
        pltpu.make_async_remote_copy(
            src_ref=ref, dst_ref=ref, send_sem=sem, recv_sem=sem, device_id=sib, device_id_type=MESH
        ).wait_recv()

    for g in range(NG):
        put(r_ref.at[1 - k, g], band.at[g, z, k], sib_s.at[g], sib_r.at[g], sib)
    for g in range(NG):
        band[g, z, k] = r_ref[k, g]
    put(t_ref, tbuf.at[k], sib_s.at[NG], sib_r.at[NG], sib)
    tcopy = pltpu.make_async_copy(t_ref, tbuf.at[k], loc.at[0])
    tcopy.start()
    put(f_ref.at[1 - k], fbuf.at[k], sib_s.at[NG + 1], sib_r.at[NG + 1], sib)
    fbuf[k] = f_ref[k]

    steps = [(g, j) for g in range(NG) for j in range(NZ)]
    lb, ld, le = 4, 5, 6
    own_copies = []

    def stage_a(i):
        g, j = steps[i]
        zz = up(z, ORDER[j], NZ)
        if j == 0:
            got(band.at[g, z, 1 - k], sib_r.at[g])
            put(band.at[g, z], band.at[g, z], zs.at[0, g, 0], zr.at[g, z], zup)
            put(band.at[g, z], band.at[g, z], zs.at[1, g, 0], zr.at[g, z], zdn)
        else:
            got(band.at[g, zz], zr.at[g, zz])
            hop = abs(ORDER[j])
            if ORDER[j] < 0 and hop < NZ // 2:
                put(band.at[g, zz], band.at[g, zz], zs.at[0, g, hop], zr.at[g, zz], zup)
            if ORDER[j] > 0 and hop < NZ // 2 - 1:
                put(band.at[g, zz], band.at[g, zz], zs.at[1, g, hop], zr.at[g, zz], zdn)
        src = d == 0
        put(band.at[g, zz], rbuf.at[g, x, zz], ys.at[0, g, j], rr.at[g, x, zz], yup, src)
        put(band.at[g, zz], rbuf.at[g, x, zz], ys.at[1, g, j], rr.at[g, x, zz], ydn, src)

        @pl.when(src)
        def _():
            rbuf[g, x, zz] = band[g, zz]

    def stage_b(i):
        g, j = steps[i]
        zz = up(z, ORDER[j], NZ)
        slot, sem = rbuf.at[g, x, zz], rr.at[g, x, zz]

        @pl.when(d != 0)
        def _():
            got(slot, sem)

        put(slot, slot, ys.at[0, g, j], sem, yup, jnp.logical_and(d >= 1, d <= 3))
        put(slot, slot, ys.at[1, g, j], sem, ydn, d >= 6)
        put(slot, slot, xsm.at[0, g, j], sem, xup)
        put(slot, slot, xsm.at[1, g, j], sem, xdn)

    def stage_d(i):
        g, j = steps[i]
        zz = up(z, ORDER[j], NZ)
        left, right = up(x, -1, NX), up(x, 1, NX)
        got(rbuf.at[g, left, zz], rr.at[g, left, zz])
        got(rbuf.at[g, right, zz], rr.at[g, right, zz])
        origin, target = (left, xup) if j % 2 == 0 else (right, xdn)
        put(rbuf.at[g, origin, zz], rbuf.at[g, origin, zz], xsm.at[2, g, j], rr.at[g, origin, zz], target)

    def stage_e(i):
        g, j = steps[i]
        zz = up(z, ORDER[j], NZ)
        far = up(x, 2, NX)
        got(rbuf.at[g, far, zz], rr.at[g, far, zz])

    def piece(g, xx):
        b = split(rbuf[g, xx].reshape(NZ * 2 * ROWS, W))
        lanes = slice(512 * (xx % 2), 512 * (xx % 2) + 512)
        a = (thi[xx // 2, :, lanes], tlo[xx // 2, :, lanes])
        part = mm_split(a, b).reshape(NZ, 2 * ROWS, W)
        if xx == 0:
            psum[g] = part
        else:
            psum[g] += part

    def scatter(g):
        for s in range(1, NZ):
            to = up(z, s, NZ)
            put(psum.at[g, to], sbuf.at[g, z], ss.at[g, s], sr.at[g, z], zpeer[s - 1])
        sbuf[g, z] = psum[g, z]

    n = len(steps)
    work = []
    for i in range(n + le):
        if i < n:
            stage_a(i)
        if 0 <= i - lb < n:
            stage_b(i - lb)
        if 0 <= i - ld < n:
            stage_d(i - ld)
        if 0 <= i - le < n:
            stage_e(i - le)
            g, j = steps[i - le]
            if work:
                work.pop(0)()
            if j == NZ - 1:
                if g == 0:
                    tcopy.wait()
                    got(tbuf.at[1 - k], sib_r.at[NG])
                    for h in range(2):
                        thi[h], tlo[h] = split(tbuf[h])
                for xx in range(NX):
                    work.append(functools.partial(piece, g, xx))
                work.append(functools.partial(scatter, g))
    for item in work:
        item()

    got(fbuf.at[1 - k], sib_r.at[NG + 1])
    for g in range(NG):
        for s in range(1, NZ):
            frm = up(z, s, NZ)
            got(sbuf.at[g, frm], sr.at[g, frm])
        total = sbuf[g, 0]
        for s in range(1, NZ):
            total = total + sbuf[g, s]
        lanes = slice(g * W, g * W + W)
        xr[:, :, lanes] = fbuf[:, :, lanes] - 2.0 * total.reshape(2, ROWS, W)

    put(xr.at[1 - k], xo.at[k], sib_s.at[NG + 2], sib_r.at[NG + 2], sib)
    xo[k] = xr[k]
    xall = xr[...].reshape(2 * ROWS, B)
    for s in range(NZ):
        xst[s] = xall[:, 64 * s : 64 * s + 64]
    for s in range(1, NZ):
        to = up(z, s, NZ)
        put(xst.at[to], xs.at[z], as_.at[s], ar.at[z], zpeer[s - 1])
    xs[z] = xst[z]
    for s in range(1, NZ):
        frm = up(z, s, NZ)
        got(xs.at[frm], ar.at[frm])
    first = k == 0
    put(xs, xs2, sib_s.at[NG + 3], sib_r.at[NG + 3], sib, k == 1)

    def gram(b, src):
        a = split(src[...].reshape(NZ * 64, 64).T)
        for g in range(NG):
            bb = split(band[g].reshape(NZ * 64, W))
            gm[b, :, :, g * W : g * W + W] = mm_split(a, bb).reshape(NY, 8, W)

    def plane_reduce_start(b, cond):
        for s in range(1, NY):
            to = up(y, s, NY)
            put(gm.at[b, to], gy.at[b, y], gys.at[b, s], gyr.at[b, y], ypeer[s - 1], cond)

    gram(0, xs)
    plane_reduce_start(0, None)

    @pl.when(first)
    def _():
        got(xs2, sib_r.at[NG + 3])
        gram(1, xs2)

    plane_reduce_start(1, first)
    conds = (None, first)

    def when(cond, fn):
        if cond is None:
            fn()
        else:
            pl.when(cond)(fn)

    def y_sum(b):
        gy[b, y] = gm[b, y]
        for s in range(1, NY):
            frm = up(y, s, NY)
            got(gy.at[b, frm], gyr.at[b, frm])
        total = gy[b, 0]
        for s in range(1, NY):
            total = total + gy[b, s]
        sg[b] = total
        gx[b, x] = total

    def x_sum(b):
        for s in range(1, NX):
            frm = up(x, s, NX)
            got(gx.at[b, frm], gxr.at[b, frm])
        gz[b, z, y] = (gx[b, 0] + gx[b, 1]) + (gx[b, 2] + gx[b, 3])

    def y_wait(b):
        for s in range(1, NY):
            frm = up(y, s, NY)
            got(gz.at[b, z, frm], gar.at[b, frm])

    for b in range(2):
        when(conds[b], functools.partial(y_sum, b))
        for s in range(1, NX):
            put(sg.at[b], gx.at[b, x], gxs.at[b, s], gxr.at[b, x], xpeer[s - 1], conds[b])
    for b in range(2):
        when(conds[b], functools.partial(x_sum, b))
        for s in range(1, NY):
            put(gz.at[b, z, y], gz.at[b, z, y], gas.at[b, s], gar.at[b, y], ypeer[s - 1], conds[b])
    for j in range(NZ):
        zz = up(z, ORDER[j], NZ)
        hop = abs(ORDER[j])
        for b in range(2):
            if j == 0:
                when(conds[b], functools.partial(y_wait, b))
            else:
                when(conds[b], functools.partial(got, gz.at[b, zz], gzr.at[b, zz]))
            if j == 0 or (ORDER[j] < 0 and hop < NZ // 2):
                put(gz.at[b, zz], gz.at[b, zz], gzs.at[0, b, hop], gzr.at[b, zz], zup, conds[b])
            if j == 0 or (ORDER[j] > 0 and hop < NZ // 2 - 1):
                put(gz.at[b, zz], gz.at[b, zz], gzs.at[1, b, hop], gzr.at[b, zz], zdn, conds[b])
    put(gz.at[0], gsib.at[0], sib_s.at[NG + 4], sib_r.at[NG + 4], sib)
    put(gz.at[1], gsib.at[1], sib_s.at[NG + 5], sib_r.at[NG + 5], sib, first)

    got(xo.at[1 - k], sib_r.at[NG + 2])
    x_ref[...] = xo[...]
    got(gsib.at[0], sib_r.at[NG + 4])

    @pl.when(first)
    def _():
        g_ref[0] = gz[0].reshape(B, B)
        g_ref[1] = gz[1].reshape(B, B)
        g_ref[2] = gsib[0].reshape(B, B)

    @pl.when(k == 1)
    def _():
        got(gsib.at[1], sib_r.at[NG + 5])
        g_ref[0] = gsib[0].reshape(B, B)
        g_ref[1] = gsib[1].reshape(B, B)
        g_ref[2] = gz[0].reshape(B, B)

    for c, cond in sends:
        if cond is None:
            c.wait_send()
        else:
            pl.when(cond)(c.wait_send)


def gather_call(trailing, rows4, grads4):
    dma = pltpu.SemaphoreType.DMA
    vm = pl.BlockSpec(memory_space=pltpu.VMEM)
    return pl.pallas_call(
        gather_kernel,
        out_shape=(
            jax.ShapeDtypeStruct((3, B, B), F32),
            jax.ShapeDtypeStruct((2, ROWS, B), F32),
        ),
        in_specs=[pl.BlockSpec(memory_space=pl.ANY), vm, vm],
        out_specs=(vm, vm),
        scratch_shapes=[
            pltpu.VMEM((2, 512, 1024), F32),
            pltpu.VMEM((2, 512, 1024), BF16),
            pltpu.VMEM((2, 512, 1024), BF16),
            pltpu.VMEM((NG, NZ, 2, ROWS, W), F32),
            pltpu.VMEM((NG, NX, NZ, 2, ROWS, W), F32),
            pltpu.VMEM((NG, NZ, 2 * ROWS, W), F32),
            pltpu.VMEM((NG, NZ, 2 * ROWS, W), F32),
            pltpu.VMEM((2, ROWS, B), F32),
            pltpu.VMEM((2, ROWS, B), F32),
            pltpu.VMEM((2, ROWS, B), F32),
            pltpu.VMEM((NZ, 64, 64), F32),
            pltpu.VMEM((NZ, 64, 64), F32),
            pltpu.VMEM((NZ, 64, 64), F32),
            pltpu.VMEM((2, NY, 8, B), F32),
            pltpu.VMEM((2, NY, 8, B), F32),
            pltpu.VMEM((2, 8, B), F32),
            pltpu.VMEM((2, NX, 8, B), F32),
            pltpu.VMEM((2, NZ, NY, 8, B), F32),
            pltpu.VMEM((2, NZ, NY, 8, B), F32),
            dma((NG + 6,)), dma((NG + 6,)), dma((1,)),
            dma((2, NG, NZ // 2)), dma((NG, NZ)),
            dma((2, NG, NZ)), dma((3, NG, NZ)), dma((NG, NX, NZ)),
            dma((NG, NZ)), dma((NG, NZ)),
            dma((NZ,)), dma((NZ,)),
            dma((2, NY)), dma((2, NY)),
            dma((2, NX)), dma((2, NX)),
            dma((2, NY)), dma((2, NY)),
            dma((2, 2, NZ // 2)), dma((2, NZ)),
        ],
        compiler_params=pltpu.CompilerParams(
            collective_id=0, has_side_effects=True, vmem_limit_bytes=48 * 1024 * 1024
        ),
        name="panel_gather_and_gram",
    )(trailing, rows4, grads4)


def invert(lower, out_ref):
    n = 128
    r = lax.broadcasted_iota(jnp.int32, (n, n), 0)
    c = lax.broadcasted_iota(jnp.int32, (n, n), 1)
    blocks = [lower(q, q) for q in range(4)]
    inv = []
    for a in blocks:
        diag = jnp.sum(jnp.where(r == c, a, 0.0), axis=1, keepdims=True)
        inv.append(jnp.where(r == c, 1.0 / diag, 0.0))
    for lb in range(7):
        mask = ((r >> (lb + 1)) == (c >> (lb + 1))) & ((r >> lb) > (c >> lb))
        for q in range(4):
            cut = jnp.where(mask, blocks[q], 0.0)
            yy = split(inv[q])
            inv[q] = inv[q] - mm_split(yy, split(mm_split(split(cut), yy)))
    zero = jnp.zeros((n, n), F32)
    wide = []
    for h in range(2):
        a, b = inv[2 * h], inv[2 * h + 1]
        low = -mm(b, mm(lower(2 * h + 1, 2 * h), a))
        wide.append(jnp.concatenate([jnp.concatenate([a, zero], 1), jnp.concatenate([low, b], 1)], 0))
    corner = jnp.concatenate(
        [jnp.concatenate([lower(2, 0), lower(2, 1)], 1), jnp.concatenate([lower(3, 0), lower(3, 1)], 1)], 0
    )
    low = -mm(wide[1], mm(corner, wide[0]))
    out_ref[0:256, 0:256] = wide[0]
    out_ref[0:256, 256:512] = jnp.zeros((256, 256), F32)
    out_ref[256:512, 0:256] = low
    out_ref[256:512, 256:512] = wide[1]


def chain_kernel(full_ref, g_ref, x_ref, h_ref, b_ref, c_ref, v1, v2, v1t, e_ref, m_ref, w1, w2):
    def part(p):
        return full_ref[:, p * B : p * B + B]

    def tile(p):
        return lambda i, j: full_ref[128 * i : 128 * i + 128, p * B + 128 * j : p * B + 128 * j + 128]

    r = lax.broadcasted_iota(jnp.int32, (B, B), 0)
    c = lax.broadcasted_iota(jnp.int32, (B, B), 1)

    def lowered(p):
        return jnp.where(r > c, p, jnp.where(r == c, 0.5 * p, 0.0))

    invert(tile(0), v1)
    invert(tile(1), v2)
    v1t[...] = v1[...].T
    v2t = split(v2[...].T)
    vs1 = split(v1[...])
    vs2 = split(v2[...])
    l21 = split(part(2))
    m_ref[...] = mm_split(l21, vs1)
    ms = split(m_ref[...])
    h2 = mm_split(split(x_ref[1]), vs2)
    h_ref[:, B : 2 * B] = h2
    h_ref[:, 0:B] = mm_split(split(x_ref[0]), vs1) - mm_split(split(h2), ms)
    hr2 = mm_split(v2t, split(g_ref[2]))
    hr1 = mm_split(v2t, split(g_ref[1]))
    p2 = part(4) - hr2
    q2 = lowered(mm_split(split(part(1).T), split(jnp.where(r >= c, p2, 0.0))))
    w1[...] = mm_split(split(q2 + q2.T), vs2)
    w2[...] = 0.5 * mm_split(v2t, split(w1[...]))
    p1 = part(3) - hr1
    coupling = mm_split(split(p1), vs1) - 2.0 * mm_split(split(w2[...]), ms)
    e_ref[...] = coupling
    corner = part(5) - mm_split(split(v1t[...]), split(g_ref[0])) + mm_split(split(m_ref[...].T), split(hr1))
    grad = jnp.where(r >= c, corner - mm_split(split(coupling.T), l21), 0.0)
    q1 = lowered(mm_split(split(part(0).T), split(grad)))
    w1[...] = q1 + q1.T
    own = pl.ds(pl.multiple_of(lax.axis_index("row") * 16, 16), 16)
    b_ref[1] = w2[own, :]
    c_ref[...] = e_ref[own, :]
    b_ref[0] = 0.5 * mm(mm(v1t[own, :], w1[...]), v1[...])


def chain_call(full, grams, xrows):
    vm = pl.BlockSpec(memory_space=pltpu.VMEM)
    square = pltpu.VMEM((B, B), F32)
    return pl.pallas_call(
        chain_kernel,
        out_shape=(
            jax.ShapeDtypeStruct((ROWS, 2 * B), F32),
            jax.ShapeDtypeStruct((2, 16, B), F32),
            jax.ShapeDtypeStruct((16, B), F32),
        ),
        in_specs=[vm, vm, vm],
        out_specs=(vm, vm, vm),
        scratch_shapes=[square] * 7,
        compiler_params=pltpu.CompilerParams(vmem_limit_bytes=48 * 1024 * 1024),
        name="small_block_chain",
    )(full, grams, xrows)


def per_device(
    trailing_grad, factor_rows, factor_grad, diag_factor, cross_factor, cross_grad, corner_grad
):
    col_place = lax.axis_index("col")
    cross_wide = lax.all_gather(cross_grad, "col", axis=1, tiled=True)
    corner_wide = lax.all_gather(corner_grad, "col", axis=1, tiled=True)
    small = jnp.concatenate([diag_factor[0], diag_factor[1], cross_factor, cross_wide, corner_wide], 1)
    full = lax.all_gather(small, "row", axis=0, tiled=True)
    rows4 = factor_rows.reshape(ROWS, 2, NG, W).transpose(1, 2, 0, 3)
    grads4 = factor_grad.reshape(ROWS, 2, B).transpose(1, 0, 2)
    grams, xrows = gather_call(trailing_grad, rows4, grads4)
    rows_grad, blocks, coupling = chain_call(full, grams, xrows)
    corner_cols = corner_grad.shape[1]
    blocks_grad = lax.dynamic_slice(blocks, (0, 0, col_place * corner_cols), (2, 16, corner_cols))
    coupling_grad = lax.dynamic_slice(coupling, (0, col_place * corner_cols), (16, corner_cols))
    return (rows_grad, blocks_grad, coupling_grad)


def solution(mesh):
    return jax.shard_map(
        per_device,
        mesh=mesh,
        in_specs=(
            P("row", "col"),
            P(("row", "col"), None),
            P(("row", "col"), None),
            P(None, "row", None),
            P("row", None),
            P("row", "col"),
            P("row", "col"),
        ),
        out_specs=(P(("row", "col"), None), P(None, "row", "col"), P("row", "col")),
        check_vma=False,
    )
```

```python
import functools

import jax
import jax.numpy as jnp
from jax import lax
from jax.experimental import pallas as pl
from jax.experimental.pallas import tpu as pltpu
from jax.sharding import PartitionSpec as P

MESH = pl.DeviceIdType.MESH
F32 = jnp.float32
BF16 = jnp.bfloat16
NX, NY, NZ = 4, 8, 8
NG = 2
B = 512
W = B // NG
W2 = B // 2
ROWS = 32
ORDER = (0, -1, 1, -2, 2, -3, 3, -4)
STEPS = sorted(((g, o) for g in range(NG) for o in ORDER), key=lambda s: (abs(s[1]) + 2 * s[0], s[0]))
STEP_COUNT = len(STEPS)
LAST0 = max(i for i, s in enumerate(STEPS) if s[0] == 0)


def pick(values, n):
    words = [sum(v << (4 * i) for i, v in enumerate(values[h : h + 8])) for h in (0, 8)]
    return (jnp.where(n < 8, words[0], words[1]) >> (4 * lax.rem(n, 8))) & 7


def split(a):
    hi = a.astype(BF16)
    return hi, (a - hi.astype(F32)).astype(BF16)


def dot(a, b):
    return jnp.dot(a, b, preferred_element_type=F32)


def mm_split(a, b):
    return dot(a[0], b[0]) + (dot(a[0], b[1]) + dot(a[1], b[0]))


def mm(a, b):
    return mm_split(split(a), split(b))


def panel_kernel(
    t_ref, r_ref, f_ref, diag_ref, cross_ref, cg_ref, co_ref,
    rows_ref, b_ref, c_ref,
    tbuf, thi, tlo, band, rbuf, psum, sbuf, fbuf, xr, xo, xst, xs, xs2, gm, gy, sg, gx, gz,
    lloc, cgl, col_, lbuf, cgb, ltr, fold, v1, v2, v1t, v2t, mmat, mt, w1, w2, sbm, cpl, outp,
    sib_s, sib_r, loc, zs, zr, ys, xsm, rr, ss, sr, as_, ar, gys, gyr, gxs, gxr, gas, gar, gbs, gbr, gzs, gzr,
    gws, gwr, lxs, lxr, lys, lyr, lzs, lzr, lfs, lfr, cs_, cr,
):
    local = [
        pltpu.make_async_copy(diag_ref, lloc.at[pl.ds(0, 2)], loc.at[1]),
        pltpu.make_async_copy(cross_ref, lloc.at[2], loc.at[2]),
        pltpu.make_async_copy(cg_ref, cgl, loc.at[3]),
        pltpu.make_async_copy(co_ref, col_, loc.at[4]),
    ]
    for c in local:
        c.start()
    row = lax.axis_index("row")
    col = lax.axis_index("col")
    y, x = row // NX, lax.rem(row, NX)
    z, k = col // 2, lax.rem(col, 2)

    def dev(px, py, pz, pk):
        return {"row": py * NX + px, "col": pz * 2 + pk}

    def up(v, s, n):
        return lax.rem(v + (s + n), n)

    sib = dev(x, y, z, 1 - k)
    zpeer = [dev(x, y, up(z, s, NZ), k) for s in range(1, NZ)]
    ypeer = [dev(x, up(y, s, NY), z, k) for s in range(1, NY)]
    xpeer = [dev(up(x, s, NX), y, z, k) for s in range(1, NX)]
    zup, zdn = zpeer[0], zpeer[-1]
    yup, ydn = ypeer[0], ypeer[-1]
    xup, xdn = xpeer[0], xpeer[-1]
    d = up(y - z, NY, NY)

    barrier = pltpu.get_barrier_semaphore()
    partners = [sib] + zpeer + ypeer + xpeer
    for p in partners:
        pl.semaphore_signal(barrier, inc=1, device_id=p, device_id_type=MESH)
    pl.semaphore_wait(barrier, len(partners))

    sends = []
    mode = ["start"]

    def put(src, dst, ssem, rsem, target, cond=None):
        c = pltpu.make_async_remote_copy(
            src_ref=src, dst_ref=dst, send_sem=ssem, recv_sem=rsem, device_id=target, device_id_type=MESH
        )
        act = c.wait_send if mode[0] == "finish" else c.start
        if cond is None:
            act()
        else:
            pl.when(cond)(act)
        if mode[0] == "start":
            sends.append((c, cond))

    def got(ref, sem):
        if mode[0] != "finish":
            pltpu.make_async_remote_copy(
                src_ref=ref, dst_ref=ref, send_sem=sem, recv_sem=sem, device_id=sib, device_id_type=MESH
            ).wait_recv()

    first = k == 0
    for g in range(NG):
        lanes = pl.ds(pl.multiple_of((1 - k) * B + g * W, 128), W)
        put(r_ref.at[:, lanes], band.at[g, z, k], sib_s.at[g], sib_r.at[g], sib)
    rcopies = []
    for g in range(NG):
        lanes = pl.ds(pl.multiple_of(k * B + g * W, 128), W)
        rcopies.append(pltpu.make_async_copy(r_ref.at[:, lanes], band.at[g, z, k], loc.at[5 + g]))
        rcopies[-1].start()
    put(t_ref, tbuf.at[k], sib_s.at[NG], sib_r.at[NG], sib)
    tcopy = pltpu.make_async_copy(t_ref, tbuf.at[k], loc.at[0])
    tcopy.start()
    put(f_ref.at[:, pl.ds(pl.multiple_of((1 - k) * B, 128), B)], fbuf.at[k], sib_s.at[NG + 1], sib_r.at[NG + 1], sib)
    fcopy = pltpu.make_async_copy(f_ref.at[:, pl.ds(pl.multiple_of(k * B, 128), B)], fbuf.at[k], loc.at[5 + NG])
    fcopy.start()
    for c in local:
        c.wait()
    quarter = lax.rem(z, 4)
    half = pl.ds(3 * k, 3)
    for p in range(4):

        @pl.when(quarter == p)
        def _():
            for q in range(3):
                lbuf[p, y, x, 2 * q : 2 * q + 2] = lloc[q, :, 128 * p : 128 * p + 128].reshape(2, 8, 128)

    for s in range(1, NX):
        put(
            lbuf.at[quarter, y, x, half], lbuf.at[quarter, y, x, half], lxs.at[s], lxr.at[x], xpeer[s - 1]
        )
    cgb[z, k] = jnp.zeros((16, 128), F32)
    cgb[z, k, :, 0:64] = cgl[...]
    cgb[z, k, :, 64:96] = col_[...]
    put(cgb.at[z, k], cgb.at[z, k], sib_s.at[NG + 4], sib_r.at[NG + 4], sib)

    def l_rows():
        for s in range(1, NX):
            frm = up(x, s, NX)
            got(lbuf.at[quarter, y, frm, half], lxr.at[frm])
        for s in range(1, NY):
            put(lbuf.at[quarter, y, :, half], lbuf.at[quarter, y, :, half], lys.at[s], lyr.at[y], ypeer[s - 1])

    def l_planes():
        for s in range(1, NY):
            frm = up(y, s, NY)
            got(lbuf.at[quarter, frm, :, half], lyr.at[frm])
        for i, to in enumerate((zup, zdn)):
            put(lbuf.at[quarter, :, :, half], lbuf.at[quarter, :, :, half], lzs.at[i], lzr.at[i], to)

    def l_far():
        below, above = up(quarter, 3, 4), up(quarter, 1, 4)
        got(lbuf.at[below, :, :, half], lzr.at[0])
        part = lbuf.at[below, pl.ds(0, NY // 2), :, half]
        put(part, part, lfs.at[0], lfr.at[0], zup)
        got(lbuf.at[above, :, :, half], lzr.at[1])
        part = lbuf.at[above, pl.ds(NY // 2, NY // 2), :, half]
        put(part, part, lfs.at[1], lfr.at[1], zdn)

    def l_cores():
        far = up(quarter, 2, 4)
        for i in range(2):
            got(lbuf.at[far, pl.ds(i * NY // 2, NY // 2), :, half], lfr.at[i])
        put(lbuf.at[:, :, :, half], lbuf.at[:, :, :, half], sib_s.at[NG + 5], sib_r.at[NG + 5], sib)

    def adjoint_rows():
        got(cgb.at[z, 1 - k], sib_r.at[NG + 4])
        for s in range(1, NZ):
            put(cgb.at[z], cgb.at[z], cs_.at[s], cr.at[z], zpeer[s - 1])

    hops = jnp.where(d <= NY // 2, d, NY - d)
    lag_b = 2 * hops
    lag_d = lag_b + 2
    lag_e = lag_d + 2
    background = {2: l_rows, 8: l_planes, 10: adjoint_rows, 16: l_far, 20: l_cores}

    def step(n):
        o = pick([st[1] + 4 for st in STEPS], n)
        return pick([st[0] for st in STEPS], n), o, lax.rem(z + o + NZ - 4, NZ)

    def stage_a(n):
        g, o, zz = step(n)
        if mode[0] != "finish":

            @pl.when(o == 4)
            def _():
                pltpu.make_async_copy(band.at[g, z, k], band.at[g, z, k], loc.at[5 + g]).wait()
                got(band.at[g, z, 1 - k], sib_r.at[g])

            @pl.when(o != 4)
            def _():
                got(band.at[g, zz], zr.at[g, zz])

        chunk = band.at[g, zz]
        put(chunk, chunk, zs.at[0, g, o], zr.at[g, zz], zup, jnp.logical_and(o >= 1, o <= 4))
        put(chunk, chunk, zs.at[1, g, o], zr.at[g, zz], zdn, jnp.logical_and(o >= 4, o <= 6))
        put(chunk, rbuf.at[g, x, zz], ys.at[0, g, o], rr.at[g, x, zz], yup, d == 0)
        put(chunk, rbuf.at[g, x, zz], ys.at[1, g, o], rr.at[g, x, zz], ydn, d == 0)
        if mode[0] != "finish":

            @pl.when(d == 0)
            def _():
                rbuf[g, x, zz] = band[g, zz]

    def stage_b(n):
        g, o, zz = step(n)
        slot, sem = rbuf.at[g, x, zz], rr.at[g, x, zz]
        if mode[0] != "finish":

            @pl.when(d != 0)
            def _():
                got(slot, sem)

        put(slot, slot, ys.at[0, g, o], sem, yup, jnp.logical_and(d >= 1, d <= 3))
        put(slot, slot, ys.at[1, g, o], sem, ydn, d >= 6)
        put(slot, slot, xsm.at[0, g, o], sem, xup)
        put(slot, slot, xsm.at[1, g, o], sem, xdn)

    def stage_d(n):
        g, o, zz = step(n)
        left, right = up(x, -1, NX), up(x, 1, NX)
        got(rbuf.at[g, left, zz], rr.at[g, left, zz])
        got(rbuf.at[g, right, zz], rr.at[g, right, zz])
        even = lax.rem(o, 2) == 0
        chunk = rbuf.at[g, left, zz]
        put(chunk, chunk, xsm.at[2, g, o], rr.at[g, left, zz], xup, even)
        chunk = rbuf.at[g, right, zz]
        put(chunk, chunk, xsm.at[2, g, o], rr.at[g, right, zz], xdn, jnp.logical_not(even))

    def stage_e(n):
        g, o, zz = step(n)
        far = up(x, 2, NX)
        got(rbuf.at[g, far, zz], rr.at[g, far, zz])

    def piece(g, xx):
        b = split(rbuf[g, xx].reshape(NZ * 2 * ROWS, W))
        psum[g] += mm_split((thi[xx], tlo[xx]), b).reshape(NZ, 2 * ROWS, W)

    def scatter(g):
        for s in range(1, NZ):
            to = up(z, s, NZ)
            put(psum.at[g, to], sbuf.at[g, z], ss.at[g, s], sr.at[g, z], zpeer[s - 1])
        if mode[0] != "finish":
            sbuf[g, z] = psum[g, z]

    def within(n, fn):
        @pl.when(jnp.logical_and(n >= 0, n < STEP_COUNT))
        def _():
            fn(n)

    def first_group(n):
        @pl.when(n == 0)
        def _():
            tcopy.wait()
            got(tbuf.at[1 - k], sib_r.at[NG])

        @pl.when(jnp.logical_and(n >= 0, n < NX))
        def _():
            lanes = pl.ds(pl.multiple_of(lax.rem(n, 2) * 512, 128), 512)
            thi[n], tlo[n] = split(tbuf[n // 2, :, lanes])
            piece(0, n)

        @pl.when(n == NX)
        def _():
            scatter(0)

    psum[...] = jnp.zeros_like(psum)
    mode[0] = "loop"

    def body(i, carry):
        for at, task in background.items():
            pl.when(i == at)(task)
        within(i, stage_a)
        within(i - lag_b, stage_b)
        within(i - lag_d, stage_d)
        within(i - lag_e, stage_e)
        first_group(i - lag_e - LAST0 - 1)
        return carry

    lax.fori_loop(0, STEP_COUNT + NY + 4 + 1, body, 0)
    mode[0] = "start"
    for xx in range(NX):
        piece(1, xx)
    scatter(1)

    got(lbuf.at[:, :, :, pl.ds(3 * (1 - k), 3)], sib_r.at[NG + 5])

    def factor(q):
        return jnp.concatenate([lbuf[p, :, :, 2 * q : 2 * q + 2].reshape(B, 128) for p in range(4)], 1)

    def tile(q):
        return lambda i, j: lbuf[j, 2 * i : 2 * i + 2, :, 2 * q : 2 * q + 2].reshape(128, 128)

    invert(tile(0), v1)
    invert(tile(1), v2)
    v1t[...] = v1[...].T
    v2t[...] = v2[...].T
    mmat[...] = mm(factor(2), v1[...])
    mt[...] = mmat[...].T
    for q in range(3):
        ltr[q] = lloc[q].T
    for s in range(1, NZ):
        frm = up(z, s, NZ)
        got(cgb.at[frm], cr.at[frm])
    mine = pl.ds(pl.multiple_of(z * 64, 64), 64)

    def cross_half(lo):
        return jnp.concatenate([cgb[c // 2, c % 2, :, 0:64] for c in range(lo, lo + NZ)], 1)

    @pl.when(first)
    def _():
        corner = jnp.concatenate([cgb[c // 2, c % 2, :, 64:96] for c in range(2 * NZ)], 1)
        cross = split(cross_half(0))
        fold[0] = mm(ltr[0, mine, :], corner) + mm_split(split(ltr[2, mine, :]), cross)
        fold[1] = mm_split(split(ltr[1, mine, :]), cross)

    @pl.when(k == 1)
    def _():
        fold[0] = mm(ltr[1, mine, :], cross_half(NZ))

    fcopy.wait()
    got(fbuf.at[1 - k], sib_r.at[NG + 1])
    for g in range(NG):
        for s in range(1, NZ):
            frm = up(z, s, NZ)
            got(sbuf.at[g, frm], sr.at[g, frm])
        total = sbuf[g, 0]
        for s in range(1, NZ):
            total = total + sbuf[g, s]
        lanes = slice(g * W, g * W + W)
        xr[:, :, lanes] = fbuf[:, :, lanes] - 2.0 * total.reshape(2, ROWS, W)

    xall = xr[...].reshape(2 * ROWS, B)
    for s in range(NZ):
        xst[s] = xall[:, 64 * s : 64 * s + 64]
    for s in range(1, NZ):
        to = up(z, s, NZ)
        put(xst.at[to], xs.at[z], as_.at[s], ar.at[z], zpeer[s - 1])
    put(xr.at[1 - k], xo.at[k], sib_s.at[NG + 2], sib_r.at[NG + 2], sib)
    xo[k] = xr[k]
    xs[z] = xst[z]
    for s in range(1, NZ):
        frm = up(z, s, NZ)
        got(xs.at[frm], ar.at[frm])
    put(xs, xs2, sib_s.at[NG + 3], sib_r.at[NG + 3], sib, k == 1)

    def gram(b, src):
        a = split(src[...].reshape(NZ * 64, 64).T)
        for g in range(NG):
            bb = split(band[g].reshape(NZ * 64, W))
            lanes = slice(g * W, g * W + W)
            gm[b, :, :, lanes] = (mm_split(a, bb) - fold[b, :, lanes]).reshape(NY, 8, W)

    def plane_reduce_start(b, cond):
        for s in range(1, NY):
            to = up(y, s, NY)
            put(gm.at[b, to], gy.at[b, y], gys.at[b, s], gyr.at[b, y], ypeer[s - 1], cond)

    gram(0, xs)
    plane_reduce_start(0, None)

    @pl.when(first)
    def _():
        got(xs2, sib_r.at[NG + 3])
        gram(1, xs2)

    plane_reduce_start(1, first)
    conds = (None, first)

    def when(cond, fn):
        if cond is None:
            fn()
        else:
            pl.when(cond)(fn)

    def y_sum(b):
        gy[b, y] = gm[b, y]
        for s in range(1, NY):
            frm = up(y, s, NY)
            got(gy.at[b, frm], gyr.at[b, frm])
        total = gy[b, 0]
        for s in range(1, NY):
            total = total + gy[b, s]
        sg[b] = total
        gx[b, x] = total

    def x_sum(b):
        for s in range(1, NX):
            frm = up(x, s, NX)
            got(gx.at[b, frm], gxr.at[b, frm])
        total = (gx[b, 0] + gx[b, 1]) + (gx[b, 2] + gx[b, 3])
        gz[b, 0, z, y] = total[:, 0:W2]
        gz[b, 1, z, y] = total[:, W2:B]

    def y_wait(b):
        for s in range(1, NY):
            frm = up(y, s, NY)
            got(gz.at[b, 0, z, frm], gar.at[b, frm])
        for s in range(1, NZ):
            frm = up(z, s, NZ)
            got(gz.at[b, 1, frm, y], gbr.at[b, frm])

    for b in range(2):
        when(conds[b], functools.partial(y_sum, b))
        for s in range(1, NX):
            put(sg.at[b], gx.at[b, x], gxs.at[b, s], gxr.at[b, x], xpeer[s - 1], conds[b])
    got(xo.at[1 - k], sib_r.at[NG + 2])
    h2 = mm(xo[1], v2[...])
    rows_ref[:, B : 2 * B] = h2
    rows_ref[:, 0:B] = mm(xo[0], v1[...]) - mm(h2, mmat[...])

    for b in range(2):
        when(conds[b], functools.partial(x_sum, b))
        for s in range(1, NY):
            put(gz.at[b, 0, z, y], gz.at[b, 0, z, y], gas.at[b, s], gar.at[b, y], ypeer[s - 1], conds[b])
        for s in range(1, NZ):
            put(gz.at[b, 1, z, y], gz.at[b, 1, z, y], gbs.at[b, s], gbr.at[b, z], zpeer[s - 1], conds[b])
    for j in range(NZ):
        zz, yy = up(z, ORDER[j], NZ), up(y, ORDER[j], NY)
        hop = abs(ORDER[j])
        for b in range(2):
            chunk, other = gz.at[b, 0, zz], gz.at[b, 1, :, yy]
            if j == 0:
                when(conds[b], functools.partial(y_wait, b))
            else:
                when(conds[b], functools.partial(got, chunk, gzr.at[b, zz]))
                when(conds[b], functools.partial(got, other, gwr.at[b, yy]))
            if j == 0 or (ORDER[j] < 0 and hop < NZ // 2):
                put(chunk, chunk, gzs.at[0, b, hop], gzr.at[b, zz], zup, conds[b])
                put(other, other, gws.at[0, b, hop], gwr.at[b, yy], yup, conds[b])
            if j == 0 or (ORDER[j] > 0 and hop < NZ // 2 - 1):
                put(chunk, chunk, gzs.at[1, b, hop], gzr.at[b, zz], zdn, conds[b])
                put(other, other, gws.at[1, b, hop], gwr.at[b, yy], ydn, conds[b])

    def gram_total(b):
        return jnp.concatenate([gz[b, 0].reshape(B, W2), gz[b, 1].reshape(B, W2)], 1)

    r = lax.broadcasted_iota(jnp.int32, (B, B), 0)
    c = lax.broadcasted_iota(jnp.int32, (B, B), 1)
    own = pl.ds(pl.multiple_of(row * 16, 16), 16)

    def lowered(p):
        return jnp.where(r > c, p, jnp.where(r == c, 0.5 * p, 0.0))

    @pl.when(k == 1)
    def _():
        left = split(v2t[...])
        p2 = mm_split(left, split(gram_total(0)))
        q2 = lowered(mm(factor(1).T, jnp.where(r >= c, -p2, 0.0)))
        w1[...] = mm(q2 + q2.T, v2[...])
        sbm[...] = 0.5 * mm_split(left, split(w1[...]))

    put(sbm, sbm, sib_s.at[NG + 6], sib_r.at[NG + 6], sib, k == 1)

    @pl.when(first)
    def _():
        p1 = split(-mm(v2t[...], gram_total(1)))
        w1[...] = mm_split(p1, split(v1[...]))
        w2[...] = mm(v1t[...], gram_total(0)) + mm_split(split(mt[...]), p1)
        got(sbm, sib_r.at[NG + 6])
        coupling = w1[...] - 2.0 * mm(sbm[...], mmat[...])
        cpl[...] = coupling
        outp[0] = cpl[own, :]
        grad = jnp.where(r >= c, -w2[...] - mm(coupling.T, factor(2)), 0.0)
        q1 = lowered(mm(factor(0).T, grad))
        w1[...] = q1 + q1.T
        outp[1] = 0.5 * mm(mm(v1t[own, :], w1[...]), v1[...])

    put(outp, outp, sib_s.at[NG + 7], sib_r.at[NG + 7], sib, first)

    @pl.when(k == 1)
    def _():
        got(outp, sib_r.at[NG + 7])

    shift = lax.rem(B - col * 32, B)
    c_ref[...] = pltpu.roll(outp[0], shift, 1)[:, 0:32]
    b_ref[0] = pltpu.roll(outp[1], shift, 1)[:, 0:32]
    b_ref[1] = pltpu.roll(sbm[own, :], shift, 1)[:, 0:32]

    for c, cond in sends:
        if cond is None:
            c.wait_send()
        else:
            pl.when(cond)(c.wait_send)
    mode[0] = "finish"
    for task in background.values():
        task()
    scatter(0)

    def sent(n, carry):
        stage_a(n)
        stage_b(n)
        stage_d(n)
        return carry

    lax.fori_loop(0, STEP_COUNT, sent, 0)


def panel_call(*args):
    dma = pltpu.SemaphoreType.DMA
    vm = pl.BlockSpec(memory_space=pltpu.VMEM)
    hbm = pl.BlockSpec(memory_space=pl.ANY)
    square = pltpu.VMEM((B, B), F32)
    return pl.pallas_call(
        panel_kernel,
        out_shape=(
            jax.ShapeDtypeStruct((ROWS, 2 * B), F32),
            jax.ShapeDtypeStruct((2, 16, 32), F32),
            jax.ShapeDtypeStruct((16, 32), F32),
        ),
        in_specs=[hbm] * 7,
        out_specs=(vm, vm, vm),
        scratch_shapes=[
            pltpu.VMEM((2, 512, 1024), F32),
            pltpu.VMEM((NX, 512, 512), BF16),
            pltpu.VMEM((NX, 512, 512), BF16),
            pltpu.VMEM((NG, NZ, 2, ROWS, W), F32),
            pltpu.VMEM((NG, NX, NZ, 2, ROWS, W), F32),
            pltpu.VMEM((NG, NZ, 2 * ROWS, W), F32),
            pltpu.VMEM((NG, NZ, 2 * ROWS, W), F32),
            pltpu.VMEM((2, ROWS, B), F32),
            pltpu.VMEM((2, ROWS, B), F32),
            pltpu.VMEM((2, ROWS, B), F32),
            pltpu.VMEM((NZ, 64, 64), F32),
            pltpu.VMEM((NZ, 64, 64), F32),
            pltpu.VMEM((NZ, 64, 64), F32),
            pltpu.VMEM((2, NY, 8, B), F32),
            pltpu.VMEM((2, NY, 8, B), F32),
            pltpu.VMEM((2, 8, B), F32),
            pltpu.VMEM((2, NX, 8, B), F32),
            pltpu.VMEM((2, 2, NZ, NY, 8, W2), F32),
            pltpu.VMEM((3, 16, B), F32),
            pltpu.VMEM((16, 64), F32),
            pltpu.VMEM((16, 32), F32),
            pltpu.VMEM((4, NY, NX, 6, 8, 128), F32),
            pltpu.VMEM((NZ, 2, 16, 128), F32),
            pltpu.VMEM((3, B, 16), F32),
            pltpu.VMEM((2, 64, B), F32),
        ]
        + [square] * 10
        + [
            pltpu.VMEM((2, 16, B), F32),
            dma((NG + 8,)), dma((NG + 8,)), dma((NG + 6,)),
            dma((2, NG, NZ)), dma((NG, NZ)),
            dma((2, NG, NZ)), dma((3, NG, NZ)), dma((NG, NX, NZ)),
            dma((NG, NZ)), dma((NG, NZ)),
            dma((NZ,)), dma((NZ,)),
            dma((2, NY)), dma((2, NY)),
            dma((2, NX)), dma((2, NX)),
            dma((2, NY)), dma((2, NY)),
            dma((2, NZ)), dma((2, NZ)),
            dma((2, 2, NZ // 2)), dma((2, NZ)),
            dma((2, 2, NY // 2)), dma((2, NY)),
            dma((NX,)), dma((NX,)), dma((NY,)), dma((NY,)),
            dma((2,)), dma((2,)), dma((2,)), dma((2,)),
            dma((NZ,)), dma((NZ,)),
        ],
        compiler_params=pltpu.CompilerParams(
            collective_id=0, has_side_effects=True, vmem_limit_bytes=52 * 1024 * 1024
        ),
        name="panel_adjoint",
    )(*args)


def invert(lower, out_ref):
    n = 128
    r = lax.broadcasted_iota(jnp.int32, (n, n), 0)
    c = lax.broadcasted_iota(jnp.int32, (n, n), 1)
    blocks = [lower(q, q) for q in range(4)]
    inv = []
    for a in blocks:
        diag = jnp.sum(jnp.where(r == c, a, 0.0), axis=1, keepdims=True)
        inv.append(jnp.where(r == c, 1.0 / diag, 0.0))
    for lb in range(7):
        mask = ((r >> (lb + 1)) == (c >> (lb + 1))) & ((r >> lb) > (c >> lb))
        for q in range(4):
            cut = jnp.where(mask, blocks[q], 0.0)
            yy = split(inv[q])
            inv[q] = inv[q] - mm_split(yy, split(mm_split(split(cut), yy)))
    zero = jnp.zeros((n, n), F32)
    wide = []
    for h in range(2):
        a, b = inv[2 * h], inv[2 * h + 1]
        low = -mm(b, mm(lower(2 * h + 1, 2 * h), a))
        wide.append(jnp.concatenate([jnp.concatenate([a, zero], 1), jnp.concatenate([low, b], 1)], 0))
    corner = jnp.concatenate(
        [jnp.concatenate([lower(2, 0), lower(2, 1)], 1), jnp.concatenate([lower(3, 0), lower(3, 1)], 1)], 0
    )
    low = -mm(wide[1], mm(corner, wide[0]))
    out_ref[0:256, 0:256] = wide[0]
    out_ref[0:256, 256:512] = jnp.zeros((256, 256), F32)
    out_ref[256:512, 0:256] = low
    out_ref[256:512, 256:512] = wide[1]


def per_device(*args):
    return panel_call(*args)


def solution(mesh):
    return jax.shard_map(
        per_device,
        mesh=mesh,
        in_specs=(
            P("row", "col"),
            P(("row", "col"), None),
            P(("row", "col"), None),
            P(None, "row", None),
            P("row", None),
            P("row", "col"),
            P("row", "col"),
        ),
        out_specs=(P(("row", "col"), None), P(None, "row", "col"), P("row", "col")),
        check_vma=False,
    )
```

```python
import functools

import jax
import jax.numpy as jnp
from jax import lax
from jax.experimental import pallas as pl
from jax.experimental.pallas import tpu as pltpu
from jax.sharding import PartitionSpec as P

MESH = pl.DeviceIdType.MESH
F32 = jnp.float32
BF16 = jnp.bfloat16
NX, NY, NZ = 4, 8, 8
NG = 2
B = 512
W = B // NG
W2 = B // 2
ROWS = 32
ORDER = (0, -1, 1, -2, 2, -3, 3, -4)
STEPS = [(g, o) for g in range(NG) for o in ORDER]
STEP_COUNT = len(STEPS)
LAST0 = NZ - 1


def pick(values, n):
    words = [sum(v << (4 * i) for i, v in enumerate(values[h : h + 8])) for h in (0, 8)]
    return (jnp.where(n < 8, words[0], words[1]) >> (4 * lax.rem(n, 8))) & 7


def split(a):
    hi = a.astype(BF16)
    return hi, (a - hi.astype(F32)).astype(BF16)


def dot(a, b):
    return jnp.dot(a, b, preferred_element_type=F32)


def mm_split(a, b):
    return dot(a[0], b[0]) + (dot(a[0], b[1]) + dot(a[1], b[0]))


def mm(a, b):
    return mm_split(split(a), split(b))


def panel_kernel(
    t_ref, r_ref, f_ref, diag_ref, cross_ref, cg_ref, co_ref,
    rows_ref, b_ref, c_ref,
    tbuf, thi, tlo, band, rbuf, psum, sbuf, fbuf, xr, xo, xst, xs, xs2, gm, gy, sg, gx, gz,
    lloc, cgl, col_, lbuf, cgb, ltr, fold, v1, v2, v1t, v2t, mmat, mt, w1, w2, sbm, cpl, outp,
    sib_s, sib_r, loc, zs, zr, ys, xsm, rr, ss, sr, as_, ar, gys, gyr, gxs, gxr, gas, gar, gbs, gbr, gzs, gzr,
    gws, gwr, lys, lyr, lzs, lzr, lfs, lfr, cs_, cr,
):
    local = [
        pltpu.make_async_copy(diag_ref, lloc.at[pl.ds(0, 2)], loc.at[1]),
        pltpu.make_async_copy(cross_ref, lloc.at[2], loc.at[2]),
        pltpu.make_async_copy(cg_ref, cgl, loc.at[3]),
        pltpu.make_async_copy(co_ref, col_, loc.at[4]),
    ]
    for c in local:
        c.start()
    row = lax.axis_index("row")
    col = lax.axis_index("col")
    y, x = row // NX, lax.rem(row, NX)
    z, k = col // 2, lax.rem(col, 2)

    def dev(px, py, pz, pk):
        return {"row": py * NX + px, "col": pz * 2 + pk}

    def up(v, s, n):
        return lax.rem(v + (s + n), n)

    sib = dev(x, y, z, 1 - k)
    zpeer = [dev(x, y, up(z, s, NZ), k) for s in range(1, NZ)]
    ypeer = [dev(x, up(y, s, NY), z, k) for s in range(1, NY)]
    xpeer = [dev(up(x, s, NX), y, z, k) for s in range(1, NX)]
    zup, zdn = zpeer[0], zpeer[-1]
    yup, ydn = ypeer[0], ypeer[-1]
    xup, xdn = xpeer[0], xpeer[-1]
    d = up(y - z, NY, NY)

    barrier = pltpu.get_barrier_semaphore()
    partners = [sib] + zpeer + ypeer + xpeer
    for p in partners:
        pl.semaphore_signal(barrier, inc=1, device_id=p, device_id_type=MESH)

    swap = [dev(x, z, y, k), dev(x, z, y, 1 - k)]

    @pl.when(d != 0)
    def _():
        for p in swap:
            pl.semaphore_signal(barrier, inc=1, device_id=p, device_id_type=MESH)

    pl.semaphore_wait(barrier, len(partners) + jnp.where(d == 0, 0, 2))

    sends = []
    mode = ["start"]

    def put(src, dst, ssem, rsem, target, cond=None):
        c = pltpu.make_async_remote_copy(
            src_ref=src, dst_ref=dst, send_sem=ssem, recv_sem=rsem, device_id=target, device_id_type=MESH
        )
        act = c.wait_send if mode[0] == "finish" else c.start
        if cond is None:
            act()
        else:
            pl.when(cond)(act)
        if mode[0] == "start":
            sends.append((c, cond))

    def got(ref, sem):
        if mode[0] != "finish":
            pltpu.make_async_remote_copy(
                src_ref=ref, dst_ref=ref, send_sem=sem, recv_sem=sem, device_id=sib, device_id_type=MESH
            ).wait_recv()

    first = k == 0
    rcopies = []
    for g in range(NG):
        ours = r_ref.at[:, pl.ds(pl.multiple_of(k * B + g * W, 128), W)]
        theirs = r_ref.at[:, pl.ds(pl.multiple_of((1 - k) * B + g * W, 128), W)]
        slot, sem = rbuf.at[g, x, z, k], rr.at[g, x, z]
        put(ours, slot, sib_s.at[NG + 8 + g], sem, swap[0], d != 0)
        put(theirs, slot, sib_s.at[NG + 10 + g], sem, swap[1])
        rcopies.append((pltpu.make_async_copy(ours, slot, sem), d == 0))
        pl.when(d == 0)(rcopies[-1][0].start)
    for g in range(NG):
        ours = r_ref.at[:, pl.ds(pl.multiple_of(k * B + g * W, 128), W)]
        theirs = r_ref.at[:, pl.ds(pl.multiple_of((1 - k) * B + g * W, 128), W)]
        put(theirs, band.at[g, z, k], sib_s.at[g], sib_r.at[g], sib)
        pltpu.make_async_copy(ours, band.at[g, z, k], loc.at[5 + g]).start()
    put(t_ref, tbuf.at[k], sib_s.at[NG], sib_r.at[NG], sib)
    tcopy = pltpu.make_async_copy(t_ref, tbuf.at[k], loc.at[0])
    tcopy.start()
    put(f_ref.at[:, pl.ds(pl.multiple_of((1 - k) * B, 128), B)], fbuf.at[k], sib_s.at[NG + 1], sib_r.at[NG + 1], sib)
    fcopy = pltpu.make_async_copy(f_ref.at[:, pl.ds(pl.multiple_of(k * B, 128), B)], fbuf.at[k], loc.at[5 + NG])
    fcopy.start()
    for c in local:
        c.wait()
    half = pl.ds(3 * k, 3)
    for q in range(3):
        for p in range(4):
            lbuf[p, y, x, 2 * q : 2 * q + 2] = lloc[q, :, 128 * p : 128 * p + 128].reshape(2, 8, 128)
    cgb[z, k] = jnp.zeros((16, 128), F32)
    cgb[z, k, :, 0:64] = cgl[...]
    cgb[z, k, :, 64:96] = col_[...]
    put(cgb.at[z, k], cgb.at[z, k], sib_s.at[NG + 4], sib_r.at[NG + 4], sib)

    def l_rows():
        part = lbuf.at[:, y, x, half]
        for s in range(1, NY):
            put(part, part, lys.at[s], lyr.at[y], ypeer[s - 1])

    def l_planes():
        for s in range(1, NY):
            frm = up(y, s, NY)
            got(lbuf.at[:, frm, x, half], lyr.at[frm])
        part = lbuf.at[:, :, x, half]
        for i, to in enumerate((xup, xdn)):
            put(part, part, lzs.at[i], lzr.at[i], to)

    def l_far():
        for i, (to, frm) in enumerate(((xup, up(x, -1, NX)), (xdn, up(x, 1, NX)))):
            got(lbuf.at[:, :, frm, half], lzr.at[i])
            part = lbuf.at[pl.ds(2 * i, 2), :, frm, half]
            put(part, part, lfs.at[i], lfr.at[i], to)

    def l_cores():
        far = up(x, 2, NX)
        for i in range(2):
            got(lbuf.at[pl.ds(2 * i, 2), :, far, half], lfr.at[i])
        put(lbuf.at[:, :, :, half], lbuf.at[:, :, :, half], sib_s.at[NG + 5], sib_r.at[NG + 5], sib)

    def adjoint_rows():
        got(cgb.at[z, 1 - k], sib_r.at[NG + 4])
        for s in range(1, NZ):
            put(cgb.at[z], cgb.at[z], cs_.at[s], cr.at[z], zpeer[s - 1])

    lag_d = 2
    lag_e = 4

    def band_ring(hop):
        low, high = up(z, -hop, NZ), up(z, hop, NZ)
        if hop == 0:
            if mode[0] != "finish":
                for g in range(NG):
                    ours = band.at[g, z, k]
                    pltpu.make_async_copy(ours, ours, loc.at[5 + g]).wait()
                    got(band.at[g, z, 1 - k], sib_r.at[g])
        else:
            got(band.at[:, low], zr.at[low])
            if hop < NZ // 2:
                got(band.at[:, high], zr.at[high])
        if hop < NZ // 2:
            put(band.at[:, low], band.at[:, low], zs.at[0, hop], zr.at[low], zup)
        if hop < NZ // 2 - 1:
            put(band.at[:, high], band.at[:, high], zs.at[1, hop], zr.at[high], zdn)

    background = [(3, adjoint_rows), (13, l_rows)]
    background += [(5 + 3 * h, functools.partial(band_ring, h)) for h in range(NZ // 2 + 1)]

    def step(n):
        o = pick([st[1] + 4 for st in STEPS], n)
        return pick([st[0] for st in STEPS], n), o, lax.rem(y + o + NZ - 4, NZ)

    def stage_b(n):
        g, o, zz = step(n)
        slot, sem = rbuf.at[g, x, zz], rr.at[g, x, zz]
        got(slot, sem)

        put(slot, slot, ys.at[0, g, o], sem, yup, jnp.logical_and(o >= 1, o <= 4))
        put(slot, slot, ys.at[1, g, o], sem, ydn, jnp.logical_and(o >= 4, o <= 6))
        put(slot, slot, xsm.at[0, g, o], sem, xup)
        put(slot, slot, xsm.at[1, g, o], sem, xdn)

    def stage_d(n):
        g, o, zz = step(n)
        left, right = up(x, -1, NX), up(x, 1, NX)
        got(rbuf.at[g, left, zz], rr.at[g, left, zz])
        got(rbuf.at[g, right, zz], rr.at[g, right, zz])
        even = lax.rem(o, 2) == 0
        chunk = rbuf.at[g, left, zz]
        put(chunk, chunk, xsm.at[2, g, o], rr.at[g, left, zz], xup, even)
        chunk = rbuf.at[g, right, zz]
        put(chunk, chunk, xsm.at[2, g, o], rr.at[g, right, zz], xdn, jnp.logical_not(even))

    def stage_e(n):
        g, o, zz = step(n)
        far = up(x, 2, NX)
        got(rbuf.at[g, far, zz], rr.at[g, far, zz])

    def piece(g, xx):
        b = split(rbuf[g, xx].reshape(NZ * 2 * ROWS, W))
        psum[g] += mm_split((thi[xx], tlo[xx]), b).reshape(NZ, 2 * ROWS, W)

    def scatter(g):
        for s in range(1, NZ):
            to = up(z, s, NZ)
            put(psum.at[g, to], sbuf.at[g, z], ss.at[g, s], sr.at[g, z], zpeer[s - 1])
        if mode[0] != "finish":
            sbuf[g, z] = psum[g, z]

    def within(n, fn):
        @pl.when(jnp.logical_and(n >= 0, n < STEP_COUNT))
        def _():
            fn(n)

    def first_group(n):
        @pl.when(jnp.logical_and(n >= 0, n < NX))
        def _():
            piece(0, n)

        @pl.when(n == NX)
        def _():
            scatter(0)

    def split_t(h):
        for i in range(2):
            thi[2 * h + i], tlo[2 * h + i] = split(tbuf[h, :, 512 * i : 512 * i + 512])

    tcopy.wait()
    got(tbuf.at[1 - k], sib_r.at[NG])
    for h in range(2):
        split_t(h)
    psum[...] = jnp.zeros_like(psum)
    mode[0] = "loop"

    def body(i, carry):
        within(i, stage_b)
        within(i - lag_d, stage_d)
        within(i - lag_e, stage_e)
        for at, task in background:
            pl.when(i == at)(task)
        first_group(i - lag_e - LAST0 - 1)
        return carry

    lax.fori_loop(0, STEP_COUNT + 4, body, 0)
    mode[0] = "start"
    l_planes()
    for xx in range(NX):
        piece(1, xx)
    scatter(1)
    l_far()

    for q in range(3):
        ltr[q] = lloc[q].T
    for s in range(1, NZ):
        frm = up(z, s, NZ)
        got(cgb.at[frm], cr.at[frm])
    mine = pl.ds(pl.multiple_of(z * 64, 64), 64)

    def cross_half(lo):
        return jnp.concatenate([cgb[c // 2, c % 2, :, 0:64] for c in range(lo, lo + NZ)], 1)

    @pl.when(first)
    def _():
        corner = jnp.concatenate([cgb[c // 2, c % 2, :, 64:96] for c in range(2 * NZ)], 1)
        cross = split(cross_half(0))
        fold[0] = mm(ltr[0, mine, :], corner) + mm_split(split(ltr[2, mine, :]), cross)
        fold[1] = mm_split(split(ltr[1, mine, :]), cross)

    @pl.when(k == 1)
    def _():
        fold[0] = mm(ltr[1, mine, :], cross_half(NZ))

    fcopy.wait()
    got(fbuf.at[1 - k], sib_r.at[NG + 1])
    for g in range(NG):
        for s in range(1, NZ):
            frm = up(z, s, NZ)
            got(sbuf.at[g, frm], sr.at[g, frm])
        total = sbuf[g, 0]
        for s in range(1, NZ):
            total = total + sbuf[g, s]
        lanes = slice(g * W, g * W + W)
        xr[:, :, lanes] = fbuf[:, :, lanes] - 2.0 * total.reshape(2, ROWS, W)

    xall = xr[...].reshape(2 * ROWS, B)
    for s in range(NZ):
        xst[s] = xall[:, 64 * s : 64 * s + 64]
    for s in range(1, NZ):
        to = up(z, s, NZ)
        put(xst.at[to], xs.at[z], as_.at[s], ar.at[z], zpeer[s - 1])
    l_cores()
    put(xr.at[1 - k], xo.at[k], sib_s.at[NG + 2], sib_r.at[NG + 2], sib)
    xo[k] = xr[k]
    xs[z] = xst[z]
    for s in range(1, NZ):
        frm = up(z, s, NZ)
        got(xs.at[frm], ar.at[frm])
    put(xs, xs2, sib_s.at[NG + 3], sib_r.at[NG + 3], sib, k == 1)

    def gram(b, src):
        a = split(src[...].reshape(NZ * 64, 64).T)
        for g in range(NG):
            bb = split(band[g].reshape(NZ * 64, W))
            lanes = slice(g * W, g * W + W)
            gm[b, :, :, lanes] = (mm_split(a, bb) - fold[b, :, lanes]).reshape(NY, 8, W)

    def plane_reduce_start(b, cond):
        for s in range(1, NY):
            to = up(y, s, NY)
            put(gm.at[b, to], gy.at[b, y], gys.at[b, s], gyr.at[b, y], ypeer[s - 1], cond)

    gram(0, xs)
    plane_reduce_start(0, None)

    @pl.when(first)
    def _():
        got(xs2, sib_r.at[NG + 3])
        gram(1, xs2)

    plane_reduce_start(1, first)
    conds = (None, first)

    def when(cond, fn):
        if cond is None:
            fn()
        else:
            pl.when(cond)(fn)

    def y_sum(b):
        gy[b, y] = gm[b, y]
        for s in range(1, NY):
            frm = up(y, s, NY)
            got(gy.at[b, frm], gyr.at[b, frm])
        total = gy[b, 0]
        for s in range(1, NY):
            total = total + gy[b, s]
        sg[b] = total
        gx[b, x] = total

    def x_sum(b):
        for s in range(1, NX):
            frm = up(x, s, NX)
            got(gx.at[b, frm], gxr.at[b, frm])
        total = (gx[b, 0] + gx[b, 1]) + (gx[b, 2] + gx[b, 3])
        gz[b, 0, z, y] = total[:, 0:W2]
        gz[b, 1, z, y] = total[:, W2:B]

    def y_wait(b):
        for s in range(1, NY):
            frm = up(y, s, NY)
            got(gz.at[b, 0, z, frm], gar.at[b, frm])
        for s in range(1, NZ):
            frm = up(z, s, NZ)
            got(gz.at[b, 1, frm, y], gbr.at[b, frm])

    for b in range(2):
        when(conds[b], functools.partial(y_sum, b))
        for s in range(1, NX):
            put(sg.at[b], gx.at[b, x], gxs.at[b, s], gxr.at[b, x], xpeer[s - 1], conds[b])
    def factor(q):
        return jnp.concatenate([lbuf[p, :, :, 2 * q : 2 * q + 2].reshape(B, 128) for p in range(4)], 1)

    def tile(q):
        return lambda i, j: lbuf[j, 2 * i : 2 * i + 2, :, 2 * q : 2 * q + 2].reshape(128, 128)

    def second_inverse():
        got(lbuf.at[:, :, :, pl.ds(3 * (1 - k), 3)], sib_r.at[NG + 5])
        invert(tile(1), v2)

    def first_inverse():
        v2t[...] = v2[...].T
        invert(tile(0), v1)

    def coupling_factor():
        v1t[...] = v1[...].T
        mmat[...] = mm(factor(2), v1[...])

    def tall_rows():
        mt[...] = mmat[...].T
        got(xo.at[1 - k], sib_r.at[NG + 2])
        h2 = mm(xo[1], v2[...])
        rows_ref[:, B : 2 * B] = h2
        rows_ref[:, 0:B] = mm(xo[0], v1[...]) - mm(h2, mmat[...])

    between = {0: first_inverse, 2: coupling_factor, 4: tall_rows}

    for b in range(2):
        when(conds[b], functools.partial(x_sum, b))
        for s in range(1, NY):
            put(gz.at[b, 0, z, y], gz.at[b, 0, z, y], gas.at[b, s], gar.at[b, y], ypeer[s - 1], conds[b])
        for s in range(1, NZ):
            put(gz.at[b, 1, z, y], gz.at[b, 1, z, y], gbs.at[b, s], gbr.at[b, z], zpeer[s - 1], conds[b])
    second_inverse()
    for j in range(NZ):
        zz, yy = up(z, ORDER[j], NZ), up(y, ORDER[j], NY)
        hop = abs(ORDER[j])
        for b in range(2):
            chunk, other = gz.at[b, 0, zz], gz.at[b, 1, :, yy]
            if j == 0:
                when(conds[b], functools.partial(y_wait, b))
            else:
                when(conds[b], functools.partial(got, chunk, gzr.at[b, zz]))
                when(conds[b], functools.partial(got, other, gwr.at[b, yy]))
            if j == 0 or (ORDER[j] < 0 and hop < NZ // 2):
                put(chunk, chunk, gzs.at[0, b, hop], gzr.at[b, zz], zup, conds[b])
                put(other, other, gws.at[0, b, hop], gwr.at[b, yy], yup, conds[b])
            if j == 0 or (ORDER[j] > 0 and hop < NZ // 2 - 1):
                put(chunk, chunk, gzs.at[1, b, hop], gzr.at[b, zz], zdn, conds[b])
                put(other, other, gws.at[1, b, hop], gwr.at[b, yy], ydn, conds[b])
        if j in between:
            between[j]()

    def gram_total(b):
        return jnp.concatenate([gz[b, 0].reshape(B, W2), gz[b, 1].reshape(B, W2)], 1)

    r = lax.broadcasted_iota(jnp.int32, (B, B), 0)
    c = lax.broadcasted_iota(jnp.int32, (B, B), 1)
    own = pl.ds(pl.multiple_of(row * 16, 16), 16)

    def lowered(p):
        return jnp.where(r > c, p, jnp.where(r == c, 0.5 * p, 0.0))

    @pl.when(k == 1)
    def _():
        left = split(v2t[...])
        p2 = mm_split(left, split(gram_total(0)))
        q2 = lowered(mm(factor(1).T, jnp.where(r >= c, -p2, 0.0)))
        w1[...] = mm(q2 + q2.T, v2[...])
        sbm[...] = 0.5 * mm_split(left, split(w1[...]))

    put(sbm, sbm, sib_s.at[NG + 6], sib_r.at[NG + 6], sib, k == 1)

    @pl.when(first)
    def _():
        p1 = split(-mm(v2t[...], gram_total(1)))
        w1[...] = mm_split(p1, split(v1[...]))
        w2[...] = mm(v1t[...], gram_total(0)) + mm_split(split(mt[...]), p1)
        got(sbm, sib_r.at[NG + 6])
        coupling = w1[...] - 2.0 * mm(sbm[...], mmat[...])
        cpl[...] = coupling
        outp[0] = cpl[own, :]
        grad = jnp.where(r >= c, -w2[...] - mm(coupling.T, factor(2)), 0.0)
        q1 = lowered(mm(factor(0).T, grad))
        w1[...] = q1 + q1.T
        outp[1] = 0.5 * mm(mm(v1t[own, :], w1[...]), v1[...])

    put(outp, outp, sib_s.at[NG + 7], sib_r.at[NG + 7], sib, first)

    @pl.when(k == 1)
    def _():
        got(outp, sib_r.at[NG + 7])

    shift = lax.rem(B - col * 32, B)
    c_ref[...] = pltpu.roll(outp[0], shift, 1)[:, 0:32]
    b_ref[0] = pltpu.roll(outp[1], shift, 1)[:, 0:32]
    b_ref[1] = pltpu.roll(sbm[own, :], shift, 1)[:, 0:32]

    for c, cond in sends:
        if cond is None:
            c.wait_send()
        else:
            pl.when(cond)(c.wait_send)
    mode[0] = "finish"
    for _, task in background:
        task()
    scatter(0)

    def sent(n, carry):
        stage_b(n)
        stage_d(n)
        return carry

    lax.fori_loop(0, STEP_COUNT, sent, 0)


def panel_call(*args):
    dma = pltpu.SemaphoreType.DMA
    vm = pl.BlockSpec(memory_space=pltpu.VMEM)
    hbm = pl.BlockSpec(memory_space=pl.ANY)
    square = pltpu.VMEM((B, B), F32)
    return pl.pallas_call(
        panel_kernel,
        out_shape=(
            jax.ShapeDtypeStruct((ROWS, 2 * B), F32),
            jax.ShapeDtypeStruct((2, 16, 32), F32),
            jax.ShapeDtypeStruct((16, 32), F32),
        ),
        in_specs=[hbm] * 7,
        out_specs=(vm, vm, vm),
        scratch_shapes=[
            pltpu.VMEM((2, 512, 1024), F32),
            pltpu.VMEM((NX, 512, 512), BF16),
            pltpu.VMEM((NX, 512, 512), BF16),
            pltpu.VMEM((NG, NZ, 2, ROWS, W), F32),
            pltpu.VMEM((NG, NX, NZ, 2, ROWS, W), F32),
            pltpu.VMEM((NG, NZ, 2 * ROWS, W), F32),
            pltpu.VMEM((NG, NZ, 2 * ROWS, W), F32),
            pltpu.VMEM((2, ROWS, B), F32),
            pltpu.VMEM((2, ROWS, B), F32),
            pltpu.VMEM((2, ROWS, B), F32),
            pltpu.VMEM((NZ, 64, 64), F32),
            pltpu.VMEM((NZ, 64, 64), F32),
            pltpu.VMEM((NZ, 64, 64), F32),
            pltpu.VMEM((2, NY, 8, B), F32),
            pltpu.VMEM((2, NY, 8, B), F32),
            pltpu.VMEM((2, 8, B), F32),
            pltpu.VMEM((2, NX, 8, B), F32),
            pltpu.VMEM((2, 2, NZ, NY, 8, W2), F32),
            pltpu.VMEM((3, 16, B), F32),
            pltpu.VMEM((16, 64), F32),
            pltpu.VMEM((16, 32), F32),
            pltpu.VMEM((4, NY, NX, 6, 8, 128), F32),
            pltpu.VMEM((NZ, 2, 16, 128), F32),
            pltpu.VMEM((3, B, 16), F32),
            pltpu.VMEM((2, 64, B), F32),
        ]
        + [square] * 10
        + [
            pltpu.VMEM((2, 16, B), F32),
            dma((NG + 12,)), dma((NG + 8,)), dma((NG + 6,)),
            dma((2, NZ)), dma((NZ,)),
            dma((2, NG, NZ)), dma((3, NG, NZ)), dma((NG, NX, NZ)),
            dma((NG, NZ)), dma((NG, NZ)),
            dma((NZ,)), dma((NZ,)),
            dma((2, NY)), dma((2, NY)),
            dma((2, NX)), dma((2, NX)),
            dma((2, NY)), dma((2, NY)),
            dma((2, NZ)), dma((2, NZ)),
            dma((2, 2, NZ // 2)), dma((2, NZ)),
            dma((2, 2, NY // 2)), dma((2, NY)),
            dma((NY,)), dma((NY,)),
            dma((2,)), dma((2,)), dma((2,)), dma((2,)),
            dma((NZ,)), dma((NZ,)),
        ],
        compiler_params=pltpu.CompilerParams(
            collective_id=0, has_side_effects=True, vmem_limit_bytes=60 * 1024 * 1024
        ),
        name="panel_adjoint",
    )(*args)


def invert(lower, out_ref):
    n = 128
    r = lax.broadcasted_iota(jnp.int32, (n, n), 0)
    c = lax.broadcasted_iota(jnp.int32, (n, n), 1)
    blocks = [lower(q, q) for q in range(4)]
    inv = []
    for a in blocks:
        diag = jnp.sum(jnp.where(r == c, a, 0.0), axis=1, keepdims=True)
        inv.append(jnp.where(r == c, 1.0 / diag, 0.0))
    for lb in range(7):
        mask = ((r >> (lb + 1)) == (c >> (lb + 1))) & ((r >> lb) > (c >> lb))
        for q in range(4):
            cut = jnp.where(mask, blocks[q], 0.0)
            yy = split(inv[q])
            inv[q] = inv[q] - mm_split(yy, split(mm_split(split(cut), yy)))
    zero = jnp.zeros((n, n), F32)
    wide = []
    for h in range(2):
        a, b = inv[2 * h], inv[2 * h + 1]
        low = -mm(b, mm(lower(2 * h + 1, 2 * h), a))
        wide.append(jnp.concatenate([jnp.concatenate([a, zero], 1), jnp.concatenate([low, b], 1)], 0))
    corner = jnp.concatenate(
        [jnp.concatenate([lower(2, 0), lower(2, 1)], 1), jnp.concatenate([lower(3, 0), lower(3, 1)], 1)], 0
    )
    low = -mm(wide[1], mm(corner, wide[0]))
    out_ref[0:256, 0:256] = wide[0]
    out_ref[0:256, 256:512] = jnp.zeros((256, 256), F32)
    out_ref[256:512, 0:256] = low
    out_ref[256:512, 256:512] = wide[1]


def per_device(*args):
    return panel_call(*args)


def solution(mesh):
    return jax.shard_map(
        per_device,
        mesh=mesh,
        in_specs=(
            P("row", "col"),
            P(("row", "col"), None),
            P(("row", "col"), None),
            P(None, "row", None),
            P("row", None),
            P("row", "col"),
            P("row", "col"),
        ),
        out_specs=(P(("row", "col"), None), P(None, "row", "col"), P("row", "col")),
        check_vma=False,
    )
```

```python
import functools

import jax
import jax.numpy as jnp
from jax import lax
from jax.experimental import pallas as pl
from jax.experimental.pallas import tpu as pltpu
from jax.sharding import PartitionSpec as P

MESH = pl.DeviceIdType.MESH
F32 = jnp.float32
BF16 = jnp.bfloat16
NX, NY, NZ = 4, 8, 8
NG = 2
B = 512
W = B // NG
W2 = B // 2
ROWS = 32
ORDER = (0, -1, 1, -2, 2, -3, 3, -4)
STEPS = [(g, o) for g in range(NG) for o in ORDER]
STEP_COUNT = len(STEPS)
LAST0 = NZ - 1


def pick(values, n):
    words = [sum(v << (4 * i) for i, v in enumerate(values[h : h + 8])) for h in (0, 8)]
    return (jnp.where(n < 8, words[0], words[1]) >> (4 * lax.rem(n, 8))) & 7


def split(a):
    hi = a.astype(BF16)
    return hi, (a - hi.astype(F32)).astype(BF16)


def dot(a, b):
    return jnp.dot(a, b, preferred_element_type=F32)


def mm_split(a, b):
    return dot(a[0], b[0]) + (dot(a[0], b[1]) + dot(a[1], b[0]))


def mm(a, b):
    return mm_split(split(a), split(b))


def panel_kernel(
    t_ref, r_ref, f_ref, diag_ref, cross_ref, cg_ref, co_ref,
    rows_ref, b_ref, c_ref,
    tbuf, thi, tlo, band, rbuf, psum, sbuf, fbuf, xr, xo, xst, xs, xs2, gm, gy, sg, gx, gz,
    lloc, cgl, col_, lbuf, cgb, ltr, fold, v1, v2, v1t, v2t, mmat, mt, w1, w2, sbm, cpl, outp,
    sib_s, sib_r, loc, zs, zr, ys, xsm, rr, ss, sr, as_, ar, gys, gyr, gxs, gxr, gas, gar, gbs, gbr, gzs, gzr,
    gws, gwr, lys, lyr, lzs, lzr, lfs, lfr, cs_, cr,
):
    local = [
        pltpu.make_async_copy(diag_ref, lloc.at[pl.ds(0, 2)], loc.at[1]),
        pltpu.make_async_copy(cross_ref, lloc.at[2], loc.at[2]),
        pltpu.make_async_copy(cg_ref, cgl, loc.at[3]),
        pltpu.make_async_copy(co_ref, col_, loc.at[4]),
    ]
    for c in local:
        c.start()
    row = lax.axis_index("row")
    col = lax.axis_index("col")
    y, x = row // NX, lax.rem(row, NX)
    z, k = col // 2, lax.rem(col, 2)

    def dev(px, py, pz, pk):
        return {"row": py * NX + px, "col": pz * 2 + pk}

    def up(v, s, n):
        return lax.rem(v + (s + n), n)

    sib = dev(x, y, z, 1 - k)
    zpeer = [dev(x, y, up(z, s, NZ), k) for s in range(1, NZ)]
    ypeer = [dev(x, up(y, s, NY), z, k) for s in range(1, NY)]
    xpeer = [dev(up(x, s, NX), y, z, k) for s in range(1, NX)]
    zup, zdn = zpeer[0], zpeer[-1]
    yup, ydn = ypeer[0], ypeer[-1]
    xup, xdn = xpeer[0], xpeer[-1]
    d = up(y - z, NY, NY)

    barrier = pltpu.get_barrier_semaphore()
    partners = [sib, zup, zdn, yup, ydn] + xpeer
    for p in partners:
        pl.semaphore_signal(barrier, inc=1, device_id=p, device_id_type=MESH)

    swap = [dev(x, z, y, k), dev(x, z, y, 1 - k)]

    @pl.when(d != 0)
    def _():
        for p in swap:
            pl.semaphore_signal(barrier, inc=1, device_id=p, device_id_type=MESH)

    pl.semaphore_wait(barrier, len(partners) + jnp.where(d == 0, 0, 2))

    sends = []
    mode = ["start"]

    def put(src, dst, ssem, rsem, target, cond=None):
        c = pltpu.make_async_remote_copy(
            src_ref=src, dst_ref=dst, send_sem=ssem, recv_sem=rsem, device_id=target, device_id_type=MESH
        )
        act = c.wait_send if mode[0] == "finish" else c.start
        if cond is None:
            act()
        else:
            pl.when(cond)(act)
        if mode[0] == "start":
            sends.append((c, cond))

    def got(ref, sem):
        if mode[0] != "finish":
            pltpu.make_async_remote_copy(
                src_ref=ref, dst_ref=ref, send_sem=sem, recv_sem=sem, device_id=sib, device_id_type=MESH
            ).wait_recv()

    first = k == 0
    rcopies = []
    for g in range(NG):
        ours = r_ref.at[:, pl.ds(pl.multiple_of(k * B + g * W, 128), W)]
        theirs = r_ref.at[:, pl.ds(pl.multiple_of((1 - k) * B + g * W, 128), W)]
        slot, sem = rbuf.at[g, x, z, k], rr.at[g, x, z]
        put(ours, slot, sib_s.at[NG + 8 + g], sem, swap[0], d != 0)
        put(theirs, slot, sib_s.at[NG + 10 + g], sem, swap[1])
        rcopies.append((pltpu.make_async_copy(ours, slot, sem), d == 0))
        pl.when(d == 0)(rcopies[-1][0].start)
    for g in range(NG):
        ours = r_ref.at[:, pl.ds(pl.multiple_of(k * B + g * W, 128), W)]
        theirs = r_ref.at[:, pl.ds(pl.multiple_of((1 - k) * B + g * W, 128), W)]
        put(theirs, band.at[g, z, k], sib_s.at[g], sib_r.at[g], sib)
        pltpu.make_async_copy(ours, band.at[g, z, k], loc.at[5 + g]).start()
    put(t_ref, tbuf.at[k], sib_s.at[NG], sib_r.at[NG], sib)
    tcopy = pltpu.make_async_copy(t_ref, tbuf.at[k], loc.at[0])
    tcopy.start()
    put(f_ref.at[:, pl.ds(pl.multiple_of((1 - k) * B, 128), B)], fbuf.at[k], sib_s.at[NG + 1], sib_r.at[NG + 1], sib)
    fcopy = pltpu.make_async_copy(f_ref.at[:, pl.ds(pl.multiple_of(k * B, 128), B)], fbuf.at[k], loc.at[5 + NG])
    fcopy.start()
    for c in local:
        c.wait()
    half = pl.ds(3 * k, 3)
    for q in range(3):
        for p in range(4):
            lbuf[p, y, x, 2 * q : 2 * q + 2] = lloc[q, :, 128 * p : 128 * p + 128].reshape(2, 8, 128)
    cgb[z, k] = jnp.zeros((16, 128), F32)
    cgb[z, k, :, 0:64] = cgl[...]
    cgb[z, k, :, 64:96] = col_[...]
    put(cgb.at[z, k], cgb.at[z, k], sib_s.at[NG + 4], sib_r.at[NG + 4], sib)

    def l_rows():
        part = lbuf.at[:, y, x, half]
        for s in range(1, NY):
            put(part, part, lys.at[s], lyr.at[y], ypeer[s - 1])

    def l_planes():
        for s in range(1, NY):
            frm = up(y, s, NY)
            got(lbuf.at[:, frm, x, half], lyr.at[frm])
        part = lbuf.at[:, :, x, half]
        for i, to in enumerate((xup, xdn)):
            put(part, part, lzs.at[i], lzr.at[i], to)

    def l_far():
        for i, (to, frm) in enumerate(((xup, up(x, -1, NX)), (xdn, up(x, 1, NX)))):
            got(lbuf.at[:, :, frm, half], lzr.at[i])
            part = lbuf.at[pl.ds(2 * i, 2), :, frm, half]
            put(part, part, lfs.at[i], lfr.at[i], to)

    def l_cores():
        far = up(x, 2, NX)
        for i in range(2):
            got(lbuf.at[pl.ds(2 * i, 2), :, far, half], lfr.at[i])
        put(lbuf.at[:, :, :, half], lbuf.at[:, :, :, half], sib_s.at[NG + 5], sib_r.at[NG + 5], sib)

    def adjoint_rows():
        got(cgb.at[z, 1 - k], sib_r.at[NG + 4])
        for s in range(1, NZ):
            put(cgb.at[z], cgb.at[z], cs_.at[s], cr.at[z], zpeer[s - 1])

    lag_d = 2
    lag_e = 4

    def band_ring(hop):
        low, high = up(z, -hop, NZ), up(z, hop, NZ)
        if hop == 0:
            if mode[0] != "finish":
                for g in range(NG):
                    ours = band.at[g, z, k]
                    pltpu.make_async_copy(ours, ours, loc.at[5 + g]).wait()
                    got(band.at[g, z, 1 - k], sib_r.at[g])
        else:
            got(band.at[:, low], zr.at[low])
            if hop < NZ // 2:
                got(band.at[:, high], zr.at[high])
        if hop < NZ // 2:
            put(band.at[:, low], band.at[:, low], zs.at[0, hop], zr.at[low], zup)
        if hop < NZ // 2 - 1:
            put(band.at[:, high], band.at[:, high], zs.at[1, hop], zr.at[high], zdn)

    background = [(17, adjoint_rows), (13, l_rows)]
    background += [(at, functools.partial(band_ring, h)) for h, at in enumerate((4, 7, 10, 13, 15))]

    def step(n):
        o = pick([st[1] + 4 for st in STEPS], n)
        return pick([st[0] for st in STEPS], n), o, lax.rem(y + o + NZ - 4, NZ)

    def stage_b(n):
        g, o, zz = step(n)
        slot, sem = rbuf.at[g, x, zz], rr.at[g, x, zz]
        got(slot, sem)

        put(slot, slot, ys.at[0, g, o], sem, yup, jnp.logical_and(o >= 1, o <= 4))
        put(slot, slot, ys.at[1, g, o], sem, ydn, jnp.logical_and(o >= 4, o <= 6))
        put(slot, slot, xsm.at[0, g, o], sem, xup)
        put(slot, slot, xsm.at[1, g, o], sem, xdn)

    def stage_d(n):
        g, o, zz = step(n)
        left, right = up(x, -1, NX), up(x, 1, NX)
        got(rbuf.at[g, left, zz], rr.at[g, left, zz])
        got(rbuf.at[g, right, zz], rr.at[g, right, zz])
        even = lax.rem(o, 2) == 0
        chunk = rbuf.at[g, left, zz]
        put(chunk, chunk, xsm.at[2, g, o], rr.at[g, left, zz], xup, even)
        chunk = rbuf.at[g, right, zz]
        put(chunk, chunk, xsm.at[2, g, o], rr.at[g, right, zz], xdn, jnp.logical_not(even))

    def stage_e(n):
        g, o, zz = step(n)
        far = up(x, 2, NX)
        got(rbuf.at[g, far, zz], rr.at[g, far, zz])

    def piece(g, xx):
        b = split(rbuf[g, xx].reshape(NZ * 2 * ROWS, W))
        psum[g] += mm_split((thi[xx], tlo[xx]), b).reshape(NZ, 2 * ROWS, W)

    def scatter(g):
        for s in range(1, NZ):
            to = up(z, s, NZ)
            put(psum.at[g, to], sbuf.at[g, z], ss.at[g, s], sr.at[g, z], zpeer[s - 1])
        if mode[0] != "finish":
            sbuf[g, z] = psum[g, z]

    def within(n, fn):
        @pl.when(jnp.logical_and(n >= 0, n < STEP_COUNT))
        def _():
            fn(n)

    def first_group(n):
        @pl.when(jnp.logical_and(n >= 0, n < NX))
        def _():
            piece(0, n)

        @pl.when(n == NX)
        def _():
            scatter(0)

    def split_t(h):
        for i in range(2):
            thi[2 * h + i], tlo[2 * h + i] = split(tbuf[h, :, 512 * i : 512 * i + 512])

    tcopy.wait()
    got(tbuf.at[1 - k], sib_r.at[NG])
    for h in range(2):
        split_t(h)
    psum[...] = jnp.zeros_like(psum)
    mode[0] = "loop"

    def body(i, carry):
        within(i, stage_b)
        within(i - lag_d, stage_d)
        within(i - lag_e, stage_e)
        for at, task in background:
            pl.when(i == at)(task)
        first_group(i - lag_e - LAST0 - 1)
        return carry

    lax.fori_loop(0, STEP_COUNT + 4, body, 0)
    mode[0] = "start"
    l_planes()
    for xx in range(NX):
        piece(1, xx)
    scatter(1)
    l_far()

    for q in range(3):
        ltr[q] = lloc[q].T
    for s in range(1, NZ):
        frm = up(z, s, NZ)
        got(cgb.at[frm], cr.at[frm])
    mine = pl.ds(pl.multiple_of(z * 64, 64), 64)

    def cross_half(lo):
        return jnp.concatenate([cgb[c // 2, c % 2, :, 0:64] for c in range(lo, lo + NZ)], 1)

    @pl.when(first)
    def _():
        corner = jnp.concatenate([cgb[c // 2, c % 2, :, 64:96] for c in range(2 * NZ)], 1)
        cross = split(cross_half(0))
        fold[0] = mm(ltr[0, mine, :], corner) + mm_split(split(ltr[2, mine, :]), cross)
        fold[1] = mm_split(split(ltr[1, mine, :]), cross)

    @pl.when(k == 1)
    def _():
        fold[0] = mm(ltr[1, mine, :], cross_half(NZ))

    fcopy.wait()
    got(fbuf.at[1 - k], sib_r.at[NG + 1])
    for g in range(NG):
        for s in range(1, NZ):
            frm = up(z, s, NZ)
            got(sbuf.at[g, frm], sr.at[g, frm])
        total = sbuf[g, 0]
        for s in range(1, NZ):
            total = total + sbuf[g, s]
        lanes = slice(g * W, g * W + W)
        xr[:, :, lanes] = fbuf[:, :, lanes] - 2.0 * total.reshape(2, ROWS, W)

    xall = xr[...].reshape(2 * ROWS, B)
    for s in range(NZ):
        xst[s] = xall[:, 64 * s : 64 * s + 64]
    for s in range(1, NZ):
        to = up(z, s, NZ)
        put(xst.at[to], xs.at[z], as_.at[s], ar.at[z], zpeer[s - 1])
    l_cores()
    put(xr.at[1 - k], xo.at[k], sib_s.at[NG + 2], sib_r.at[NG + 2], sib)
    xo[k] = xr[k]
    xs[z] = xst[z]
    for s in range(1, NZ):
        frm = up(z, s, NZ)
        got(xs.at[frm], ar.at[frm])
    put(xs, xs2, sib_s.at[NG + 3], sib_r.at[NG + 3], sib, k == 1)

    def gram(b, src):
        a = split(src[...].reshape(NZ * 64, 64).T)
        for g in range(NG):
            bb = split(band[g].reshape(NZ * 64, W))
            lanes = slice(g * W, g * W + W)
            gm[b, :, :, lanes] = (mm_split(a, bb) - fold[b, :, lanes]).reshape(NY, 8, W)

    gram(0, xs)

    @pl.when(first)
    def _():
        got(xs2, sib_r.at[NG + 3])
        gram(1, xs2)

    sides = ((2, first), (1, k == 1))

    def each(fn):
        for nb, cond in sides:
            pl.when(cond)(functools.partial(fn, nb, pl.ds(0, nb)))

    for nb, cond in sides:
        for s in range(1, NY):
            to = up(y, s, NY)
            put(gm.at[pl.ds(0, nb), to], gy.at[pl.ds(0, nb), y], gys.at[s], gyr.at[y], ypeer[s - 1], cond)

    def y_sum(nb, bs):
        gy[0:nb, y] = gm[0:nb, y]
        for s in range(1, NY):
            frm = up(y, s, NY)
            got(gy.at[bs, frm], gyr.at[frm])
        total = gy[0:nb, 0]
        for s in range(1, NY):
            total = total + gy[0:nb, s]
        sg[0:nb] = total
        gx[0:nb, x] = total

    def x_sum(nb, bs):
        for s in range(1, NX):
            frm = up(x, s, NX)
            got(gx.at[bs, frm], gxr.at[frm])
        total = (gx[0:nb, 0] + gx[0:nb, 1]) + (gx[0:nb, 2] + gx[0:nb, 3])
        gz[0:nb, 0, z, y] = total[:, :, 0:W2]
        gz[0:nb, 1, z, y] = total[:, :, W2:B]

    def y_wait(nb, bs):
        for s in range(1, NY):
            frm = up(y, s, NY)
            got(gz.at[bs, 0, z, frm], gar.at[frm])
        for s in range(1, NZ):
            frm = up(z, s, NZ)
            got(gz.at[bs, 1, frm, y], gbr.at[frm])

    each(y_sum)
    for nb, cond in sides:
        for s in range(1, NX):
            put(sg.at[pl.ds(0, nb)], gx.at[pl.ds(0, nb), x], gxs.at[s], gxr.at[x], xpeer[s - 1], cond)

    def factor(q):
        return jnp.concatenate([lbuf[p, :, :, 2 * q : 2 * q + 2].reshape(B, 128) for p in range(4)], 1)

    def tile(q):
        return lambda i, j: lbuf[j, 2 * i : 2 * i + 2, :, 2 * q : 2 * q + 2].reshape(128, 128)

    def second_inverse():
        got(lbuf.at[:, :, :, pl.ds(3 * (1 - k), 3)], sib_r.at[NG + 5])
        invert(tile(1), v2)

    def first_inverse():
        v2t[...] = v2[...].T
        invert(tile(0), v1)

    def coupling_factor():
        v1t[...] = v1[...].T
        mmat[...] = mm(factor(2), v1[...])

    def tall_rows():
        mt[...] = mmat[...].T
        got(xo.at[1 - k], sib_r.at[NG + 2])
        h2 = mm(xo[1], v2[...])
        rows_ref[:, B : 2 * B] = h2
        rows_ref[:, 0:B] = mm(xo[0], v1[...]) - mm(h2, mmat[...])

    between = {0: first_inverse, 2: coupling_factor, 4: tall_rows}

    each(x_sum)
    for nb, cond in sides:
        bs = pl.ds(0, nb)
        for s in range(1, NY):
            put(gz.at[bs, 0, z, y], gz.at[bs, 0, z, y], gas.at[s], gar.at[y], ypeer[s - 1], cond)
            put(gz.at[bs, 1, z, y], gz.at[bs, 1, z, y], gbs.at[s], gbr.at[z], zpeer[s - 1], cond)
    second_inverse()
    each(y_wait)
    for j in range(NZ):
        zz, yy = up(z, ORDER[j], NZ), up(y, ORDER[j], NY)
        hop = abs(ORDER[j])
        for nb, cond in sides:
            bs = pl.ds(0, nb)
            chunk, other = gz.at[bs, 0, zz], gz.at[bs, 1, :, yy]
            if j > 0:
                pl.when(cond)(functools.partial(got, chunk, gzr.at[zz]))
                pl.when(cond)(functools.partial(got, other, gwr.at[yy]))
            if j == 0 or (ORDER[j] < 0 and hop < NZ // 2):
                put(chunk, chunk, gzs.at[0, hop], gzr.at[zz], zup, cond)
                put(other, other, gws.at[0, hop], gwr.at[yy], yup, cond)
            if j == 0 or (ORDER[j] > 0 and hop < NZ // 2 - 1):
                put(chunk, chunk, gzs.at[1, hop], gzr.at[zz], zdn, cond)
                put(other, other, gws.at[1, hop], gwr.at[yy], ydn, cond)
        if j in between:
            between[j]()

    def gram_total(b):
        return jnp.concatenate([gz[b, 0].reshape(B, W2), gz[b, 1].reshape(B, W2)], 1)

    r = lax.broadcasted_iota(jnp.int32, (B, B), 0)
    c = lax.broadcasted_iota(jnp.int32, (B, B), 1)
    own = pl.ds(pl.multiple_of(row * 16, 16), 16)

    def lowered(p):
        return jnp.where(r > c, p, jnp.where(r == c, 0.5 * p, 0.0))

    @pl.when(k == 1)
    def _():
        left = split(v2t[...])
        p2 = mm_split(left, split(gram_total(0)))
        q2 = lowered(mm(factor(1).T, jnp.where(r >= c, -p2, 0.0)))
        w1[...] = mm(q2 + q2.T, v2[...])
        sbm[...] = 0.5 * mm_split(left, split(w1[...]))

    put(sbm, sbm, sib_s.at[NG + 6], sib_r.at[NG + 6], sib, k == 1)

    @pl.when(first)
    def _():
        p1 = split(-mm(v2t[...], gram_total(1)))
        w1[...] = mm_split(p1, split(v1[...]))
        w2[...] = mm(v1t[...], gram_total(0)) + mm_split(split(mt[...]), p1)
        got(sbm, sib_r.at[NG + 6])
        coupling = w1[...] - 2.0 * mm(sbm[...], mmat[...])
        cpl[...] = coupling
        outp[0] = cpl[own, :]
        grad = jnp.where(r >= c, -w2[...] - mm(coupling.T, factor(2)), 0.0)
        q1 = lowered(mm(factor(0).T, grad))
        w1[...] = q1 + q1.T
        outp[1] = 0.5 * mm(mm(v1t[own, :], w1[...]), v1[...])

    put(outp, outp, sib_s.at[NG + 7], sib_r.at[NG + 7], sib, first)

    @pl.when(k == 1)
    def _():
        got(outp, sib_r.at[NG + 7])

    shift = lax.rem(B - col * 32, B)
    c_ref[...] = pltpu.roll(outp[0], shift, 1)[:, 0:32]
    b_ref[0] = pltpu.roll(outp[1], shift, 1)[:, 0:32]
    b_ref[1] = pltpu.roll(sbm[own, :], shift, 1)[:, 0:32]

    for c, cond in sends:
        if cond is None:
            c.wait_send()
        else:
            pl.when(cond)(c.wait_send)
    mode[0] = "finish"
    for _, task in background:
        task()
    scatter(0)

    def sent(n, carry):
        stage_b(n)
        stage_d(n)
        return carry

    lax.fori_loop(0, STEP_COUNT, sent, 0)


def panel_call(*args):
    dma = pltpu.SemaphoreType.DMA
    vm = pl.BlockSpec(memory_space=pltpu.VMEM)
    hbm = pl.BlockSpec(memory_space=pl.ANY)
    square = pltpu.VMEM((B, B), F32)
    return pl.pallas_call(
        panel_kernel,
        out_shape=(
            jax.ShapeDtypeStruct((ROWS, 2 * B), F32),
            jax.ShapeDtypeStruct((2, 16, 32), F32),
            jax.ShapeDtypeStruct((16, 32), F32),
        ),
        in_specs=[hbm] * 7,
        out_specs=(vm, vm, vm),
        scratch_shapes=[
            pltpu.VMEM((2, 512, 1024), F32),
            pltpu.VMEM((NX, 512, 512), BF16),
            pltpu.VMEM((NX, 512, 512), BF16),
            pltpu.VMEM((NG, NZ, 2, ROWS, W), F32),
            pltpu.VMEM((NG, NX, NZ, 2, ROWS, W), F32),
            pltpu.VMEM((NG, NZ, 2 * ROWS, W), F32),
            pltpu.VMEM((NG, NZ, 2 * ROWS, W), F32),
            pltpu.VMEM((2, ROWS, B), F32),
            pltpu.VMEM((2, ROWS, B), F32),
            pltpu.VMEM((2, ROWS, B), F32),
            pltpu.VMEM((NZ, 64, 64), F32),
            pltpu.VMEM((NZ, 64, 64), F32),
            pltpu.VMEM((NZ, 64, 64), F32),
            pltpu.VMEM((2, NY, 8, B), F32),
            pltpu.VMEM((2, NY, 8, B), F32),
            pltpu.VMEM((2, 8, B), F32),
            pltpu.VMEM((2, NX, 8, B), F32),
            pltpu.VMEM((2, 2, NZ, NY, 8, W2), F32),
            pltpu.VMEM((3, 16, B), F32),
            pltpu.VMEM((16, 64), F32),
            pltpu.VMEM((16, 32), F32),
            pltpu.VMEM((4, NY, NX, 6, 8, 128), F32),
            pltpu.VMEM((NZ, 2, 16, 128), F32),
            pltpu.VMEM((3, B, 16), F32),
            pltpu.VMEM((2, 64, B), F32),
        ]
        + [square] * 10
        + [
            pltpu.VMEM((2, 16, B), F32),
            dma((NG + 12,)), dma((NG + 8,)), dma((NG + 6,)),
            dma((2, NZ)), dma((NZ,)),
            dma((2, NG, NZ)), dma((3, NG, NZ)), dma((NG, NX, NZ)),
            dma((NG, NZ)), dma((NG, NZ)),
            dma((NZ,)), dma((NZ,)),
            dma((NY,)), dma((NY,)),
            dma((NX,)), dma((NX,)),
            dma((NY,)), dma((NY,)),
            dma((NZ,)), dma((NZ,)),
            dma((2, NZ // 2)), dma((NZ,)),
            dma((2, NY // 2)), dma((NY,)),
            dma((NY,)), dma((NY,)),
            dma((2,)), dma((2,)), dma((2,)), dma((2,)),
            dma((NZ,)), dma((NZ,)),
        ],
        compiler_params=pltpu.CompilerParams(
            collective_id=0, has_side_effects=True, vmem_limit_bytes=60 * 1024 * 1024
        ),
        name="panel_adjoint",
    )(*args)


def invert(lower, out_ref):
    n = 128
    r = lax.broadcasted_iota(jnp.int32, (n, n), 0)
    c = lax.broadcasted_iota(jnp.int32, (n, n), 1)
    blocks = [lower(q, q) for q in range(4)]
    inv = []
    for a in blocks:
        diag = jnp.sum(jnp.where(r == c, a, 0.0), axis=1, keepdims=True)
        inv.append(jnp.where(r == c, 1.0 / diag, 0.0))
    for lb in range(7):
        mask = ((r >> (lb + 1)) == (c >> (lb + 1))) & ((r >> lb) > (c >> lb))
        for q in range(4):
            cut = jnp.where(mask, blocks[q], 0.0)
            yy = split(inv[q])
            inv[q] = inv[q] - mm_split(yy, split(mm_split(split(cut), yy)))
    zero = jnp.zeros((n, n), F32)
    wide = []
    for h in range(2):
        a, b = inv[2 * h], inv[2 * h + 1]
        low = -mm(b, mm(lower(2 * h + 1, 2 * h), a))
        wide.append(jnp.concatenate([jnp.concatenate([a, zero], 1), jnp.concatenate([low, b], 1)], 0))
    corner = jnp.concatenate(
        [jnp.concatenate([lower(2, 0), lower(2, 1)], 1), jnp.concatenate([lower(3, 0), lower(3, 1)], 1)], 0
    )
    low = -mm(wide[1], mm(corner, wide[0]))
    out_ref[0:256, 0:256] = wide[0]
    out_ref[0:256, 256:512] = jnp.zeros((256, 256), F32)
    out_ref[256:512, 0:256] = low
    out_ref[256:512, 256:512] = wide[1]


def store_kernel(*refs):
    for src, dst in zip(refs[:3], refs[3:]):
        dst[...] = src[...]


def per_device(*args):
    found = panel_call(*args)
    vm = pl.BlockSpec(memory_space=pltpu.VMEM)
    return pl.pallas_call(
        store_kernel,
        out_shape=tuple(jax.ShapeDtypeStruct(f.shape, F32) for f in found),
        in_specs=[vm] * 3,
        out_specs=(vm,) * 3,
        name="store",
    )(*found)


def solution(mesh):
    return jax.shard_map(
        per_device,
        mesh=mesh,
        in_specs=(
            P("row", "col"),
            P(("row", "col"), None),
            P(("row", "col"), None),
            P(None, "row", None),
            P("row", None),
            P("row", "col"),
            P("row", "col"),
        ),
        out_specs=(P(("row", "col"), None), P(None, "row", "col"), P("row", "col")),
        check_vma=False,
    )
```

```python
import functools

import jax
import jax.numpy as jnp
from jax import lax
from jax.experimental import pallas as pl
from jax.experimental.pallas import tpu as pltpu
from jax.sharding import PartitionSpec as P

MESH = pl.DeviceIdType.MESH
F32 = jnp.float32
BF16 = jnp.bfloat16
NX, NY, NZ = 4, 8, 8
B = 512
WIDTHS = (384, 128)
STARTS = (0, 384)
NG = 2
W2 = B // 2
ROWS = 32
ORDER = (0, -1, 1, -2, 2, -3, 3, -4)
STEPS = [(g, o) for g in range(NG) for o in ORDER]
STEP_COUNT = len(STEPS)
LAST0 = NZ - 1


def split(a):
    hi = a.astype(BF16)
    return hi, (a - hi.astype(F32)).astype(BF16)


def dot(a, b):
    return jnp.dot(a, b, preferred_element_type=F32)


def mm_split(a, b):
    return dot(a[0], b[0]) + (dot(a[0], b[1]) + dot(a[1], b[0]))


def mm(a, b):
    return mm_split(split(a), split(b))


def panel_kernel(
    t_ref, r_ref, f_ref, diag_ref, cross_ref, cg_ref, co_ref,
    rows_ref, b_ref, c_ref,
    tbuf, thi, tlo, band, rb0, rb1, ps0, ps1, sb0, sb1, fbuf, xr, xo, xst, xs, xs2, gm, gy, sg, gx, gz,
    lloc, cgl, col_, lbuf, cgb, ltr, fold, v1, v2, v1t, v2t, mmat, mt, w1, w2, sbm, outp,
    l1t, l2t, l21, v1s, v2s, v2ts, ms,
    sib_s, sib_r, loc, zs, zr, ys, xsm, rr, ss, sr, as_, ar, gys, gyr, gxs, gxr, gas, gar, gbs, gbr, gzs, gzr,
    gws, gwr, lys, lyr, lzs, lzr, lfs, lfr, cs_, cr,
):
    local = [
        pltpu.make_async_copy(diag_ref, lloc.at[pl.ds(0, 2)], loc.at[1]),
        pltpu.make_async_copy(cross_ref, lloc.at[2], loc.at[2]),
        pltpu.make_async_copy(cg_ref, cgl, loc.at[3]),
        pltpu.make_async_copy(co_ref, col_, loc.at[4]),
    ]
    for c in local:
        c.start()
    rbuf, psum, sbuf = (rb0, rb1), (ps0, ps1), (sb0, sb1)
    row = lax.axis_index("row")
    col = lax.axis_index("col")
    y, x = row // NX, lax.rem(row, NX)
    z, k = col // 2, lax.rem(col, 2)

    def dev(px, py, pz, pk):
        return {"row": py * NX + px, "col": pz * 2 + pk}

    def up(v, s, n):
        return lax.rem(v + (s + n), n)

    sib = dev(x, y, z, 1 - k)
    zpeer = [dev(x, y, up(z, s, NZ), k) for s in range(1, NZ)]
    ypeer = [dev(x, up(y, s, NY), z, k) for s in range(1, NY)]
    xpeer = [dev(up(x, s, NX), y, z, k) for s in range(1, NX)]
    zup, zdn = zpeer[0], zpeer[-1]
    yup, ydn = ypeer[0], ypeer[-1]
    xup, xdn = xpeer[0], xpeer[-1]
    d = up(y - z, NY, NY)

    barrier = pltpu.get_barrier_semaphore()
    partners = [sib, zup, zdn, yup, ydn] + xpeer
    for p in partners:
        pl.semaphore_signal(barrier, inc=1, device_id=p, device_id_type=MESH)

    swap = [dev(x, z, y, k), dev(x, z, y, 1 - k)]

    @pl.when(d != 0)
    def _():
        for p in swap:
            pl.semaphore_signal(barrier, inc=1, device_id=p, device_id_type=MESH)

    pl.semaphore_wait(barrier, len(partners) + jnp.where(d == 0, 0, 2))

    sends = []

    def put(src, dst, ssem, rsem, target, cond=None):
        c = pltpu.make_async_remote_copy(
            src_ref=src, dst_ref=dst, send_sem=ssem, recv_sem=rsem, device_id=target, device_id_type=MESH
        )
        if cond is None:
            c.start()
        else:
            pl.when(cond)(c.start)
        sends.append((c, cond))

    def got(ref, sem):
        pltpu.make_async_remote_copy(
            src_ref=ref, dst_ref=ref, send_sem=sem, recv_sem=sem, device_id=sib, device_id_type=MESH
        ).wait_recv()

    first = k == 0
    def rows_of(core, g):
        return r_ref.at[:, pl.ds(pl.multiple_of(core * B + STARTS[g], 128), WIDTHS[g])]

    for g in range(NG):
        slot, sem = rbuf[g].at[x, z, k], rr.at[g, x, z]
        put(rows_of(k, g), slot, sib_s.at[NG + 8 + g], sem, swap[0], d != 0)
        put(rows_of(1 - k, g), slot, sib_s.at[NG + 10 + g], sem, swap[1])
        pl.when(d == 0)(pltpu.make_async_copy(rows_of(k, g), slot, sem).start)
    ours = r_ref.at[:, pl.ds(pl.multiple_of(k * B, 128), B)]
    theirs = r_ref.at[:, pl.ds(pl.multiple_of((1 - k) * B, 128), B)]
    put(theirs, band.at[z, k], sib_s.at[0], sib_r.at[0], sib)
    rcopy = pltpu.make_async_copy(ours, band.at[z, k], loc.at[5])
    rcopy.start()
    put(t_ref, tbuf.at[k], sib_s.at[NG], sib_r.at[NG], sib)
    tcopy = pltpu.make_async_copy(t_ref, tbuf.at[k], loc.at[0])
    tcopy.start()
    put(f_ref.at[:, pl.ds(pl.multiple_of((1 - k) * B, 128), B)], fbuf.at[k], sib_s.at[NG + 1], sib_r.at[NG + 1], sib)
    fcopy = pltpu.make_async_copy(f_ref.at[:, pl.ds(pl.multiple_of(k * B, 128), B)], fbuf.at[k], loc.at[5 + NG])
    fcopy.start()
    for c in local:
        c.wait()
    half = pl.ds(3 * k, 3)
    for q in range(3):
        for p in range(4):
            lbuf[p, y, x, 2 * q : 2 * q + 2] = lloc[q, :, 128 * p : 128 * p + 128].reshape(2, 8, 128)
    cgb[z, k] = jnp.zeros((16, 128), F32)
    cgb[z, k, :, 0:64] = cgl[...]
    cgb[z, k, :, 64:96] = col_[...]
    put(cgb.at[z, k], cgb.at[z, k], sib_s.at[NG + 4], sib_r.at[NG + 4], sib)

    def l_rows():
        part = lbuf.at[:, y, x, half]
        for s in range(1, NY):
            put(part, part, lys.at[s], lyr.at[y], ypeer[s - 1])

    def l_planes():
        for s in range(1, NY):
            frm = up(y, s, NY)
            got(lbuf.at[:, frm, x, half], lyr.at[frm])
        part = lbuf.at[:, :, x, half]
        for i, to in enumerate((xup, xdn)):
            put(part, part, lzs.at[i], lzr.at[i], to)

    def l_far():
        for i, (to, frm) in enumerate(((xup, up(x, -1, NX)), (xdn, up(x, 1, NX)))):
            got(lbuf.at[:, :, frm, half], lzr.at[i])
            part = lbuf.at[pl.ds(2 * i, 2), :, frm, half]
            put(part, part, lfs.at[i], lfr.at[i], to)

    def l_cores():
        far = up(x, 2, NX)
        for i in range(2):
            got(lbuf.at[pl.ds(2 * i, 2), :, far, half], lfr.at[i])
        put(lbuf.at[:, :, :, half], lbuf.at[:, :, :, half], sib_s.at[NG + 5], sib_r.at[NG + 5], sib)

    def adjoint_rows():
        got(cgb.at[z, 1 - k], sib_r.at[NG + 4])
        for s in range(1, NZ):
            put(cgb.at[z], cgb.at[z], cs_.at[s], cr.at[z], zpeer[s - 1])

    lag_d = 2
    lag_e = 4

    def band_ring(hop):
        low, high = up(z, -hop, NZ), up(z, hop, NZ)
        if hop == 0:
            rcopy.wait()
            got(band.at[z, 1 - k], sib_r.at[0])
        else:
            got(band.at[low], zr.at[low])
            if hop < NZ // 2:
                got(band.at[high], zr.at[high])
        if hop < NZ // 2:
            put(band.at[low], band.at[low], zs.at[0, hop], zr.at[low], zup)
        if hop < NZ // 2 - 1:
            put(band.at[high], band.at[high], zs.at[1, hop], zr.at[high], zdn)

    def stage_b(g, o):
        yy = up(y, o, NY)
        slot, sem = rbuf[g].at[x, yy], rr.at[g, x, yy]
        got(slot, sem)
        if -NY // 2 < o <= 0:
            put(slot, slot, ys.at[0, g, o + 4], sem, yup)
        if 0 <= o < NY // 2 - 1:
            put(slot, slot, ys.at[1, g, o + 4], sem, ydn)
        put(slot, slot, xsm.at[0, g, o + 4], sem, xup)
        put(slot, slot, xsm.at[1, g, o + 4], sem, xdn)

    left, right, far = up(x, -1, NX), up(x, 1, NX), up(x, 2, NX)

    def stage_d(g, o):
        yy = up(y, o, NY)
        got(rbuf[g].at[left, yy], rr.at[g, left, yy])
        got(rbuf[g].at[right, yy], rr.at[g, right, yy])
        origin, target = (left, xup) if o % 2 == 0 else (right, xdn)
        chunk = rbuf[g].at[origin, yy]
        put(chunk, chunk, xsm.at[2, g, o + 4], rr.at[g, origin, yy], target)

    def stage_e(g, o):
        yy = up(y, o, NY)
        got(rbuf[g].at[far, yy], rr.at[g, far, yy])

    def piece(g, xx, fresh):
        b = split(rbuf[g][xx].reshape(NZ * 2 * ROWS, WIDTHS[g]))
        part = mm_split((thi[xx], tlo[xx]), b).reshape(NZ, 2 * ROWS, WIDTHS[g])
        psum[g][...] = part if fresh else psum[g][...] + part

    def scatter(g):
        for s in range(1, NZ):
            to = up(z, s, NZ)
            put(psum[g].at[to], sbuf[g].at[z], ss.at[g, s], sr.at[g, z], zpeer[s - 1])
        sbuf[g][z] = psum[g][z]

    tcopy.wait()
    got(tbuf.at[1 - k], sib_r.at[NG])
    for h in range(2):
        for i in range(2):
            thi[2 * h + i], tlo[2 * h + i] = split(tbuf[h, :, 512 * i : 512 * i + 512])

    after = {i: [] for i in range(STEP_COUNT + lag_e)}
    for h, at in enumerate((4, 7, 10, 13, 15)):
        after[at].append(functools.partial(band_ring, h))
    after[13].append(l_rows)
    after[17].append(adjoint_rows)
    for xx in range(NX):
        after[LAST0 + lag_e + 1 + xx].append(functools.partial(piece, 0, xx, xx == 0))
    after[LAST0 + lag_e + 5].append(functools.partial(scatter, 0))
    after[STEP_COUNT].append(functools.partial(piece, 1, x, True))
    after[STEP_COUNT + lag_d].append(functools.partial(piece, 1, left, False))
    after[STEP_COUNT + lag_d].append(functools.partial(piece, 1, right, False))
    for i in range(STEP_COUNT + lag_e):
        for lag, stage in ((0, stage_b), (lag_d, stage_d), (lag_e, stage_e)):
            if 0 <= i - lag < STEP_COUNT:
                stage(*STEPS[i - lag])
        for task in after[i]:
            task()
    l_planes()
    piece(1, far, False)
    scatter(1)
    l_far()

    for q in range(3):
        ltr[q] = lloc[q].T
    for s in range(1, NZ):
        frm = up(z, s, NZ)
        got(cgb.at[frm], cr.at[frm])
    mine = pl.ds(pl.multiple_of(z * 64, 64), 64)

    def cross_half(lo):
        return jnp.concatenate([cgb[c // 2, c % 2, :, 0:64] for c in range(lo, lo + NZ)], 1)

    @pl.when(first)
    def _():
        corner = jnp.concatenate([cgb[c // 2, c % 2, :, 64:96] for c in range(2 * NZ)], 1)
        cross = split(cross_half(0))
        fold[0] = mm(ltr[0, mine, :], corner) + mm_split(split(ltr[2, mine, :]), cross)
        fold[1] = mm_split(split(ltr[1, mine, :]), cross)

    @pl.when(k == 1)
    def _():
        fold[0] = mm(ltr[1, mine, :], cross_half(NZ))

    fcopy.wait()
    got(fbuf.at[1 - k], sib_r.at[NG + 1])
    for g in range(NG):
        for s in range(1, NZ):
            frm = up(z, s, NZ)
            got(sbuf[g].at[frm], sr.at[g, frm])
        total = sbuf[g][0]
        for s in range(1, NZ):
            total = total + sbuf[g][s]
        lanes = slice(STARTS[g], STARTS[g] + WIDTHS[g])
        xr[:, :, lanes] = fbuf[:, :, lanes] - 2.0 * total.reshape(2, ROWS, WIDTHS[g])

    xall = xr[...].reshape(2 * ROWS, B)
    for s in range(NZ):
        xst[s] = xall[:, 64 * s : 64 * s + 64]
    for s in range(1, NZ):
        to = up(z, s, NZ)
        put(xst.at[to], xs.at[z], as_.at[s], ar.at[z], zpeer[s - 1])
    l_cores()
    put(xr.at[1 - k], xo.at[k], sib_s.at[NG + 2], sib_r.at[NG + 2], sib)
    xo[k] = xr[k]
    xs[z] = xst[z]
    for s in range(1, NZ):
        frm = up(z, s, NZ)
        got(xs.at[frm], ar.at[frm])
    put(xs, xs2, sib_s.at[NG + 3], sib_r.at[NG + 3], sib, k == 1)

    def gram(b, src):
        a = split(src[...].reshape(NZ * 64, 64).T)
        gm[b] = (mm_split(a, split(band[...].reshape(B, B))) - fold[b]).reshape(NY, 8, B)

    gram(0, xs)

    @pl.when(first)
    def _():
        got(xs2, sib_r.at[NG + 3])
        gram(1, xs2)

    sides = ((2, first), (1, k == 1))

    def each(fn):
        for nb, cond in sides:
            pl.when(cond)(functools.partial(fn, nb, pl.ds(0, nb)))

    for nb, cond in sides:
        for s in range(1, NY):
            to = up(y, s, NY)
            put(gm.at[pl.ds(0, nb), to], gy.at[pl.ds(0, nb), y], gys.at[s], gyr.at[y], ypeer[s - 1], cond)

    def y_sum(nb, bs):
        gy[0:nb, y] = gm[0:nb, y]
        for s in range(1, NY):
            frm = up(y, s, NY)
            got(gy.at[bs, frm], gyr.at[frm])
        total = gy[0:nb, 0]
        for s in range(1, NY):
            total = total + gy[0:nb, s]
        sg[0:nb] = total
        gx[0:nb, x] = total

    def x_sum(nb, bs):
        for s in range(1, NX):
            frm = up(x, s, NX)
            got(gx.at[bs, frm], gxr.at[frm])
        total = (gx[0:nb, 0] + gx[0:nb, 1]) + (gx[0:nb, 2] + gx[0:nb, 3])
        gz[0:nb, 0, z, y] = total[:, :, 0:W2]
        gz[0:nb, 1, z, y] = total[:, :, W2:B]

    def y_wait(nb, bs):
        for s in range(1, NY):
            frm = up(y, s, NY)
            got(gz.at[bs, 0, z, frm], gar.at[frm])
        for s in range(1, NZ):
            frm = up(z, s, NZ)
            got(gz.at[bs, 1, frm, y], gbr.at[frm])

    each(y_sum)
    for nb, cond in sides:
        for s in range(1, NX):
            put(sg.at[pl.ds(0, nb)], gx.at[pl.ds(0, nb), x], gxs.at[s], gxr.at[x], xpeer[s - 1], cond)

    def factor(q):
        return jnp.concatenate([lbuf[p, :, :, 2 * q : 2 * q + 2].reshape(B, 128) for p in range(4)], 1)

    def tile(q):
        return lambda i, j: lbuf[j, 2 * i : 2 * i + 2, :, 2 * q : 2 * q + 2].reshape(128, 128)

    def second_inverse():
        got(lbuf.at[:, :, :, pl.ds(3 * (1 - k), 3)], sib_r.at[NG + 5])
        invert(tile(1), v2)

    def first_inverse():
        v2t[...] = v2[...].T
        invert(tile(0), v1)

    def coupling_factor():
        l2t[0], l2t[1] = split(factor(1).T)
        l1t[0], l1t[1] = split(factor(0).T)
        l21[0], l21[1] = split(factor(2))
        v1s[0], v1s[1] = split(v1[...])
        v2s[0], v2s[1] = split(v2[...])
        v2ts[0], v2ts[1] = split(v2t[...])
        v1t[...] = v1[...].T
        mmat[...] = mm(factor(2), v1[...])

    def tall_rows():
        mt[...] = mmat[...].T
        ms[0], ms[1] = split(mmat[...])
        got(xo.at[1 - k], sib_r.at[NG + 2])
        h2 = mm(xo[1], v2[...])
        rows_ref[:, B : 2 * B] = h2
        rows_ref[:, 0:B] = mm(xo[0], v1[...]) - mm(h2, mmat[...])

    between = {0: first_inverse, 2: coupling_factor, 4: tall_rows}

    each(x_sum)
    for nb, cond in sides:
        bs = pl.ds(0, nb)
        for s in range(1, NY):
            put(gz.at[bs, 0, z, y], gz.at[bs, 0, z, y], gas.at[s], gar.at[y], ypeer[s - 1], cond)
            put(gz.at[bs, 1, z, y], gz.at[bs, 1, z, y], gbs.at[s], gbr.at[z], zpeer[s - 1], cond)
    second_inverse()
    each(y_wait)
    for j in range(NZ):
        zz, yy = up(z, ORDER[j], NZ), up(y, ORDER[j], NY)
        hop = abs(ORDER[j])
        for nb, cond in sides:
            bs = pl.ds(0, nb)
            chunk, other = gz.at[bs, 0, zz], gz.at[bs, 1, :, yy]
            if j > 0:
                pl.when(cond)(functools.partial(got, chunk, gzr.at[zz]))
                pl.when(cond)(functools.partial(got, other, gwr.at[yy]))
            if j == 0 or (ORDER[j] < 0 and hop < NZ // 2):
                put(chunk, chunk, gzs.at[0, hop], gzr.at[zz], zup, cond)
                put(other, other, gws.at[0, hop], gwr.at[yy], yup, cond)
            if j == 0 or (ORDER[j] > 0 and hop < NZ // 2 - 1):
                put(chunk, chunk, gzs.at[1, hop], gzr.at[zz], zdn, cond)
                put(other, other, gws.at[1, hop], gwr.at[yy], ydn, cond)
        if j in between:
            between[j]()

    def gram_total(b):
        return jnp.concatenate([gz[b, 0].reshape(B, W2), gz[b, 1].reshape(B, W2)], 1)

    r = lax.broadcasted_iota(jnp.int32, (B, B), 0)
    c = lax.broadcasted_iota(jnp.int32, (B, B), 1)
    own = pl.ds(pl.multiple_of(row * 16, 16), 16)

    def lowered(p):
        return jnp.where(r > c, p, jnp.where(r == c, 0.5 * p, 0.0))

    @pl.when(k == 1)
    def _():
        p2 = mm_split(v2ts, split(gram_total(0)))
        q2 = lowered(mm_split(l2t, split(jnp.where(r >= c, -p2, 0.0))))
        w1[...] = mm_split(split(q2 + q2.T), v2s)
        sbm[...] = 0.5 * mm_split(v2ts, split(w1[...]))

    put(sbm, sbm, sib_s.at[NG + 6], sib_r.at[NG + 6], sib, k == 1)

    @pl.when(first)
    def _():
        p1 = split(-mm_split(v2ts, split(gram_total(1))))
        w1[...] = mm_split(p1, v1s)
        w2[...] = mm(v1t[...], gram_total(0)) + mm_split(split(mt[...]), p1)
        got(sbm, sib_r.at[NG + 6])
        coupling = w1[...] - 2.0 * mm_split(split(sbm[...]), ms)
        w1[...] = coupling
        outp[0] = w1[own, :]
        grad = jnp.where(r >= c, -w2[...] - mm_split(split(coupling.T), l21), 0.0)
        q1 = lowered(mm_split(l1t, split(grad)))
        w1[...] = q1 + q1.T
        outp[1] = 0.5 * mm_split(split(mm(v1t[own, :], w1[...])), v1s)

    put(outp, outp, sib_s.at[NG + 7], sib_r.at[NG + 7], sib, first)

    @pl.when(k == 1)
    def _():
        got(outp, sib_r.at[NG + 7])

    shift = lax.rem(B - col * 32, B)
    c_ref[...] = pltpu.roll(outp[0], shift, 1)[:, 0:32]
    b_ref[0] = pltpu.roll(outp[1], shift, 1)[:, 0:32]
    b_ref[1] = pltpu.roll(sbm[own, :], shift, 1)[:, 0:32]

    for c, cond in sends:
        if cond is None:
            c.wait_send()
        else:
            pl.when(cond)(c.wait_send)


def panel_call(*args):
    dma = pltpu.SemaphoreType.DMA
    vm = pl.BlockSpec(memory_space=pltpu.VMEM)
    hbm = pl.BlockSpec(memory_space=pl.ANY)
    square = pltpu.VMEM((B, B), F32)
    return pl.pallas_call(
        panel_kernel,
        out_shape=(
            jax.ShapeDtypeStruct((ROWS, 2 * B), F32),
            jax.ShapeDtypeStruct((2, 16, 32), F32),
            jax.ShapeDtypeStruct((16, 32), F32),
        ),
        in_specs=[hbm] * 7,
        out_specs=(vm, vm, vm),
        scratch_shapes=[
            pltpu.VMEM((2, 512, 1024), F32),
            pltpu.VMEM((NX, 512, 512), BF16),
            pltpu.VMEM((NX, 512, 512), BF16),
            pltpu.VMEM((NZ, 2, ROWS, B), F32),
        ]
        + [pltpu.VMEM((NX, NZ, 2, ROWS, w), F32) for w in WIDTHS]
        + [pltpu.VMEM((NZ, 2 * ROWS, w), F32) for w in WIDTHS]
        + [pltpu.VMEM((NZ, 2 * ROWS, w), F32) for w in WIDTHS]
        + [
            pltpu.VMEM((2, ROWS, B), F32),
            pltpu.VMEM((2, ROWS, B), F32),
            pltpu.VMEM((2, ROWS, B), F32),
            pltpu.VMEM((NZ, 64, 64), F32),
            pltpu.VMEM((NZ, 64, 64), F32),
            pltpu.VMEM((NZ, 64, 64), F32),
            pltpu.VMEM((2, NY, 8, B), F32),
            pltpu.VMEM((2, NY, 8, B), F32),
            pltpu.VMEM((2, 8, B), F32),
            pltpu.VMEM((2, NX, 8, B), F32),
            pltpu.VMEM((2, 2, NZ, NY, 8, W2), F32),
            pltpu.VMEM((3, 16, B), F32),
            pltpu.VMEM((16, 64), F32),
            pltpu.VMEM((16, 32), F32),
            pltpu.VMEM((4, NY, NX, 6, 8, 128), F32),
            pltpu.VMEM((NZ, 2, 16, 128), F32),
            pltpu.VMEM((3, B, 16), F32),
            pltpu.VMEM((2, 64, B), F32),
        ]
        + [square] * 9
        + [pltpu.VMEM((2, 16, B), F32)]
        + [pltpu.VMEM((2, B, B), BF16)] * 7
        + [
            dma((NG + 12,)), dma((NG + 8,)), dma((NG + 6,)),
            dma((2, NZ)), dma((NZ,)),
            dma((2, NG, NZ)), dma((3, NG, NZ)), dma((NG, NX, NZ)),
            dma((NG, NZ)), dma((NG, NZ)),
            dma((NZ,)), dma((NZ,)),
            dma((NY,)), dma((NY,)),
            dma((NX,)), dma((NX,)),
            dma((NY,)), dma((NY,)),
            dma((NZ,)), dma((NZ,)),
            dma((2, NZ // 2)), dma((NZ,)),
            dma((2, NY // 2)), dma((NY,)),
            dma((NY,)), dma((NY,)),
            dma((2,)), dma((2,)), dma((2,)), dma((2,)),
            dma((NZ,)), dma((NZ,)),
        ],
        compiler_params=pltpu.CompilerParams(
            collective_id=0, has_side_effects=True, vmem_limit_bytes=60 * 1024 * 1024
        ),
        name="panel_adjoint",
    )(*args)


def invert(lower, out_ref):
    n = 128
    r = lax.broadcasted_iota(jnp.int32, (n, n), 0)
    c = lax.broadcasted_iota(jnp.int32, (n, n), 1)
    blocks = [lower(q, q) for q in range(4)]
    inv = []
    for a in blocks:
        diag = jnp.sum(jnp.where(r == c, a, 0.0), axis=1, keepdims=True)
        inv.append(jnp.where(r == c, 1.0 / diag, 0.0))
    for lb in range(7):
        mask = ((r >> (lb + 1)) == (c >> (lb + 1))) & ((r >> lb) > (c >> lb))
        for q in range(4):
            cut = jnp.where(mask, blocks[q], 0.0)
            yy = split(inv[q])
            inv[q] = inv[q] - mm_split(yy, split(mm_split(split(cut), yy)))
    zero = jnp.zeros((n, n), F32)
    wide = []
    for h in range(2):
        a, b = inv[2 * h], inv[2 * h + 1]
        low = -mm(b, mm(lower(2 * h + 1, 2 * h), a))
        wide.append(jnp.concatenate([jnp.concatenate([a, zero], 1), jnp.concatenate([low, b], 1)], 0))
    corner = jnp.concatenate(
        [jnp.concatenate([lower(2, 0), lower(2, 1)], 1), jnp.concatenate([lower(3, 0), lower(3, 1)], 1)], 0
    )
    low = -mm(wide[1], mm(corner, wide[0]))
    out_ref[0:256, 0:256] = wide[0]
    out_ref[0:256, 256:512] = jnp.zeros((256, 256), F32)
    out_ref[256:512, 0:256] = low
    out_ref[256:512, 256:512] = wide[1]


def store_kernel(*refs):
    for src, dst in zip(refs[:3], refs[3:]):
        dst[...] = src[...]


def per_device(*args):
    found = panel_call(*args)
    vm = pl.BlockSpec(memory_space=pltpu.VMEM)
    return pl.pallas_call(
        store_kernel,
        out_shape=tuple(jax.ShapeDtypeStruct(f.shape, F32) for f in found),
        in_specs=[vm] * 3,
        out_specs=(vm,) * 3,
        name="store",
    )(*found)


def solution(mesh):
    return jax.shard_map(
        per_device,
        mesh=mesh,
        in_specs=(
            P("row", "col"),
            P(("row", "col"), None),
            P(("row", "col"), None),
            P(None, "row", None),
            P("row", None),
            P("row", "col"),
            P("row", "col"),
        ),
        out_specs=(P(("row", "col"), None), P(None, "row", "col"), P("row", "col")),
        check_vma=False,
    )
```

```python
import functools

import jax
import jax.numpy as jnp
from jax import lax
from jax.experimental import pallas as pl
from jax.experimental.pallas import tpu as pltpu
from jax.sharding import PartitionSpec as P

MESH = pl.DeviceIdType.MESH
F32 = jnp.float32
BF16 = jnp.bfloat16
NX, NY, NZ = 4, 8, 8
B = 512
WIDTHS = (256, 256)
STARTS = (0, 256)
NG = 2
W2 = B // 2
ROWS = 32
ORDER = (0, -1, 1, -2, 2, -3, 3, -4)
STEPS = [(g, o) for g in range(NG) for o in ORDER]
STEP_COUNT = len(STEPS)
LAST0 = NZ - 1


def split(a):
    hi = a.astype(BF16)
    return hi, (a - hi.astype(F32)).astype(BF16)


def dot(a, b):
    return jnp.dot(a, b, preferred_element_type=F32)


def mm_split(a, b):
    return dot(a[0], b[0]) + (dot(a[0], b[1]) + dot(a[1], b[0]))


def mm(a, b):
    return mm_split(split(a), split(b))


def panel_kernel(
    t_ref, r_ref, f_ref, diag_ref, cross_ref, cg_ref, co_ref,
    rows_ref, b_ref, c_ref,
    tbuf, thi, tlo, band, rb0, rb1, ps0, ps1, sb0, sb1, fbuf, xr, xo, xst, xs, xs2, gm, gy, sg, gx, gz,
    lloc, cgl, col_, lbuf, cgb, ltr, fold, v1, v2, v1t, v2t, mmat, mt, w1, w2, sbm, outp,
    l1t, l2t, l21, v1s, v2s, v2ts, ms,
    sib_s, sib_r, loc, zs, zr, ys, xsm, rr, ss, sr, as_, ar, gys, gyr, gxs, gxr, gas, gar, gbs, gbr, gzs, gzr,
    gws, gwr, lys, lyr, lzs, lzr, lfs, lfr, cs_, cr,
):
    local = [
        pltpu.make_async_copy(diag_ref, lloc.at[pl.ds(0, 2)], loc.at[1]),
        pltpu.make_async_copy(cross_ref, lloc.at[2], loc.at[2]),
        pltpu.make_async_copy(cg_ref, cgl, loc.at[3]),
        pltpu.make_async_copy(co_ref, col_, loc.at[4]),
    ]
    for c in local:
        c.start()
    rbuf, psum, sbuf = (rb0, rb1), (ps0, ps1), (sb0, sb1)
    row = lax.axis_index("row")
    col = lax.axis_index("col")
    y, x = row // NX, lax.rem(row, NX)
    z, k = col // 2, lax.rem(col, 2)

    def dev(px, py, pz, pk):
        return {"row": py * NX + px, "col": pz * 2 + pk}

    def up(v, s, n):
        return lax.rem(v + (s + n), n)

    sib = dev(x, y, z, 1 - k)
    zpeer = [dev(x, y, up(z, s, NZ), k) for s in range(1, NZ)]
    ypeer = [dev(x, up(y, s, NY), z, k) for s in range(1, NY)]
    xpeer = [dev(up(x, s, NX), y, z, k) for s in range(1, NX)]
    zup, zdn = zpeer[0], zpeer[-1]
    yup, ydn = ypeer[0], ypeer[-1]
    xup, xdn = xpeer[0], xpeer[-1]
    d = up(y - z, NY, NY)

    barrier = pltpu.get_barrier_semaphore()
    partners = [sib, zup, zdn, yup, ydn] + xpeer
    for p in partners:
        pl.semaphore_signal(barrier, inc=1, device_id=p, device_id_type=MESH)

    swap = [dev(x, z, y, k), dev(x, z, y, 1 - k)]

    @pl.when(d != 0)
    def _():
        for p in swap:
            pl.semaphore_signal(barrier, inc=1, device_id=p, device_id_type=MESH)

    pl.semaphore_wait(barrier, len(partners) + jnp.where(d == 0, 0, 2))

    sends = []

    def put(src, dst, ssem, rsem, target, cond=None):
        c = pltpu.make_async_remote_copy(
            src_ref=src, dst_ref=dst, send_sem=ssem, recv_sem=rsem, device_id=target, device_id_type=MESH
        )
        if cond is None:
            c.start()
        else:
            pl.when(cond)(c.start)
        sends.append((c, cond))

    def got(ref, sem):
        pltpu.make_async_remote_copy(
            src_ref=ref, dst_ref=ref, send_sem=sem, recv_sem=sem, device_id=sib, device_id_type=MESH
        ).wait_recv()

    first = k == 0
    def rows_of(core, g):
        return r_ref.at[:, pl.ds(pl.multiple_of(core * B + STARTS[g], 128), WIDTHS[g])]

    for g in range(NG):
        slot, sem = rbuf[g].at[x, z, k], rr.at[g, x, z]
        put(rows_of(k, g), slot, sib_s.at[NG + 8 + g], sem, swap[0], d != 0)
        put(rows_of(1 - k, g), slot, sib_s.at[NG + 10 + g], sem, swap[1])
        pl.when(d == 0)(pltpu.make_async_copy(rows_of(k, g), slot, sem).start)
    ours = r_ref.at[:, pl.ds(pl.multiple_of(k * B, 128), B)]
    theirs = r_ref.at[:, pl.ds(pl.multiple_of((1 - k) * B, 128), B)]
    put(theirs, band.at[z, k], sib_s.at[0], sib_r.at[0], sib)
    rcopy = pltpu.make_async_copy(ours, band.at[z, k], loc.at[5])
    rcopy.start()
    put(t_ref, tbuf.at[k], sib_s.at[NG], sib_r.at[NG], sib)
    tcopy = pltpu.make_async_copy(t_ref, tbuf.at[k], loc.at[0])
    tcopy.start()
    put(f_ref.at[:, pl.ds(pl.multiple_of((1 - k) * B, 128), B)], fbuf.at[k], sib_s.at[NG + 1], sib_r.at[NG + 1], sib)
    fcopy = pltpu.make_async_copy(f_ref.at[:, pl.ds(pl.multiple_of(k * B, 128), B)], fbuf.at[k], loc.at[5 + NG])
    fcopy.start()
    for c in local:
        c.wait()
    half = pl.ds(3 * k, 3)
    for q in range(3):
        for p in range(4):
            lbuf[p, y, x, 2 * q : 2 * q + 2] = lloc[q, :, 128 * p : 128 * p + 128].reshape(2, 8, 128)
    cgb[z, k] = jnp.zeros((16, 128), F32)
    cgb[z, k, :, 0:64] = cgl[...]
    cgb[z, k, :, 64:96] = col_[...]
    put(cgb.at[z, k], cgb.at[z, k], sib_s.at[NG + 4], sib_r.at[NG + 4], sib)

    def l_rows():
        part = lbuf.at[:, y, x, half]
        for s in range(1, NY):
            put(part, part, lys.at[s], lyr.at[y], ypeer[s - 1])

    def l_planes():
        for s in range(1, NY):
            frm = up(y, s, NY)
            got(lbuf.at[:, frm, x, half], lyr.at[frm])
        part = lbuf.at[:, :, x, half]
        for i, to in enumerate((xup, xdn)):
            put(part, part, lzs.at[i], lzr.at[i], to)

    def l_far():
        for i, (to, frm) in enumerate(((xup, up(x, -1, NX)), (xdn, up(x, 1, NX)))):
            got(lbuf.at[:, :, frm, half], lzr.at[i])
            part = lbuf.at[pl.ds(2 * i, 2), :, frm, half]
            put(part, part, lfs.at[i], lfr.at[i], to)

    def l_cores():
        far = up(x, 2, NX)
        for i in range(2):
            got(lbuf.at[pl.ds(2 * i, 2), :, far, half], lfr.at[i])
        put(lbuf.at[:, :, :, half], lbuf.at[:, :, :, half], sib_s.at[NG + 5], sib_r.at[NG + 5], sib)

    def adjoint_rows():
        got(cgb.at[z, 1 - k], sib_r.at[NG + 4])
        for s in range(1, NZ):
            put(cgb.at[z], cgb.at[z], cs_.at[s], cr.at[z], zpeer[s - 1])

    lag_d = 4
    lag_e = 8

    def band_ring(hop):
        low, high = up(z, -hop, NZ), up(z, hop, NZ)
        if hop == 0:
            rcopy.wait()
            got(band.at[z, 1 - k], sib_r.at[0])
        else:
            got(band.at[low], zr.at[low])
            if hop < NZ // 2:
                got(band.at[high], zr.at[high])
        if hop < NZ // 2:
            put(band.at[low], band.at[low], zs.at[0, hop], zr.at[low], zup)
        if hop < NZ // 2 - 1:
            put(band.at[high], band.at[high], zs.at[1, hop], zr.at[high], zdn)

    def stage_b(g, o):
        yy = up(y, o, NY)
        slot, sem = rbuf[g].at[x, yy], rr.at[g, x, yy]
        got(slot, sem)
        if -NY // 2 < o <= 0:
            put(slot, slot, ys.at[0, g, o + 4], sem, yup)
        if 0 <= o < NY // 2 - 1:
            put(slot, slot, ys.at[1, g, o + 4], sem, ydn)
        put(slot, slot, xsm.at[0, g, o + 4], sem, xup)
        put(slot, slot, xsm.at[1, g, o + 4], sem, xdn)

    left, right, far = up(x, -1, NX), up(x, 1, NX), up(x, 2, NX)

    def stage_d(g, o):
        yy = up(y, o, NY)
        got(rbuf[g].at[left, yy], rr.at[g, left, yy])
        got(rbuf[g].at[right, yy], rr.at[g, right, yy])
        origin, target = (left, xup) if o % 2 == 0 else (right, xdn)
        chunk = rbuf[g].at[origin, yy]
        put(chunk, chunk, xsm.at[2, g, o + 4], rr.at[g, origin, yy], target)

    def stage_e(g, o):
        yy = up(y, o, NY)
        got(rbuf[g].at[far, yy], rr.at[g, far, yy])

    def piece(g, xx, fresh):
        b = split(rbuf[g][xx].reshape(NZ * 2 * ROWS, WIDTHS[g]))
        part = mm_split((thi[xx], tlo[xx]), b).reshape(NZ, 2 * ROWS, WIDTHS[g])
        psum[g][...] = part if fresh else psum[g][...] + part

    def scatter(g):
        for s in range(1, NZ):
            to = up(z, s, NZ)
            put(psum[g].at[to], sbuf[g].at[z], ss.at[g, s], sr.at[g, z], zpeer[s - 1])
        sbuf[g][z] = psum[g][z]

    tcopy.wait()
    got(tbuf.at[1 - k], sib_r.at[NG])
    for h in range(2):
        for i in range(2):
            thi[2 * h + i], tlo[2 * h + i] = split(tbuf[h, :, 512 * i : 512 * i + 512])

    after = {i: [] for i in range(STEP_COUNT + lag_e)}
    for h, at in enumerate((4, 7, 10, 13, 15)):
        after[at].append(functools.partial(band_ring, h))
    after[13].append(l_rows)
    after[17].append(adjoint_rows)
    for xx in range(NX):
        after[LAST0 + lag_e + 1 + xx].append(functools.partial(piece, 0, xx, xx == 0))
    after[LAST0 + lag_e + 5].append(functools.partial(scatter, 0))
    after[STEP_COUNT].append(functools.partial(piece, 1, x, True))
    after[STEP_COUNT + lag_d].append(functools.partial(piece, 1, left, False))
    after[STEP_COUNT + lag_d].append(functools.partial(piece, 1, right, False))
    for i in range(STEP_COUNT + lag_e):
        for lag, stage in ((0, stage_b), (lag_d, stage_d), (lag_e, stage_e)):
            if 0 <= i - lag < STEP_COUNT:
                stage(*STEPS[i - lag])
        for task in after[i]:
            task()
    l_planes()
    piece(1, far, False)
    scatter(1)
    l_far()

    for q in range(3):
        ltr[q] = lloc[q].T
    for s in range(1, NZ):
        frm = up(z, s, NZ)
        got(cgb.at[frm], cr.at[frm])
    mine = pl.ds(pl.multiple_of(z * 64, 64), 64)

    def cross_half(lo):
        return jnp.concatenate([cgb[c // 2, c % 2, :, 0:64] for c in range(lo, lo + NZ)], 1)

    @pl.when(first)
    def _():
        corner = jnp.concatenate([cgb[c // 2, c % 2, :, 64:96] for c in range(2 * NZ)], 1)
        cross = split(cross_half(0))
        fold[0] = mm(ltr[0, mine, :], corner) + mm_split(split(ltr[2, mine, :]), cross)
        fold[1] = mm_split(split(ltr[1, mine, :]), cross)

    @pl.when(k == 1)
    def _():
        fold[0] = mm(ltr[1, mine, :], cross_half(NZ))

    fcopy.wait()
    got(fbuf.at[1 - k], sib_r.at[NG + 1])
    for g in range(NG):
        for s in range(1, NZ):
            frm = up(z, s, NZ)
            got(sbuf[g].at[frm], sr.at[g, frm])
        total = sbuf[g][0]
        for s in range(1, NZ):
            total = total + sbuf[g][s]
        lanes = slice(STARTS[g], STARTS[g] + WIDTHS[g])
        xr[:, :, lanes] = fbuf[:, :, lanes] - 2.0 * total.reshape(2, ROWS, WIDTHS[g])

    xall = xr[...].reshape(2 * ROWS, B)
    for s in range(NZ):
        xst[s] = xall[:, 64 * s : 64 * s + 64]
    for s in range(1, NZ):
        to = up(z, s, NZ)
        put(xst.at[to], xs.at[z], as_.at[s], ar.at[z], zpeer[s - 1])
    l_cores()
    put(xr.at[1 - k], xo.at[k], sib_s.at[NG + 2], sib_r.at[NG + 2], sib)
    xo[k] = xr[k]
    xs[z] = xst[z]
    for s in range(1, NZ):
        frm = up(z, s, NZ)
        got(xs.at[frm], ar.at[frm])
    put(xs, xs2, sib_s.at[NG + 3], sib_r.at[NG + 3], sib, k == 1)

    def gram(b, src):
        a = split(src[...].reshape(NZ * 64, 64).T)
        gm[b] = (mm_split(a, split(band[...].reshape(B, B))) - fold[b]).reshape(NY, 8, B)

    gram(0, xs)

    @pl.when(first)
    def _():
        got(xs2, sib_r.at[NG + 3])
        gram(1, xs2)

    sides = ((2, first), (1, k == 1))

    def each(fn):
        for nb, cond in sides:
            pl.when(cond)(functools.partial(fn, nb, pl.ds(0, nb)))

    for nb, cond in sides:
        for s in range(1, NY):
            to = up(y, s, NY)
            put(gm.at[pl.ds(0, nb), to], gy.at[pl.ds(0, nb), y], gys.at[s], gyr.at[y], ypeer[s - 1], cond)

    def y_sum(nb, bs):
        gy[0:nb, y] = gm[0:nb, y]
        for s in range(1, NY):
            frm = up(y, s, NY)
            got(gy.at[bs, frm], gyr.at[frm])
        total = gy[0:nb, 0]
        for s in range(1, NY):
            total = total + gy[0:nb, s]
        sg[0:nb] = total
        gx[0:nb, x] = total

    def x_sum(nb, bs):
        for s in range(1, NX):
            frm = up(x, s, NX)
            got(gx.at[bs, frm], gxr.at[frm])
        total = (gx[0:nb, 0] + gx[0:nb, 1]) + (gx[0:nb, 2] + gx[0:nb, 3])
        gz[0:nb, 0, z, y] = total[:, :, 0:W2]
        gz[0:nb, 1, z, y] = total[:, :, W2:B]

    def y_wait(nb, bs):
        for s in range(1, NY):
            frm = up(y, s, NY)
            got(gz.at[bs, 0, z, frm], gar.at[frm])
        for s in range(1, NZ):
            frm = up(z, s, NZ)
            got(gz.at[bs, 1, frm, y], gbr.at[frm])

    each(y_sum)
    for nb, cond in sides:
        for s in range(1, NX):
            put(sg.at[pl.ds(0, nb)], gx.at[pl.ds(0, nb), x], gxs.at[s], gxr.at[x], xpeer[s - 1], cond)

    def factor(q):
        return jnp.concatenate([lbuf[p, :, :, 2 * q : 2 * q + 2].reshape(B, 128) for p in range(4)], 1)

    def tile(q):
        return lambda i, j: lbuf[j, 2 * i : 2 * i + 2, :, 2 * q : 2 * q + 2].reshape(128, 128)

    def second_inverse():
        got(lbuf.at[:, :, :, pl.ds(3 * (1 - k), 3)], sib_r.at[NG + 5])
        invert(tile(1), v2)

    def first_inverse():
        v2t[...] = v2[...].T
        invert(tile(0), v1)

    def coupling_factor():
        l2t[0], l2t[1] = split(factor(1).T)
        l1t[0], l1t[1] = split(factor(0).T)
        l21[0], l21[1] = split(factor(2))
        v1s[0], v1s[1] = split(v1[...])
        v2s[0], v2s[1] = split(v2[...])
        v2ts[0], v2ts[1] = split(v2t[...])
        v1t[...] = v1[...].T
        mmat[...] = mm(factor(2), v1[...])

    def tall_rows():
        mt[...] = mmat[...].T
        ms[0], ms[1] = split(mmat[...])
        got(xo.at[1 - k], sib_r.at[NG + 2])
        h2 = mm(xo[1], v2[...])
        rows_ref[:, B : 2 * B] = h2
        rows_ref[:, 0:B] = mm(xo[0], v1[...]) - mm(h2, mmat[...])

    between = {0: first_inverse, 2: coupling_factor, 4: tall_rows}

    each(x_sum)
    for nb, cond in sides:
        bs = pl.ds(0, nb)
        for s in range(1, NY):
            put(gz.at[bs, 0, z, y], gz.at[bs, 0, z, y], gas.at[s], gar.at[y], ypeer[s - 1], cond)
            put(gz.at[bs, 1, z, y], gz.at[bs, 1, z, y], gbs.at[s], gbr.at[z], zpeer[s - 1], cond)
    second_inverse()
    each(y_wait)
    for j in range(NZ):
        zz, yy = up(z, ORDER[j], NZ), up(y, ORDER[j], NY)
        hop = abs(ORDER[j])
        for nb, cond in sides:
            bs = pl.ds(0, nb)
            chunk, other = gz.at[bs, 0, zz], gz.at[bs, 1, :, yy]
            if j > 0:
                pl.when(cond)(functools.partial(got, chunk, gzr.at[zz]))
                pl.when(cond)(functools.partial(got, other, gwr.at[yy]))
            if j == 0 or (ORDER[j] < 0 and hop < NZ // 2):
                put(chunk, chunk, gzs.at[0, hop], gzr.at[zz], zup, cond)
                put(other, other, gws.at[0, hop], gwr.at[yy], yup, cond)
            if j == 0 or (ORDER[j] > 0 and hop < NZ // 2 - 1):
                put(chunk, chunk, gzs.at[1, hop], gzr.at[zz], zdn, cond)
                put(other, other, gws.at[1, hop], gwr.at[yy], ydn, cond)
        if j in between:
            between[j]()

    def gram_total(b):
        return jnp.concatenate([gz[b, 0].reshape(B, W2), gz[b, 1].reshape(B, W2)], 1)

    r = lax.broadcasted_iota(jnp.int32, (B, B), 0)
    c = lax.broadcasted_iota(jnp.int32, (B, B), 1)
    own = pl.ds(pl.multiple_of(row * 16, 16), 16)

    def lowered(p):
        return jnp.where(r > c, p, jnp.where(r == c, 0.5 * p, 0.0))

    @pl.when(k == 1)
    def _():
        p2 = mm_split(v2ts, split(gram_total(0)))
        q2 = lowered(mm_split(l2t, split(jnp.where(r >= c, -p2, 0.0))))
        w1[...] = mm_split(split(q2 + q2.T), v2s)
        sbm[...] = 0.5 * mm_split(v2ts, split(w1[...]))

    put(sbm, sbm, sib_s.at[NG + 6], sib_r.at[NG + 6], sib, k == 1)

    @pl.when(first)
    def _():
        p1 = split(-mm_split(v2ts, split(gram_total(1))))
        w1[...] = mm_split(p1, v1s)
        w2[...] = mm(v1t[...], gram_total(0)) + mm_split(split(mt[...]), p1)
        got(sbm, sib_r.at[NG + 6])
        coupling = w1[...] - 2.0 * mm_split(split(sbm[...]), ms)
        w1[...] = coupling
        outp[0] = w1[own, :]
        grad = jnp.where(r >= c, -w2[...] - mm_split(split(coupling.T), l21), 0.0)
        q1 = lowered(mm_split(l1t, split(grad)))
        w1[...] = q1 + q1.T
        outp[1] = 0.5 * mm_split(split(mm(v1t[own, :], w1[...])), v1s)

    put(outp, outp, sib_s.at[NG + 7], sib_r.at[NG + 7], sib, first)

    @pl.when(k == 1)
    def _():
        got(outp, sib_r.at[NG + 7])

    shift = lax.rem(B - col * 32, B)
    c_ref[...] = pltpu.roll(outp[0], shift, 1)[:, 0:32]
    b_ref[0] = pltpu.roll(outp[1], shift, 1)[:, 0:32]
    b_ref[1] = pltpu.roll(sbm[own, :], shift, 1)[:, 0:32]

    for c, cond in sends:
        if cond is None:
            c.wait_send()
        else:
            pl.when(cond)(c.wait_send)


def panel_call(*args):
    dma = pltpu.SemaphoreType.DMA
    vm = pl.BlockSpec(memory_space=pltpu.VMEM)
    hbm = pl.BlockSpec(memory_space=pl.ANY)
    square = pltpu.VMEM((B, B), F32)
    return pl.pallas_call(
        panel_kernel,
        out_shape=(
            jax.ShapeDtypeStruct((ROWS, 2 * B), F32),
            jax.ShapeDtypeStruct((2, 16, 32), F32),
            jax.ShapeDtypeStruct((16, 32), F32),
        ),
        in_specs=[hbm] * 7,
        out_specs=(vm, vm, vm),
        scratch_shapes=[
            pltpu.VMEM((2, 512, 1024), F32),
            pltpu.VMEM((NX, 512, 512), BF16),
            pltpu.VMEM((NX, 512, 512), BF16),
            pltpu.VMEM((NZ, 2, ROWS, B), F32),
        ]
        + [pltpu.VMEM((NX, NZ, 2, ROWS, w), F32) for w in WIDTHS]
        + [pltpu.VMEM((NZ, 2 * ROWS, w), F32) for w in WIDTHS]
        + [pltpu.VMEM((NZ, 2 * ROWS, w), F32) for w in WIDTHS]
        + [
            pltpu.VMEM((2, ROWS, B), F32),
            pltpu.VMEM((2, ROWS, B), F32),
            pltpu.VMEM((2, ROWS, B), F32),
            pltpu.VMEM((NZ, 64, 64), F32),
            pltpu.VMEM((NZ, 64, 64), F32),
            pltpu.VMEM((NZ, 64, 64), F32),
            pltpu.VMEM((2, NY, 8, B), F32),
            pltpu.VMEM((2, NY, 8, B), F32),
            pltpu.VMEM((2, 8, B), F32),
            pltpu.VMEM((2, NX, 8, B), F32),
            pltpu.VMEM((2, 2, NZ, NY, 8, W2), F32),
            pltpu.VMEM((3, 16, B), F32),
            pltpu.VMEM((16, 64), F32),
            pltpu.VMEM((16, 32), F32),
            pltpu.VMEM((4, NY, NX, 6, 8, 128), F32),
            pltpu.VMEM((NZ, 2, 16, 128), F32),
            pltpu.VMEM((3, B, 16), F32),
            pltpu.VMEM((2, 64, B), F32),
        ]
        + [square] * 9
        + [pltpu.VMEM((2, 16, B), F32)]
        + [pltpu.VMEM((2, B, B), BF16)] * 7
        + [
            dma((NG + 12,)), dma((NG + 8,)), dma((NG + 6,)),
            dma((2, NZ)), dma((NZ,)),
            dma((2, NG, NZ)), dma((3, NG, NZ)), dma((NG, NX, NZ)),
            dma((NG, NZ)), dma((NG, NZ)),
            dma((NZ,)), dma((NZ,)),
            dma((NY,)), dma((NY,)),
            dma((NX,)), dma((NX,)),
            dma((NY,)), dma((NY,)),
            dma((NZ,)), dma((NZ,)),
            dma((2, NZ // 2)), dma((NZ,)),
            dma((2, NY // 2)), dma((NY,)),
            dma((NY,)), dma((NY,)),
            dma((2,)), dma((2,)), dma((2,)), dma((2,)),
            dma((NZ,)), dma((NZ,)),
        ],
        compiler_params=pltpu.CompilerParams(
            collective_id=0, has_side_effects=True, vmem_limit_bytes=60 * 1024 * 1024
        ),
        name="panel_adjoint",
    )(*args)


def invert(lower, out_ref):
    n = 128
    r = lax.broadcasted_iota(jnp.int32, (n, n), 0)
    c = lax.broadcasted_iota(jnp.int32, (n, n), 1)
    blocks = [lower(q, q) for q in range(4)]
    inv = []
    for a in blocks:
        diag = jnp.sum(jnp.where(r == c, a, 0.0), axis=1, keepdims=True)
        inv.append(jnp.where(r == c, 1.0 / diag, 0.0))
    for lb in range(7):
        mask = ((r >> (lb + 1)) == (c >> (lb + 1))) & ((r >> lb) > (c >> lb))
        for q in range(4):
            cut = jnp.where(mask, blocks[q], 0.0)
            yy = split(inv[q])
            inv[q] = inv[q] - mm_split(yy, split(mm_split(split(cut), yy)))
    zero = jnp.zeros((n, n), F32)
    wide = []
    for h in range(2):
        a, b = inv[2 * h], inv[2 * h + 1]
        low = -mm(b, mm(lower(2 * h + 1, 2 * h), a))
        wide.append(jnp.concatenate([jnp.concatenate([a, zero], 1), jnp.concatenate([low, b], 1)], 0))
    corner = jnp.concatenate(
        [jnp.concatenate([lower(2, 0), lower(2, 1)], 1), jnp.concatenate([lower(3, 0), lower(3, 1)], 1)], 0
    )
    low = -mm(wide[1], mm(corner, wide[0]))
    out_ref[0:256, 0:256] = wide[0]
    out_ref[0:256, 256:512] = jnp.zeros((256, 256), F32)
    out_ref[256:512, 0:256] = low
    out_ref[256:512, 256:512] = wide[1]


def store_kernel(*refs):
    for src, dst in zip(refs[:3], refs[3:]):
        dst[...] = src[...]


def per_device(*args):
    found = panel_call(*args)
    vm = pl.BlockSpec(memory_space=pltpu.VMEM)
    return pl.pallas_call(
        store_kernel,
        out_shape=tuple(jax.ShapeDtypeStruct(f.shape, F32) for f in found),
        in_specs=[vm] * 3,
        out_specs=(vm,) * 3,
        name="store",
    )(*found)


def solution(mesh):
    return jax.shard_map(
        per_device,
        mesh=mesh,
        in_specs=(
            P("row", "col"),
            P(("row", "col"), None),
            P(("row", "col"), None),
            P(None, "row", None),
            P("row", None),
            P("row", "col"),
            P("row", "col"),
        ),
        out_specs=(P(("row", "col"), None), P(None, "row", "col"), P("row", "col")),
        check_vma=False,
    )
```

```python
import functools

import jax
import jax.numpy as jnp
from jax import lax
from jax.experimental import pallas as pl
from jax.experimental.pallas import tpu as pltpu
from jax.sharding import PartitionSpec as P

MESH = pl.DeviceIdType.MESH
F32 = jnp.float32
BF16 = jnp.bfloat16
NX, NY, NZ = 4, 8, 8
B = 512
WIDTHS = (256, 256)
STARTS = (0, 256)
NG = 2
W2 = B // 2
ROWS = 32
ORDER = (0, -1, 1, -2, 2, -3, 3, -4)
STEPS = [(g, o) for g in range(NG) for o in ORDER]
STEP_COUNT = len(STEPS)
LAST0 = NZ - 1


def split(a):
    hi = a.astype(BF16)
    return hi, (a - hi.astype(F32)).astype(BF16)


def dot(a, b):
    return jnp.dot(a, b, preferred_element_type=F32)


def mm_split(a, b):
    return dot(a[0], b[0]) + (dot(a[0], b[1]) + dot(a[1], b[0]))


def mm(a, b):
    return mm_split(split(a), split(b))


def panel_kernel(
    t_ref, r_ref, f_ref, diag_ref, cross_ref, cg_ref, co_ref,
    rows_ref, b_ref, c_ref,
    tbuf, thi, tlo, band, rb0, rb1, ps0, ps1, sb0, sb1, fbuf, xr, xo, xst, xs, xs2, gm, gy, sg, gx, gz,
    lloc, cgl, col_, lbuf, cgb, ltr, fold, v1, v2, v1t, v2t, mmat, mt, w1, w2, sbm, outp,
    l1t, l2t, l21, v1s, v2s, v2ts, ms, bsp,
    sib_s, sib_r, loc, zs, zr, ys, xsm, rr, ss, sr, as_, ar, gys, gyr, gxs, gxr, gas, gar, gbs, gbr, gzs, gzr,
    gws, gwr, lys, lyr, lzs, lzr, lfs, lfr, cs_, cr,
):
    local = [
        pltpu.make_async_copy(diag_ref, lloc.at[pl.ds(0, 2)], loc.at[1]),
        pltpu.make_async_copy(cross_ref, lloc.at[2], loc.at[2]),
        pltpu.make_async_copy(cg_ref, cgl, loc.at[3]),
        pltpu.make_async_copy(co_ref, col_, loc.at[4]),
    ]
    for c in local:
        c.start()
    rbuf, psum, sbuf = (rb0, rb1), (ps0, ps1), (sb0, sb1)
    row = lax.axis_index("row")
    col = lax.axis_index("col")
    y, x = row // NX, lax.rem(row, NX)
    z, k = col // 2, lax.rem(col, 2)

    def dev(px, py, pz, pk):
        return {"row": py * NX + px, "col": pz * 2 + pk}

    def up(v, s, n):
        return lax.rem(v + (s + n), n)

    sib = dev(x, y, z, 1 - k)
    zpeer = [dev(x, y, up(z, s, NZ), k) for s in range(1, NZ)]
    ypeer = [dev(x, up(y, s, NY), z, k) for s in range(1, NY)]
    xpeer = [dev(up(x, s, NX), y, z, k) for s in range(1, NX)]
    zup, zdn = zpeer[0], zpeer[-1]
    yup, ydn = ypeer[0], ypeer[-1]
    xup, xdn = xpeer[0], xpeer[-1]
    d = up(y - z, NY, NY)

    barrier = pltpu.get_barrier_semaphore()
    partners = [sib, zup, zdn, yup, ydn] + xpeer
    for p in partners:
        pl.semaphore_signal(barrier, inc=1, device_id=p, device_id_type=MESH)

    swap = [dev(x, z, y, k), dev(x, z, y, 1 - k)]

    @pl.when(d != 0)
    def _():
        for p in swap:
            pl.semaphore_signal(barrier, inc=1, device_id=p, device_id_type=MESH)

    pl.semaphore_wait(barrier, len(partners) + jnp.where(d == 0, 0, 2))

    sends = []

    def put(src, dst, ssem, rsem, target, cond=None):
        c = pltpu.make_async_remote_copy(
            src_ref=src, dst_ref=dst, send_sem=ssem, recv_sem=rsem, device_id=target, device_id_type=MESH
        )
        if cond is None:
            c.start()
        else:
            pl.when(cond)(c.start)
        sends.append((c, cond))

    def got(ref, sem):
        pltpu.make_async_remote_copy(
            src_ref=ref, dst_ref=ref, send_sem=sem, recv_sem=sem, device_id=sib, device_id_type=MESH
        ).wait_recv()

    first = k == 0
    def rows_of(core, g):
        return r_ref.at[:, pl.ds(pl.multiple_of(core * B + STARTS[g], 128), WIDTHS[g])]

    for g in range(NG):
        slot, sem = rbuf[g].at[x, z, k], rr.at[g, x, z]
        put(rows_of(k, g), slot, sib_s.at[NG + 8 + g], sem, swap[0], d != 0)
        put(rows_of(1 - k, g), slot, sib_s.at[NG + 10 + g], sem, swap[1])
        pl.when(d == 0)(pltpu.make_async_copy(rows_of(k, g), slot, sem).start)
    ours = r_ref.at[:, pl.ds(pl.multiple_of(k * B, 128), B)]
    theirs = r_ref.at[:, pl.ds(pl.multiple_of((1 - k) * B, 128), B)]
    put(theirs, band.at[z, k], sib_s.at[0], sib_r.at[0], sib)
    rcopy = pltpu.make_async_copy(ours, band.at[z, k], loc.at[5])
    rcopy.start()
    put(t_ref, tbuf.at[k], sib_s.at[NG], sib_r.at[NG], sib)
    tcopy = pltpu.make_async_copy(t_ref, tbuf.at[k], loc.at[0])
    tcopy.start()
    put(f_ref.at[:, pl.ds(pl.multiple_of((1 - k) * B, 128), B)], fbuf.at[k], sib_s.at[NG + 1], sib_r.at[NG + 1], sib)
    fcopy = pltpu.make_async_copy(f_ref.at[:, pl.ds(pl.multiple_of(k * B, 128), B)], fbuf.at[k], loc.at[5 + NG])
    fcopy.start()
    for c in local:
        c.wait()
    half = pl.ds(3 * k, 3)
    for q in range(3):
        for p in range(4):
            lbuf[p, y, x, 2 * q : 2 * q + 2] = lloc[q, :, 128 * p : 128 * p + 128].reshape(2, 8, 128)
    cgb[z, k] = jnp.zeros((16, 128), F32)
    cgb[z, k, :, 0:64] = cgl[...]
    cgb[z, k, :, 64:96] = col_[...]
    put(cgb.at[z, k], cgb.at[z, k], sib_s.at[NG + 4], sib_r.at[NG + 4], sib)

    def l_rows():
        part = lbuf.at[:, y, x, half]
        for s in range(1, NY):
            put(part, part, lys.at[s], lyr.at[y], ypeer[s - 1])

    def l_planes():
        for s in range(1, NY):
            frm = up(y, s, NY)
            got(lbuf.at[:, frm, x, half], lyr.at[frm])
        part = lbuf.at[:, :, x, half]
        for i, to in enumerate((xup, xdn)):
            put(part, part, lzs.at[i], lzr.at[i], to)

    def l_far():
        for i, (to, frm) in enumerate(((xup, up(x, -1, NX)), (xdn, up(x, 1, NX)))):
            got(lbuf.at[:, :, frm, half], lzr.at[i])
            part = lbuf.at[pl.ds(2 * i, 2), :, frm, half]
            put(part, part, lfs.at[i], lfr.at[i], to)

    def l_cores():
        far = up(x, 2, NX)
        for i in range(2):
            got(lbuf.at[pl.ds(2 * i, 2), :, far, half], lfr.at[i])
        put(lbuf.at[:, :, :, half], lbuf.at[:, :, :, half], sib_s.at[NG + 5], sib_r.at[NG + 5], sib)

    def adjoint_rows():
        got(cgb.at[z, 1 - k], sib_r.at[NG + 4])
        for s in range(1, NZ):
            put(cgb.at[z], cgb.at[z], cs_.at[s], cr.at[z], zpeer[s - 1])

    lag_d = 4
    lag_e = 8

    def band_ring(hop):
        low, high = up(z, -hop, NZ), up(z, hop, NZ)
        if hop == 0:
            rcopy.wait()
            got(band.at[z, 1 - k], sib_r.at[0])
        else:
            got(band.at[low], zr.at[low])
            if hop < NZ // 2:
                got(band.at[high], zr.at[high])
        if hop < NZ // 2:
            put(band.at[low], band.at[low], zs.at[0, hop], zr.at[low], zup)
        if hop < NZ // 2 - 1:
            put(band.at[high], band.at[high], zs.at[1, hop], zr.at[high], zdn)

    def stage_b(g, o):
        yy = up(y, o, NY)
        slot, sem = rbuf[g].at[x, yy], rr.at[g, x, yy]
        got(slot, sem)
        if -NY // 2 < o <= 0:
            put(slot, slot, ys.at[0, g, o + 4], sem, yup)
        if 0 <= o < NY // 2 - 1:
            put(slot, slot, ys.at[1, g, o + 4], sem, ydn)
        put(slot, slot, xsm.at[0, g, o + 4], sem, xup)
        put(slot, slot, xsm.at[1, g, o + 4], sem, xdn)

    left, right, far = up(x, -1, NX), up(x, 1, NX), up(x, 2, NX)

    def stage_d(g, o):
        yy = up(y, o, NY)
        got(rbuf[g].at[left, yy], rr.at[g, left, yy])
        got(rbuf[g].at[right, yy], rr.at[g, right, yy])
        origin, target = (left, xup) if o % 2 == 0 else (right, xdn)
        chunk = rbuf[g].at[origin, yy]
        put(chunk, chunk, xsm.at[2, g, o + 4], rr.at[g, origin, yy], target)

    def stage_e(g, o):
        yy = up(y, o, NY)
        got(rbuf[g].at[far, yy], rr.at[g, far, yy])

    def piece(g, xx, fresh):
        b = split(rbuf[g][xx].reshape(NZ * 2 * ROWS, WIDTHS[g]))
        part = mm_split((thi[xx], tlo[xx]), b).reshape(NZ, 2 * ROWS, WIDTHS[g])
        psum[g][...] = part if fresh else psum[g][...] + part

    def scatter(g):
        for s in range(1, NZ):
            to = up(z, s, NZ)
            put(psum[g].at[to], sbuf[g].at[z], ss.at[g, s], sr.at[g, z], zpeer[s - 1])
        sbuf[g][z] = psum[g][z]

    tcopy.wait()
    got(tbuf.at[1 - k], sib_r.at[NG])
    for h in range(2):
        for i in range(2):
            thi[2 * h + i], tlo[2 * h + i] = split(tbuf[h, :, 512 * i : 512 * i + 512])

    after = {i: [] for i in range(STEP_COUNT + lag_e)}
    for h, at in enumerate((4, 7, 10, 13, 15)):
        after[at].append(functools.partial(band_ring, h))
    after[13].append(l_rows)
    after[17].append(adjoint_rows)
    for xx in range(NX):
        after[LAST0 + lag_e + 1 + xx].append(functools.partial(piece, 0, xx, xx == 0))
    after[LAST0 + lag_e + 5].append(functools.partial(scatter, 0))
    after[STEP_COUNT].append(functools.partial(piece, 1, x, True))
    after[STEP_COUNT + lag_d].append(functools.partial(piece, 1, left, False))
    after[STEP_COUNT + lag_d].append(functools.partial(piece, 1, right, False))
    for i in range(STEP_COUNT + lag_e):
        for lag, stage in ((0, stage_b), (lag_d, stage_d), (lag_e, stage_e)):
            if 0 <= i - lag < STEP_COUNT:
                stage(*STEPS[i - lag])
        for task in after[i]:
            task()
    l_planes()
    piece(1, far, False)
    scatter(1)
    l_far()

    for q in range(3):
        ltr[q] = lloc[q].T
    for s in range(1, NZ):
        frm = up(z, s, NZ)
        got(cgb.at[frm], cr.at[frm])
    mine = pl.ds(pl.multiple_of(z * 64, 64), 64)

    def cross_half(lo):
        return jnp.concatenate([cgb[c // 2, c % 2, :, 0:64] for c in range(lo, lo + NZ)], 1)

    @pl.when(first)
    def _():
        corner = jnp.concatenate([cgb[c // 2, c % 2, :, 64:96] for c in range(2 * NZ)], 1)
        cross = split(cross_half(0))
        fold[0] = mm(ltr[0, mine, :], corner) + mm_split(split(ltr[2, mine, :]), cross)
        fold[1] = mm_split(split(ltr[1, mine, :]), cross)

    @pl.when(k == 1)
    def _():
        fold[0] = mm(ltr[1, mine, :], cross_half(NZ))

    bsp[0], bsp[1] = split(band[...].reshape(B, B))
    fcopy.wait()
    got(fbuf.at[1 - k], sib_r.at[NG + 1])
    for g in range(NG):
        for s in range(1, NZ):
            frm = up(z, s, NZ)
            got(sbuf[g].at[frm], sr.at[g, frm])
        total = sbuf[g][0]
        for s in range(1, NZ):
            total = total + sbuf[g][s]
        lanes = slice(STARTS[g], STARTS[g] + WIDTHS[g])
        xr[:, :, lanes] = fbuf[:, :, lanes] - 2.0 * total.reshape(2, ROWS, WIDTHS[g])

    xall = xr[...].reshape(2 * ROWS, B)
    for s in range(NZ):
        xst[s] = xall[:, 64 * s : 64 * s + 64]
    for s in range(1, NZ):
        to = up(z, s, NZ)
        put(xst.at[to], xs.at[z], as_.at[s], ar.at[z], zpeer[s - 1])
    put(xr.at[1 - k], xo.at[k], sib_s.at[NG + 2], sib_r.at[NG + 2], sib)
    xo[k] = xr[k]
    xs[z] = xst[z]
    for s in range(1, NZ):
        frm = up(z, s, NZ)
        got(xs.at[frm], ar.at[frm])
    put(xs, xs2, sib_s.at[NG + 3], sib_r.at[NG + 3], sib, k == 1)

    def gram(b, src):
        a = split(src[...].reshape(NZ * 64, 64).T)
        gm[b] = (mm_split(a, bsp) - fold[b]).reshape(NY, 8, B)

    gram(0, xs)

    @pl.when(first)
    def _():
        got(xs2, sib_r.at[NG + 3])
        gram(1, xs2)

    sides = ((2, first), (1, k == 1))

    def each(fn):
        for nb, cond in sides:
            pl.when(cond)(functools.partial(fn, nb, pl.ds(0, nb)))

    for nb, cond in sides:
        for s in range(1, NY):
            to = up(y, s, NY)
            put(gm.at[pl.ds(0, nb), to], gy.at[pl.ds(0, nb), y], gys.at[s], gyr.at[y], ypeer[s - 1], cond)

    l_cores()

    def y_sum(nb, bs):
        gy[0:nb, y] = gm[0:nb, y]
        for s in range(1, NY):
            frm = up(y, s, NY)
            got(gy.at[bs, frm], gyr.at[frm])
        total = gy[0:nb, 0]
        for s in range(1, NY):
            total = total + gy[0:nb, s]
        sg[0:nb] = total
        gx[0:nb, x] = total

    def x_sum(nb, bs):
        for s in range(1, NX):
            frm = up(x, s, NX)
            got(gx.at[bs, frm], gxr.at[frm])
        total = (gx[0:nb, 0] + gx[0:nb, 1]) + (gx[0:nb, 2] + gx[0:nb, 3])
        gz[0:nb, 0, z, y] = total[:, :, 0:W2]
        gz[0:nb, 1, z, y] = total[:, :, W2:B]

    def y_wait(nb, bs):
        for s in range(1, NY):
            frm = up(y, s, NY)
            got(gz.at[bs, 0, z, frm], gar.at[frm])
        for s in range(1, NZ):
            frm = up(z, s, NZ)
            got(gz.at[bs, 1, frm, y], gbr.at[frm])

    each(y_sum)
    for nb, cond in sides:
        for s in range(1, NX):
            put(sg.at[pl.ds(0, nb)], gx.at[pl.ds(0, nb), x], gxs.at[s], gxr.at[x], xpeer[s - 1], cond)

    def factor(q):
        return jnp.concatenate([lbuf[p, :, :, 2 * q : 2 * q + 2].reshape(B, 128) for p in range(4)], 1)

    def tile(q):
        return lambda i, j: lbuf[j, 2 * i : 2 * i + 2, :, 2 * q : 2 * q + 2].reshape(128, 128)

    def second_inverse():
        got(lbuf.at[:, :, :, pl.ds(3 * (1 - k), 3)], sib_r.at[NG + 5])
        invert(tile(1), v2)

    def first_inverse():
        v2t[...] = v2[...].T
        invert(tile(0), v1)

    def coupling_factor():
        l2t[0], l2t[1] = split(factor(1).T)
        l1t[0], l1t[1] = split(factor(0).T)
        l21[0], l21[1] = split(factor(2))
        v1s[0], v1s[1] = split(v1[...])
        v2s[0], v2s[1] = split(v2[...])
        v2ts[0], v2ts[1] = split(v2t[...])
        v1t[...] = v1[...].T
        mmat[...] = mm(factor(2), v1[...])

    def tall_rows():
        mt[...] = mmat[...].T
        ms[0], ms[1] = split(mmat[...])
        got(xo.at[1 - k], sib_r.at[NG + 2])
        h2 = mm(xo[1], v2[...])
        rows_ref[:, B : 2 * B] = h2
        rows_ref[:, 0:B] = mm(xo[0], v1[...]) - mm(h2, mmat[...])

    between = {0: first_inverse, 2: coupling_factor, 4: tall_rows}

    each(x_sum)
    for nb, cond in sides:
        bs = pl.ds(0, nb)
        for s in range(1, NY):
            put(gz.at[bs, 0, z, y], gz.at[bs, 0, z, y], gas.at[s], gar.at[y], ypeer[s - 1], cond)
            put(gz.at[bs, 1, z, y], gz.at[bs, 1, z, y], gbs.at[s], gbr.at[z], zpeer[s - 1], cond)
    second_inverse()
    each(y_wait)
    for j in range(NZ):
        zz, yy = up(z, ORDER[j], NZ), up(y, ORDER[j], NY)
        hop = abs(ORDER[j])
        for nb, cond in sides:
            bs = pl.ds(0, nb)
            chunk, other = gz.at[bs, 0, zz], gz.at[bs, 1, :, yy]
            if j > 0:
                pl.when(cond)(functools.partial(got, chunk, gzr.at[zz]))
                pl.when(cond)(functools.partial(got, other, gwr.at[yy]))
            if j == 0 or (ORDER[j] < 0 and hop < NZ // 2):
                put(chunk, chunk, gzs.at[0, hop], gzr.at[zz], zup, cond)
                put(other, other, gws.at[0, hop], gwr.at[yy], yup, cond)
            if j == 0 or (ORDER[j] > 0 and hop < NZ // 2 - 1):
                put(chunk, chunk, gzs.at[1, hop], gzr.at[zz], zdn, cond)
                put(other, other, gws.at[1, hop], gwr.at[yy], ydn, cond)
        if j in between:
            between[j]()

    def gram_total(b):
        return jnp.concatenate([gz[b, 0].reshape(B, W2), gz[b, 1].reshape(B, W2)], 1)

    r = lax.broadcasted_iota(jnp.int32, (B, B), 0)
    c = lax.broadcasted_iota(jnp.int32, (B, B), 1)
    own = pl.ds(pl.multiple_of(row * 16, 16), 16)

    def lowered(p):
        return jnp.where(r > c, p, jnp.where(r == c, 0.5 * p, 0.0))

    @pl.when(k == 1)
    def _():
        p2 = mm_split(v2ts, split(gram_total(0)))
        q2 = lowered(mm_split(l2t, split(jnp.where(r >= c, -p2, 0.0))))
        w1[...] = mm_split(split(q2 + q2.T), v2s)
        sbm[...] = 0.5 * mm_split(v2ts, split(w1[...]))

    put(sbm, sbm, sib_s.at[NG + 6], sib_r.at[NG + 6], sib, k == 1)

    @pl.when(first)
    def _():
        p1 = split(-mm_split(v2ts, split(gram_total(1))))
        w1[...] = mm_split(p1, v1s)
        w2[...] = mm(v1t[...], gram_total(0)) + mm_split(split(mt[...]), p1)
        got(sbm, sib_r.at[NG + 6])
        coupling = w1[...] - 2.0 * mm_split(split(sbm[...]), ms)
        w1[...] = coupling
        outp[0] = w1[own, :]
        grad = jnp.where(r >= c, -w2[...] - mm_split(split(coupling.T), l21), 0.0)
        q1 = lowered(mm_split(l1t, split(grad)))
        w1[...] = q1 + q1.T
        outp[1] = 0.5 * mm_split(split(mm(v1t[own, :], w1[...])), v1s)

    put(outp, outp, sib_s.at[NG + 7], sib_r.at[NG + 7], sib, first)

    @pl.when(k == 1)
    def _():
        got(outp, sib_r.at[NG + 7])

    shift = lax.rem(B - col * 32, B)
    c_ref[...] = pltpu.roll(outp[0], shift, 1)[:, 0:32]
    b_ref[0] = pltpu.roll(outp[1], shift, 1)[:, 0:32]
    b_ref[1] = pltpu.roll(sbm[own, :], shift, 1)[:, 0:32]

    for c, cond in sends:
        if cond is None:
            c.wait_send()
        else:
            pl.when(cond)(c.wait_send)


def panel_call(*args):
    dma = pltpu.SemaphoreType.DMA
    vm = pl.BlockSpec(memory_space=pltpu.VMEM)
    hbm = pl.BlockSpec(memory_space=pl.ANY)
    square = pltpu.VMEM((B, B), F32)
    return pl.pallas_call(
        panel_kernel,
        out_shape=(
            jax.ShapeDtypeStruct((ROWS, 2 * B), F32),
            jax.ShapeDtypeStruct((2, 16, 32), F32),
            jax.ShapeDtypeStruct((16, 32), F32),
        ),
        in_specs=[hbm] * 7,
        out_specs=(vm, vm, vm),
        scratch_shapes=[
            pltpu.VMEM((2, 512, 1024), F32),
            pltpu.VMEM((NX, 512, 512), BF16),
            pltpu.VMEM((NX, 512, 512), BF16),
            pltpu.VMEM((NZ, 2, ROWS, B), F32),
        ]
        + [pltpu.VMEM((NX, NZ, 2, ROWS, w), F32) for w in WIDTHS]
        + [pltpu.VMEM((NZ, 2 * ROWS, w), F32) for w in WIDTHS]
        + [pltpu.VMEM((NZ, 2 * ROWS, w), F32) for w in WIDTHS]
        + [
            pltpu.VMEM((2, ROWS, B), F32),
            pltpu.VMEM((2, ROWS, B), F32),
            pltpu.VMEM((2, ROWS, B), F32),
            pltpu.VMEM((NZ, 64, 64), F32),
            pltpu.VMEM((NZ, 64, 64), F32),
            pltpu.VMEM((NZ, 64, 64), F32),
            pltpu.VMEM((2, NY, 8, B), F32),
            pltpu.VMEM((2, NY, 8, B), F32),
            pltpu.VMEM((2, 8, B), F32),
            pltpu.VMEM((2, NX, 8, B), F32),
            pltpu.VMEM((2, 2, NZ, NY, 8, W2), F32),
            pltpu.VMEM((3, 16, B), F32),
            pltpu.VMEM((16, 64), F32),
            pltpu.VMEM((16, 32), F32),
            pltpu.VMEM((4, NY, NX, 6, 8, 128), F32),
            pltpu.VMEM((NZ, 2, 16, 128), F32),
            pltpu.VMEM((3, B, 16), F32),
            pltpu.VMEM((2, 64, B), F32),
        ]
        + [square] * 9
        + [pltpu.VMEM((2, 16, B), F32)]
        + [pltpu.VMEM((2, B, B), BF16)] * 8
        + [
            dma((NG + 12,)), dma((NG + 8,)), dma((NG + 6,)),
            dma((2, NZ)), dma((NZ,)),
            dma((2, NG, NZ)), dma((3, NG, NZ)), dma((NG, NX, NZ)),
            dma((NG, NZ)), dma((NG, NZ)),
            dma((NZ,)), dma((NZ,)),
            dma((NY,)), dma((NY,)),
            dma((NX,)), dma((NX,)),
            dma((NY,)), dma((NY,)),
            dma((NZ,)), dma((NZ,)),
            dma((2, NZ // 2)), dma((NZ,)),
            dma((2, NY // 2)), dma((NY,)),
            dma((NY,)), dma((NY,)),
            dma((2,)), dma((2,)), dma((2,)), dma((2,)),
            dma((NZ,)), dma((NZ,)),
        ],
        compiler_params=pltpu.CompilerParams(
            collective_id=0, has_side_effects=True, vmem_limit_bytes=60 * 1024 * 1024
        ),
        name="panel_adjoint",
    )(*args)


def invert(lower, out_ref):
    n = 128
    r = lax.broadcasted_iota(jnp.int32, (n, n), 0)
    c = lax.broadcasted_iota(jnp.int32, (n, n), 1)
    blocks = [lower(q, q) for q in range(4)]
    inv = []
    for a in blocks:
        diag = jnp.sum(jnp.where(r == c, a, 0.0), axis=1, keepdims=True)
        inv.append(jnp.where(r == c, 1.0 / diag, 0.0))
    for lb in range(7):
        mask = ((r >> (lb + 1)) == (c >> (lb + 1))) & ((r >> lb) > (c >> lb))
        for q in range(4):
            cut = jnp.where(mask, blocks[q], 0.0)
            yy = split(inv[q])
            inv[q] = inv[q] - mm_split(yy, split(mm_split(split(cut), yy)))
    zero = jnp.zeros((n, n), F32)
    wide = []
    for h in range(2):
        a, b = inv[2 * h], inv[2 * h + 1]
        low = -mm(b, mm(lower(2 * h + 1, 2 * h), a))
        wide.append(jnp.concatenate([jnp.concatenate([a, zero], 1), jnp.concatenate([low, b], 1)], 0))
    corner = jnp.concatenate(
        [jnp.concatenate([lower(2, 0), lower(2, 1)], 1), jnp.concatenate([lower(3, 0), lower(3, 1)], 1)], 0
    )
    low = -mm(wide[1], mm(corner, wide[0]))
    out_ref[0:256, 0:256] = wide[0]
    out_ref[0:256, 256:512] = jnp.zeros((256, 256), F32)
    out_ref[256:512, 0:256] = low
    out_ref[256:512, 256:512] = wide[1]


def store_kernel(*refs):
    for src, dst in zip(refs[:3], refs[3:]):
        dst[...] = src[...]


def per_device(*args):
    found = panel_call(*args)
    vm = pl.BlockSpec(memory_space=pltpu.VMEM)
    return pl.pallas_call(
        store_kernel,
        out_shape=tuple(jax.ShapeDtypeStruct(f.shape, F32) for f in found),
        in_specs=[vm] * 3,
        out_specs=(vm,) * 3,
        name="store",
    )(*found)


def solution(mesh):
    return jax.shard_map(
        per_device,
        mesh=mesh,
        in_specs=(
            P("row", "col"),
            P(("row", "col"), None),
            P(("row", "col"), None),
            P(None, "row", None),
            P("row", None),
            P("row", "col"),
            P("row", "col"),
        ),
        out_specs=(P(("row", "col"), None), P(None, "row", "col"), P("row", "col")),
        check_vma=False,
    )
```

```python
import functools

import jax
import jax.numpy as jnp
from jax import lax
from jax.experimental import pallas as pl
from jax.experimental.pallas import tpu as pltpu
from jax.sharding import PartitionSpec as P

MESH = pl.DeviceIdType.MESH
F32 = jnp.float32
BF16 = jnp.bfloat16
NX, NY, NZ = 4, 8, 8
NG = 2
B = 512
W = B // NG
W2 = B // 2
ROWS = 32
ORDER = (0, -1, 1, -2, 2, -3, 3, -4)
STEPS = [(g, o) for g in range(NG) for o in ORDER]
STEP_COUNT = len(STEPS)
LAST0 = NZ - 1


def pick(values, n):
    words = [sum(v << (4 * i) for i, v in enumerate(values[h : h + 8])) for h in (0, 8)]
    return (jnp.where(n < 8, words[0], words[1]) >> (4 * lax.rem(n, 8))) & 7


def split(a):
    hi = a.astype(BF16)
    return hi, (a - hi.astype(F32)).astype(BF16)


def dot(a, b):
    return jnp.dot(a, b, preferred_element_type=F32)


def mm_split(a, b):
    return dot(a[0], b[0]) + (dot(a[0], b[1]) + dot(a[1], b[0]))


def mm(a, b):
    return mm_split(split(a), split(b))


def panel_kernel(
    t_ref, r_ref, f_ref, diag_ref, cross_ref, cg_ref, co_ref,
    rows_ref, b_ref, c_ref,
    tbuf, thi, tlo, band, rbuf, psum, sbuf, fbuf, xr, xo, xst, xs, xs2, gm, gy, sg, gx, gz,
    lloc, cgl, col_, lbuf, cgb, ltr, fold, v1, v2, v1t, v2t, mmat, mt, w1, w2, sbm, cpl, outp,
    sib_s, sib_r, loc, zs, zr, ys, xsm, rr, ss, sr, as_, ar, gys, gyr, gxs, gxr, gas, gar, gbs, gbr, gzs, gzr,
    gws, gwr, lys, lyr, lzs, lzr, lfs, lfr, cs_, cr,
):
    local = [
        pltpu.make_async_copy(diag_ref, lloc.at[pl.ds(0, 2)], loc.at[1]),
        pltpu.make_async_copy(cross_ref, lloc.at[2], loc.at[2]),
        pltpu.make_async_copy(cg_ref, cgl, loc.at[3]),
        pltpu.make_async_copy(co_ref, col_, loc.at[4]),
    ]
    for c in local:
        c.start()
    row = lax.axis_index("row")
    col = lax.axis_index("col")
    y, x = row // NX, lax.rem(row, NX)
    z, k = col // 2, lax.rem(col, 2)

    def dev(px, py, pz, pk):
        return {"row": py * NX + px, "col": pz * 2 + pk}

    def up(v, s, n):
        return lax.rem(v + (s + n), n)

    sib = dev(x, y, z, 1 - k)
    zpeer = [dev(x, y, up(z, s, NZ), k) for s in range(1, NZ)]
    ypeer = [dev(x, up(y, s, NY), z, k) for s in range(1, NY)]
    xpeer = [dev(up(x, s, NX), y, z, k) for s in range(1, NX)]
    zup, zdn = zpeer[0], zpeer[-1]
    yup, ydn = ypeer[0], ypeer[-1]
    xup, xdn = xpeer[0], xpeer[-1]
    d = up(y - z, NY, NY)

    barrier = pltpu.get_barrier_semaphore()
    partners = [sib, zup, zdn, yup, ydn] + xpeer
    for p in partners:
        pl.semaphore_signal(barrier, inc=1, device_id=p, device_id_type=MESH)

    swap = [dev(x, z, y, k), dev(x, z, y, 1 - k)]

    @pl.when(d != 0)
    def _():
        for p in swap:
            pl.semaphore_signal(barrier, inc=1, device_id=p, device_id_type=MESH)

    pl.semaphore_wait(barrier, len(partners) + jnp.where(d == 0, 0, 2))

    sends = []
    mode = ["start"]

    def put(src, dst, ssem, rsem, target, cond=None):
        c = pltpu.make_async_remote_copy(
            src_ref=src, dst_ref=dst, send_sem=ssem, recv_sem=rsem, device_id=target, device_id_type=MESH
        )
        act = c.wait_send if mode[0] == "finish" else c.start
        if cond is None:
            act()
        else:
            pl.when(cond)(act)
        if mode[0] == "start":
            sends.append((c, cond))

    def got(ref, sem):
        if mode[0] != "finish":
            pltpu.make_async_remote_copy(
                src_ref=ref, dst_ref=ref, send_sem=sem, recv_sem=sem, device_id=sib, device_id_type=MESH
            ).wait_recv()

    first = k == 0
    rcopies = []
    for g in range(NG):
        ours = r_ref.at[:, pl.ds(pl.multiple_of(k * B + g * W, 128), W)]
        theirs = r_ref.at[:, pl.ds(pl.multiple_of((1 - k) * B + g * W, 128), W)]
        slot, sem = rbuf.at[g, x, z, k], rr.at[g, x, z]
        put(ours, slot, sib_s.at[NG + 8 + g], sem, swap[0], d != 0)
        put(theirs, slot, sib_s.at[NG + 10 + g], sem, swap[1])
        rcopies.append((pltpu.make_async_copy(ours, slot, sem), d == 0))
        pl.when(d == 0)(rcopies[-1][0].start)
    for g in range(NG):
        ours = r_ref.at[:, pl.ds(pl.multiple_of(k * B + g * W, 128), W)]
        theirs = r_ref.at[:, pl.ds(pl.multiple_of((1 - k) * B + g * W, 128), W)]
        put(theirs, band.at[g, z, k], sib_s.at[g], sib_r.at[g], sib)
        pltpu.make_async_copy(ours, band.at[g, z, k], loc.at[5 + g]).start()
    put(t_ref, tbuf.at[k], sib_s.at[NG], sib_r.at[NG], sib)
    tcopy = pltpu.make_async_copy(t_ref, tbuf.at[k], loc.at[0])
    tcopy.start()
    put(f_ref.at[:, pl.ds(pl.multiple_of((1 - k) * B, 128), B)], fbuf.at[k], sib_s.at[NG + 1], sib_r.at[NG + 1], sib)
    fcopy = pltpu.make_async_copy(f_ref.at[:, pl.ds(pl.multiple_of(k * B, 128), B)], fbuf.at[k], loc.at[5 + NG])
    fcopy.start()
    for c in local:
        c.wait()
    half = pl.ds(3 * k, 3)
    for q in range(3):
        for p in range(4):
            lbuf[p, y, x, 2 * q : 2 * q + 2] = lloc[q, :, 128 * p : 128 * p + 128].reshape(2, 8, 128)
    cgb[z, k] = jnp.zeros((16, 128), F32)
    cgb[z, k, :, 0:64] = cgl[...]
    cgb[z, k, :, 64:96] = col_[...]
    put(cgb.at[z, k], cgb.at[z, k], sib_s.at[NG + 4], sib_r.at[NG + 4], sib)

    def l_rows():
        part = lbuf.at[:, y, x, half]
        for s in range(1, NY):
            put(part, part, lys.at[s], lyr.at[y], ypeer[s - 1])

    def l_planes():
        for s in range(1, NY):
            frm = up(y, s, NY)
            got(lbuf.at[:, frm, x, half], lyr.at[frm])
        part = lbuf.at[:, :, x, half]
        for i, to in enumerate((xup, xdn)):
            put(part, part, lzs.at[i], lzr.at[i], to)

    def l_far():
        for i, (to, frm) in enumerate(((xup, up(x, -1, NX)), (xdn, up(x, 1, NX)))):
            got(lbuf.at[:, :, frm, half], lzr.at[i])
            part = lbuf.at[pl.ds(2 * i, 2), :, frm, half]
            put(part, part, lfs.at[i], lfr.at[i], to)

    def l_cores():
        far = up(x, 2, NX)
        for i in range(2):
            got(lbuf.at[pl.ds(2 * i, 2), :, far, half], lfr.at[i])
        put(lbuf.at[:, :, :, half], lbuf.at[:, :, :, half], sib_s.at[NG + 5], sib_r.at[NG + 5], sib)

    def adjoint_rows():
        got(cgb.at[z, 1 - k], sib_r.at[NG + 4])
        for s in range(1, NZ):
            put(cgb.at[z], cgb.at[z], cs_.at[s], cr.at[z], zpeer[s - 1])

    lag_d = 2
    lag_e = 4

    def band_ring(hop):
        low, high = up(z, -hop, NZ), up(z, hop, NZ)
        if hop == 0:
            if mode[0] != "finish":
                for g in range(NG):
                    ours = band.at[g, z, k]
                    pltpu.make_async_copy(ours, ours, loc.at[5 + g]).wait()
                    got(band.at[g, z, 1 - k], sib_r.at[g])
        else:
            got(band.at[:, low], zr.at[low])
            if hop < NZ // 2:
                got(band.at[:, high], zr.at[high])
        if hop < NZ // 2:
            put(band.at[:, low], band.at[:, low], zs.at[0, hop], zr.at[low], zup)
        if hop < NZ // 2 - 1:
            put(band.at[:, high], band.at[:, high], zs.at[1, hop], zr.at[high], zdn)

    background = [(17, adjoint_rows), (13, l_rows)]
    background += [(at, functools.partial(band_ring, h)) for h, at in enumerate((4, 7, 10, 13, 15))]

    def step(n):
        o = pick([st[1] + 4 for st in STEPS], n)
        return pick([st[0] for st in STEPS], n), o, lax.rem(y + o + NZ - 4, NZ)

    def stage_b(n):
        g, o, zz = step(n)
        slot, sem = rbuf.at[g, x, zz], rr.at[g, x, zz]
        got(slot, sem)

        put(slot, slot, ys.at[0, g, o], sem, yup, jnp.logical_and(o >= 1, o <= 4))
        put(slot, slot, ys.at[1, g, o], sem, ydn, jnp.logical_and(o >= 4, o <= 6))
        put(slot, slot, xsm.at[0, g, o], sem, xup)
        put(slot, slot, xsm.at[1, g, o], sem, xdn)

    def stage_d(n):
        g, o, zz = step(n)
        left, right = up(x, -1, NX), up(x, 1, NX)
        got(rbuf.at[g, left, zz], rr.at[g, left, zz])
        got(rbuf.at[g, right, zz], rr.at[g, right, zz])
        even = lax.rem(o, 2) == 0
        chunk = rbuf.at[g, left, zz]
        put(chunk, chunk, xsm.at[2, g, o], rr.at[g, left, zz], xup, even)
        chunk = rbuf.at[g, right, zz]
        put(chunk, chunk, xsm.at[2, g, o], rr.at[g, right, zz], xdn, jnp.logical_not(even))

    def stage_e(n):
        g, o, zz = step(n)
        far = up(x, 2, NX)
        got(rbuf.at[g, far, zz], rr.at[g, far, zz])

    def piece(g, xx):
        b = split(rbuf[g, xx].reshape(NZ * 2 * ROWS, W))
        psum[g] += mm_split((thi[xx], tlo[xx]), b).reshape(NZ, 2 * ROWS, W)

    def scatter(g):
        for s in range(1, NZ):
            to = up(z, s, NZ)
            put(psum.at[g, to], sbuf.at[g, z], ss.at[g, s], sr.at[g, z], zpeer[s - 1])
        if mode[0] != "finish":
            sbuf[g, z] = psum[g, z]

    def within(n, fn):
        @pl.when(jnp.logical_and(n >= 0, n < STEP_COUNT))
        def _():
            fn(n)

    def first_group(n):
        @pl.when(jnp.logical_and(n >= 0, n < NX))
        def _():
            piece(0, n)

        @pl.when(n == NX)
        def _():
            scatter(0)

    def split_t(h):
        for i in range(2):
            thi[2 * h + i], tlo[2 * h + i] = split(tbuf[h, :, 512 * i : 512 * i + 512])

    tcopy.wait()
    got(tbuf.at[1 - k], sib_r.at[NG])
    for h in range(2):
        split_t(h)
    psum[...] = jnp.zeros_like(psum)
    mode[0] = "loop"

    def body(i, carry):
        within(i, stage_b)
        within(i - lag_d, stage_d)
        within(i - lag_e, stage_e)
        for at, task in background:
            pl.when(i == at)(task)
        first_group(i - lag_e - LAST0 - 1)
        return carry

    lax.fori_loop(0, STEP_COUNT + 4, body, 0)
    mode[0] = "start"
    l_planes()
    for xx in range(NX):
        piece(1, xx)
    scatter(1)
    l_far()

    for q in range(3):
        ltr[q] = lloc[q].T
    for s in range(1, NZ):
        frm = up(z, s, NZ)
        got(cgb.at[frm], cr.at[frm])
    mine = pl.ds(pl.multiple_of(z * 64, 64), 64)

    def cross_half(lo):
        return jnp.concatenate([cgb[c // 2, c % 2, :, 0:64] for c in range(lo, lo + NZ)], 1)

    @pl.when(first)
    def _():
        corner = jnp.concatenate([cgb[c // 2, c % 2, :, 64:96] for c in range(2 * NZ)], 1)
        cross = split(cross_half(0))
        fold[0] = mm(ltr[0, mine, :], corner) + mm_split(split(ltr[2, mine, :]), cross)
        fold[1] = mm_split(split(ltr[1, mine, :]), cross)

    @pl.when(k == 1)
    def _():
        fold[0] = mm(ltr[1, mine, :], cross_half(NZ))

    fcopy.wait()
    got(fbuf.at[1 - k], sib_r.at[NG + 1])
    for g in range(NG):
        for s in range(1, NZ):
            frm = up(z, s, NZ)
            got(sbuf.at[g, frm], sr.at[g, frm])
        total = sbuf[g, 0]
        for s in range(1, NZ):
            total = total + sbuf[g, s]
        lanes = slice(g * W, g * W + W)
        xr[:, :, lanes] = fbuf[:, :, lanes] - 2.0 * total.reshape(2, ROWS, W)

    xall = xr[...].reshape(2 * ROWS, B)
    for s in range(NZ):
        xst[s] = xall[:, 64 * s : 64 * s + 64]
    for s in range(1, NZ):
        to = up(z, s, NZ)
        put(xst.at[to], xs.at[z], as_.at[s], ar.at[z], zpeer[s - 1])
    l_cores()
    put(xr.at[1 - k], xo.at[k], sib_s.at[NG + 2], sib_r.at[NG + 2], sib)
    xo[k] = xr[k]
    xs[z] = xst[z]
    for s in range(1, NZ):
        frm = up(z, s, NZ)
        got(xs.at[frm], ar.at[frm])
    put(xs, xs2, sib_s.at[NG + 3], sib_r.at[NG + 3], sib, k == 1)

    def gram(b, src):
        a = split(src[...].reshape(NZ * 64, 64).T)
        for g in range(NG):
            bb = split(band[g].reshape(NZ * 64, W))
            lanes = slice(g * W, g * W + W)
            gm[b, :, :, lanes] = (mm_split(a, bb) - fold[b, :, lanes]).reshape(NY, 8, W)

    gram(0, xs)

    @pl.when(first)
    def _():
        got(xs2, sib_r.at[NG + 3])
        gram(1, xs2)

    sides = ((2, first), (1, k == 1))

    def each(fn):
        for nb, cond in sides:
            pl.when(cond)(functools.partial(fn, nb, pl.ds(0, nb)))

    for nb, cond in sides:
        for s in range(1, NY):
            to = up(y, s, NY)
            put(gm.at[pl.ds(0, nb), to], gy.at[pl.ds(0, nb), y], gys.at[s], gyr.at[y], ypeer[s - 1], cond)

    def y_sum(nb, bs):
        gy[0:nb, y] = gm[0:nb, y]
        for s in range(1, NY):
            frm = up(y, s, NY)
            got(gy.at[bs, frm], gyr.at[frm])
        total = gy[0:nb, 0]
        for s in range(1, NY):
            total = total + gy[0:nb, s]
        sg[0:nb] = total
        gx[0:nb, x] = total

    def x_sum(nb, bs):
        for s in range(1, NX):
            frm = up(x, s, NX)
            got(gx.at[bs, frm], gxr.at[frm])
        total = (gx[0:nb, 0] + gx[0:nb, 1]) + (gx[0:nb, 2] + gx[0:nb, 3])
        gz[0:nb, 0, z, y] = total[:, :, 0:W2]
        gz[0:nb, 1, z, y] = total[:, :, W2:B]

    def y_wait(nb, bs):
        for s in range(1, NY):
            frm = up(y, s, NY)
            got(gz.at[bs, 0, z, frm], gar.at[frm])
        for s in range(1, NZ):
            frm = up(z, s, NZ)
            got(gz.at[bs, 1, frm, y], gbr.at[frm])

    each(y_sum)
    for nb, cond in sides:
        for s in range(1, NX):
            put(sg.at[pl.ds(0, nb)], gx.at[pl.ds(0, nb), x], gxs.at[s], gxr.at[x], xpeer[s - 1], cond)

    def factor(q):
        return jnp.concatenate([lbuf[p, :, :, 2 * q : 2 * q + 2].reshape(B, 128) for p in range(4)], 1)

    def tile(q):
        return lambda i, j: lbuf[j, 2 * i : 2 * i + 2, :, 2 * q : 2 * q + 2].reshape(128, 128)

    def second_inverse():
        got(lbuf.at[:, :, :, pl.ds(3 * (1 - k), 3)], sib_r.at[NG + 5])
        invert(tile(1), v2)

    def first_inverse():
        v2t[...] = v2[...].T
        invert(tile(0), v1)

    def coupling_factor():
        v1t[...] = v1[...].T
        mmat[...] = mm(factor(2), v1[...])

    def tall_rows():
        mt[...] = mmat[...].T
        got(xo.at[1 - k], sib_r.at[NG + 2])
        h2 = mm(xo[1], v2[...])
        rows_ref[:, B : 2 * B] = h2
        rows_ref[:, 0:B] = mm(xo[0], v1[...]) - mm(h2, mmat[...])

    between = {0: second_inverse, 2: first_inverse, 4: coupling_factor, 6: tall_rows}

    each(x_sum)
    for nb, cond in sides:
        bs = pl.ds(0, nb)
        for s in range(1, NY):
            put(gz.at[bs, 0, z, y], gz.at[bs, 0, z, y], gas.at[s], gar.at[y], ypeer[s - 1], cond)
            put(gz.at[bs, 1, z, y], gz.at[bs, 1, z, y], gbs.at[s], gbr.at[z], zpeer[s - 1], cond)
    each(y_wait)
    for j in range(NZ):
        zz, yy = up(z, ORDER[j], NZ), up(y, ORDER[j], NY)
        hop = abs(ORDER[j])
        for nb, cond in sides:
            bs = pl.ds(0, nb)
            chunk, other = gz.at[bs, 0, zz], gz.at[bs, 1, :, yy]
            if j > 0:
                pl.when(cond)(functools.partial(got, chunk, gzr.at[zz]))
                pl.when(cond)(functools.partial(got, other, gwr.at[yy]))
            if j == 0 or (ORDER[j] < 0 and hop < NZ // 2):
                put(chunk, chunk, gzs.at[0, hop], gzr.at[zz], zup, cond)
                put(other, other, gws.at[0, hop], gwr.at[yy], yup, cond)
            if j == 0 or (ORDER[j] > 0 and hop < NZ // 2 - 1):
                put(chunk, chunk, gzs.at[1, hop], gzr.at[zz], zdn, cond)
                put(other, other, gws.at[1, hop], gwr.at[yy], ydn, cond)
        if j in between:
            between[j]()

    def gram_total(b):
        return jnp.concatenate([gz[b, 0].reshape(B, W2), gz[b, 1].reshape(B, W2)], 1)

    r = lax.broadcasted_iota(jnp.int32, (B, B), 0)
    c = lax.broadcasted_iota(jnp.int32, (B, B), 1)
    own = pl.ds(pl.multiple_of(row * 16, 16), 16)

    def lowered(p):
        return jnp.where(r > c, p, jnp.where(r == c, 0.5 * p, 0.0))

    @pl.when(k == 1)
    def _():
        left = split(v2t[...])
        p2 = mm_split(left, split(gram_total(0)))
        q2 = lowered(mm(factor(1).T, jnp.where(r >= c, -p2, 0.0)))
        w1[...] = mm(q2 + q2.T, v2[...])
        sbm[...] = 0.5 * mm_split(left, split(w1[...]))

    put(sbm, sbm, sib_s.at[NG + 6], sib_r.at[NG + 6], sib, k == 1)

    @pl.when(first)
    def _():
        p1 = split(-mm(v2t[...], gram_total(1)))
        w1[...] = mm_split(p1, split(v1[...]))
        w2[...] = mm(v1t[...], gram_total(0)) + mm_split(split(mt[...]), p1)
        got(sbm, sib_r.at[NG + 6])
        coupling = w1[...] - 2.0 * mm(sbm[...], mmat[...])
        cpl[...] = coupling
        outp[0] = cpl[own, :]
        grad = jnp.where(r >= c, -w2[...] - mm(coupling.T, factor(2)), 0.0)
        q1 = lowered(mm(factor(0).T, grad))
        w1[...] = q1 + q1.T
        outp[1] = 0.5 * mm(mm(v1t[own, :], w1[...]), v1[...])

    put(outp, outp, sib_s.at[NG + 7], sib_r.at[NG + 7], sib, first)

    @pl.when(k == 1)
    def _():
        got(outp, sib_r.at[NG + 7])

    shift = lax.rem(B - col * 32, B)
    c_ref[...] = pltpu.roll(outp[0], shift, 1)[:, 0:32]
    b_ref[0] = pltpu.roll(outp[1], shift, 1)[:, 0:32]
    b_ref[1] = pltpu.roll(sbm[own, :], shift, 1)[:, 0:32]

    for c, cond in sends:
        if cond is None:
            c.wait_send()
        else:
            pl.when(cond)(c.wait_send)
    mode[0] = "finish"
    for _, task in background:
        task()
    scatter(0)

    def sent(n, carry):
        stage_b(n)
        stage_d(n)
        return carry

    lax.fori_loop(0, STEP_COUNT, sent, 0)


def panel_call(*args):
    dma = pltpu.SemaphoreType.DMA
    vm = pl.BlockSpec(memory_space=pltpu.VMEM)
    hbm = pl.BlockSpec(memory_space=pl.ANY)
    square = pltpu.VMEM((B, B), F32)
    return pl.pallas_call(
        panel_kernel,
        out_shape=(
            jax.ShapeDtypeStruct((ROWS, 2 * B), F32),
            jax.ShapeDtypeStruct((2, 16, 32), F32),
            jax.ShapeDtypeStruct((16, 32), F32),
        ),
        in_specs=[hbm] * 7,
        out_specs=(vm, vm, vm),
        scratch_shapes=[
            pltpu.VMEM((2, 512, 1024), F32),
            pltpu.VMEM((NX, 512, 512), BF16),
            pltpu.VMEM((NX, 512, 512), BF16),
            pltpu.VMEM((NG, NZ, 2, ROWS, W), F32),
            pltpu.VMEM((NG, NX, NZ, 2, ROWS, W), F32),
            pltpu.VMEM((NG, NZ, 2 * ROWS, W), F32),
            pltpu.VMEM((NG, NZ, 2 * ROWS, W), F32),
            pltpu.VMEM((2, ROWS, B), F32),
            pltpu.VMEM((2, ROWS, B), F32),
            pltpu.VMEM((2, ROWS, B), F32),
            pltpu.VMEM((NZ, 64, 64), F32),
            pltpu.VMEM((NZ, 64, 64), F32),
            pltpu.VMEM((NZ, 64, 64), F32),
            pltpu.VMEM((2, NY, 8, B), F32),
            pltpu.VMEM((2, NY, 8, B), F32),
            pltpu.VMEM((2, 8, B), F32),
            pltpu.VMEM((2, NX, 8, B), F32),
            pltpu.VMEM((2, 2, NZ, NY, 8, W2), F32),
            pltpu.VMEM((3, 16, B), F32),
            pltpu.VMEM((16, 64), F32),
            pltpu.VMEM((16, 32), F32),
            pltpu.VMEM((4, NY, NX, 6, 8, 128), F32),
            pltpu.VMEM((NZ, 2, 16, 128), F32),
            pltpu.VMEM((3, B, 16), F32),
            pltpu.VMEM((2, 64, B), F32),
        ]
        + [square] * 10
        + [
            pltpu.VMEM((2, 16, B), F32),
            dma((NG + 12,)), dma((NG + 8,)), dma((NG + 6,)),
            dma((2, NZ)), dma((NZ,)),
            dma((2, NG, NZ)), dma((3, NG, NZ)), dma((NG, NX, NZ)),
            dma((NG, NZ)), dma((NG, NZ)),
            dma((NZ,)), dma((NZ,)),
            dma((NY,)), dma((NY,)),
            dma((NX,)), dma((NX,)),
            dma((NY,)), dma((NY,)),
            dma((NZ,)), dma((NZ,)),
            dma((2, NZ // 2)), dma((NZ,)),
            dma((2, NY // 2)), dma((NY,)),
            dma((NY,)), dma((NY,)),
            dma((2,)), dma((2,)), dma((2,)), dma((2,)),
            dma((NZ,)), dma((NZ,)),
        ],
        compiler_params=pltpu.CompilerParams(
            collective_id=0, has_side_effects=True, vmem_limit_bytes=60 * 1024 * 1024
        ),
        name="panel_adjoint",
    )(*args)


def invert(lower, out_ref):
    n = 128
    r = lax.broadcasted_iota(jnp.int32, (n, n), 0)
    c = lax.broadcasted_iota(jnp.int32, (n, n), 1)
    blocks = [lower(q, q) for q in range(4)]
    inv = []
    for a in blocks:
        diag = jnp.sum(jnp.where(r == c, a, 0.0), axis=1, keepdims=True)
        inv.append(jnp.where(r == c, 1.0 / diag, 0.0))
    for lb in range(7):
        mask = ((r >> (lb + 1)) == (c >> (lb + 1))) & ((r >> lb) > (c >> lb))
        for q in range(4):
            cut = jnp.where(mask, blocks[q], 0.0)
            yy = split(inv[q])
            inv[q] = inv[q] - mm_split(yy, split(mm_split(split(cut), yy)))
    zero = jnp.zeros((n, n), F32)
    wide = []
    for h in range(2):
        a, b = inv[2 * h], inv[2 * h + 1]
        low = -mm(b, mm(lower(2 * h + 1, 2 * h), a))
        wide.append(jnp.concatenate([jnp.concatenate([a, zero], 1), jnp.concatenate([low, b], 1)], 0))
    corner = jnp.concatenate(
        [jnp.concatenate([lower(2, 0), lower(2, 1)], 1), jnp.concatenate([lower(3, 0), lower(3, 1)], 1)], 0
    )
    low = -mm(wide[1], mm(corner, wide[0]))
    out_ref[0:256, 0:256] = wide[0]
    out_ref[0:256, 256:512] = jnp.zeros((256, 256), F32)
    out_ref[256:512, 0:256] = low
    out_ref[256:512, 256:512] = wide[1]


def store_kernel(*refs):
    for src, dst in zip(refs[:3], refs[3:]):
        dst[...] = src[...]


def per_device(*args):
    found = panel_call(*args)
    vm = pl.BlockSpec(memory_space=pltpu.VMEM)
    return pl.pallas_call(
        store_kernel,
        out_shape=tuple(jax.ShapeDtypeStruct(f.shape, F32) for f in found),
        in_specs=[vm] * 3,
        out_specs=(vm,) * 3,
        name="store",
    )(*found)


def solution(mesh):
    return jax.shard_map(
        per_device,
        mesh=mesh,
        in_specs=(
            P("row", "col"),
            P(("row", "col"), None),
            P(("row", "col"), None),
            P(None, "row", None),
            P("row", None),
            P("row", "col"),
            P("row", "col"),
        ),
        out_specs=(P(("row", "col"), None), P(None, "row", "col"), P("row", "col")),
        check_vma=False,
    )
```
